32 devices in a mesh: seq: 16 (over z, x, core), head: 2 (over y).
Axes of the slice: x: 2, y: 2, z: 4, core: 2. Of those that a mesh axis runs over, the one named last changes fastest.
Arguments:
- queries: bfloat16 [8192, 3072], P('seq', 'head'), may hold values from -6 to 6
- key_vectors: bfloat16 [8192, 3072], P('seq', 'head'), may hold values from -6 to 6
- value_vectors: bfloat16 [8192, 3072], P('seq', 'head'), may hold values from -6 to 6
- doc_lengths: int32 [16], replicated, may hold values from 1 to 5120, 8192 in all
- norm_gain: float32 [3072], P('head'), may hold values from 0.1 to 1.9
- out_weight: bfloat16 [3072, 4096], P('head'), may hold values from -0.15625 to 0.15625
Outputs:
- layer_out: bfloat16 [8192, 4096], P('seq', 'head')
The draws below stay inside these ranges and needn't reach their ends.
Inputs may be any that keep to these rules, and one draw needn't show every extreme that they name: doc_lengths sum to 8192; the longest document has exactly 5120 tokens.
All inputs are finite; a program needn't handle non-finite values.
Results may differ from the reference program's by a relative error of at most 0.014.
Values may be sent and summed in bfloat16 or wider, within the bound.
No kernel may reach another device: no remote copies, remote signals or barrier semaphores. Data moves between devices by JAX's collectives and lax.ppermute only.
A program may use at most 64 MiB of HBM per device.

```python
import math
import jax
import jax.numpy as jnp
import numpy as np
from jax import lax

D = 4096
DH = 128
HEADS = 24
TOK_DEV = 512
NDOC = 16
TOKENS = 8192
MOST = 5120
N_SEQ = 16
N_HEAD = 2


def with_spikes(entries, own_key, source, target, parts, factor):
    def block_of(dim):
        return (jnp.arange(entries.shape[dim]) // (entries.shape[dim] // parts)).reshape((-1,) + (1,) * (entries.ndim - 1 - dim))

    near = jax.random.permutation(own_key, parts)[block_of(target)]
    other_side = (block_of(target) + parts // 2) % parts
    return jnp.where((block_of(source) == near) | (block_of(source) == other_side), factor * entries, entries)


def block_levels(rng, dims, pieces, low, largest):
    loudness, own = 1.0, jax.random.fold_in(rng, 6)
    for dim, shards_of in pieces:
        draws = jnp.exp(jax.random.uniform(jax.random.fold_in(own, dim), (shards_of,), jnp.float32, low / len(pieces), largest / len(pieces)))
        loudness = loudness * jnp.repeat(draws, dims[dim] // shards_of).reshape([-1 if axis == dim else 1 for axis in range(len(dims))])
    return loudness


def split_up(count, total, most, skew):
    weights = [(1 << 20) // math.isqrt(rank ** skew) + 1 for rank in range(2, count + 1)]
    surplus, counts = total - most - (count - 1), [1] * (count - 1)
    while surplus > 0:
        free = [i for i in range(count - 1) if counts[i] < most]
        mass, budget = sum([weights[i] for i in free]), surplus
        for i in free:
            more = min(most - counts[i], max(1, budget * weights[i] // mass), surplus)
            counts[i] = counts[i] + more
            surplus = surplus - more
    return np.array([most] + counts)


def ragged_sizes(key, count, total, reach, slope):
    if count == 2:
        one = jax.random.randint(key, (), max(1, total - reach), min(reach, total - 1) + 1)
        return jnp.stack([one, total - one])
    lengths = jnp.asarray(split_up(count, total, reach, slope), jnp.int32)
    pairs = (count - 1) // 2
    source_of, sink = lengths[1:1 + 2 * pairs:2], lengths[2:2 + 2 * pairs:2]
    slack = jnp.minimum(source_of - 1, reach - sink)
    passed = jax.random.randint(jax.random.fold_in(key, 1), (pairs,), 0, 1 << 20) % (slack + 1)
    lengths = lengths.at[1:1 + 2 * pairs:2].set(source_of - passed).at[2:2 + 2 * pairs:2].set(sink + passed)
    return lengths[jax.random.permutation(jax.random.fold_in(key, 2), count)]


def scatter_about(rng, extent, width, reach, cuts=(), kind=jnp.bfloat16):
    entries = jax.random.normal(rng, extent, jnp.float32) * width
    if len(cuts) > 0:
        entries = block_levels(rng, extent, cuts, -0.22, 0.18) * entries
    return jnp.clip(entries, min=-reach, max=reach).astype(kind)


def bell_draw_with(key, shape, width, most, pieces, heavy, held_as=jnp.bfloat16):
    array = width * jax.random.normal(key, shape, jnp.float32)
    if pieces:
        array = array * block_levels(key, shape, pieces, -0.22, 0.18)
    return jnp.clip(with_spikes(array, jax.random.fold_in(key, 3), *heavy), -most, most).astype(held_as)


def setup_inputs(seed: int = 0) -> dict:
    key_of = jax.random.split(jax.random.key(seed), 7)
    queries = scatter_about(key_of[0], (TOKENS, HEADS * DH), 1.0, 6.0, ((0, 16), (1, 2)))
    key_vectors = scatter_about(key_of[1], (TOKENS, HEADS * DH), 1.0, 6.0, ((0, 16), (1, 2)))
    value_vectors = scatter_about(key_of[2], (TOKENS, HEADS * DH), 1.0, 6.0, ((0, 16), (1, 2)))
    doc_lengths = ragged_sizes(key_of[3], NDOC, TOKENS, MOST, 2).astype(jnp.int32)
    norm_gain = jnp.clip(1.0 + 0.18 * jax.random.normal(key_of[4], (HEADS * DH,), jnp.float32), 0.1, 1.9)
    out_weight = bell_draw_with(key_of[5], (HEADS * DH, D), (HEADS * DH) ** -0.5, 0.15625, ((0, 2),), (0, 1, 2, 2.0))
    return {"queries": queries, "key_vectors": key_vectors, "value_vectors": value_vectors, "doc_lengths": doc_lengths, "norm_gain": norm_gain, "out_weight": out_weight}


def reference(queries, key_vectors, value_vectors, doc_lengths, norm_gain, out_weight):
    head_count = queries.shape[1] // DH
    group_width = head_count // N_HEAD * DH
    doc_bounds = jnp.cumsum(doc_lengths).astype(jnp.int32)
    positions = jnp.arange(TOKENS, dtype=jnp.int32)
    before = doc_bounds[None, :] <= positions[:, None]
    segment = lax.optimization_barrier(jnp.sum(before.astype(jnp.int32), axis=1)).astype(jnp.int32)
    starts = lax.optimization_barrier(jnp.sum(jnp.where(before, doc_lengths[None, :], 0), axis=1)).astype(jnp.int32)
    block_shape = (N_SEQ, TOK_DEV, head_count, DH)
    block_items = (queries.reshape(block_shape), key_vectors.reshape(block_shape), value_vectors.reshape(block_shape), segment.reshape(N_SEQ, TOK_DEV), starts.reshape(N_SEQ, TOK_DEV), jnp.arange(N_SEQ, dtype=jnp.int32))
    gain_heads = norm_gain.reshape(head_count, DH).astype(jnp.float32)

    def advance(running, block_item):
        query_h, key_h, value_h, seg_block, start_block, block_index = block_item
        offset = block_index * TOK_DEV
        row_ids = jnp.arange(TOK_DEV, dtype=jnp.int32)
        allowed = (row_ids[None, :] <= row_ids[:, None]) & (seg_block[None, :] == seg_block[:, None])
        scores = jnp.einsum('thd,shd->hts', query_h.astype(jnp.float32), key_h.astype(jnp.float32))
        scores = lax.optimization_barrier(jnp.where(allowed[None], scores, 0.0).astype(jnp.bfloat16))
        within = jnp.einsum('hts,shd->thd', scores.astype(jnp.float32), value_h.astype(jnp.float32))
        last_rows = seg_block == seg_block[-1]
        key_last = jnp.where(last_rows[:, None, None], key_h, jnp.zeros_like(key_h))
        block_state = jnp.einsum('thd,the->hde', key_last.astype(jnp.float32), value_h.astype(jnp.float32))
        carried = lax.optimization_barrier(running.astype(jnp.bfloat16))
        cross_rows = (seg_block == seg_block[0]) & (start_block[0] < offset)
        query_cross = jnp.where(cross_rows[:, None, None], query_h, jnp.zeros_like(query_h))
        carried_term = jnp.einsum('thd,hde->the', query_cross.astype(jnp.float32), carried.astype(jnp.float32))
        mixture = within + carried_term
        square_mean = lax.optimization_barrier(jnp.mean(mixture * mixture, axis=-1, keepdims=True))
        normed = (mixture * lax.rsqrt(square_mean + 1e-06) * gain_heads).astype(jnp.bfloat16)
        normed = normed.reshape(TOK_DEV, head_count * DH)
        summed = jnp.zeros((TOK_DEV, D), jnp.float32)
        for member in range(N_HEAD):
            lower = member * group_width
            partial_value = jnp.dot(normed[:, lower:lower + group_width], out_weight[lower:lower + group_width], preferred_element_type=jnp.float32)
            partial_value = lax.optimization_barrier(partial_value.astype(jnp.bfloat16))
            summed = summed + partial_value.astype(jnp.float32)
        restart = start_block[-1] >= offset
        next_state = block_state + jnp.where(restart, jnp.zeros_like(running), running)
        return (next_state, summed.astype(jnp.bfloat16))
    initial = jnp.zeros((head_count, DH, DH), jnp.float32)
    final_state, outputs = lax.scan(advance, initial, block_items)
    return outputs.reshape(TOKENS, D)
```

```python
import functools

import jax
import jax.numpy as jnp
from jax import lax
from jax.experimental import pallas as pl
from jax.experimental.pallas import tpu as pltpu
from jax.sharding import PartitionSpec as P

DH = 128
PLANES = 4
F32, BF16 = jnp.float32, jnp.bfloat16
LENS = 8
VMEM_LIMIT = 48 * 1024 * 1024


def doc_start(meta, doc_count, token):
    bound = jnp.int32(0)
    start = jnp.int32(0)
    for d in range(doc_count):
        bound = bound + meta[LENS + d]
        start = jnp.where(bound <= token, bound, start)
    return start


def call(kernel, grid, in_specs, out_specs, out_shape, flops, bytes_accessed, scratch=()):
    return pl.pallas_call(
        kernel,
        grid_spec=pltpu.PrefetchScalarGridSpec(
            num_scalar_prefetch=1,
            grid=grid,
            in_specs=in_specs,
            out_specs=out_specs,
            scratch_shapes=scratch,
        ),
        out_shape=out_shape,
        compiler_params=pltpu.CompilerParams(vmem_limit_bytes=VMEM_LIMIT),
        cost_estimate=pl.CostEstimate(flops=flops, bytes_accessed=bytes_accessed, transcendentals=0),
    )


def block_states(meta, key, value, doc_count, steps):
    rows, width = key.shape
    part = width // steps

    def kernel(meta_ref, k_ref, v_ref, o_ref):
        offset = meta_ref[0] * rows
        first = doc_start(meta_ref, doc_count, offset + rows - 1) - offset
        live = lax.broadcasted_iota(jnp.int32, (rows, DH), 0) >= first
        for h in range(part // DH):
            cols = slice(h * DH, (h + 1) * DH)
            k = jnp.where(live, k_ref[:, cols], jnp.zeros((), BF16))
            s = lax.dot_general(k, v_ref[:, cols], (((0,), (0,)), ((), ())), preferred_element_type=F32)
            o_ref[0, cols, :] = s.astype(BF16)

    def slot(g, m):
        return (g ^ m[1], 0, 0) if steps > 1 else (0, 0, 0)

    return call(
        kernel,
        (steps,),
        [pl.BlockSpec((rows, part), lambda g, m: (0, g))] * 2,
        pl.BlockSpec((1, part, DH), slot),
        jax.ShapeDtypeStruct((steps, part, DH), BF16),
        2 * rows * width * DH,
        2 * 2 * rows * width,
    )(meta, key, value)


def within_block(meta, query, key, value, doc_count):
    rows, width = query.shape
    part = DH
    for heads in (4, 3, 2):
        if width % (heads * DH) == 0:
            part = heads * DH
            break
    tile = rows // 2

    def kernel(meta_ref, q_ref, k_ref, v_ref, o_ref, mask_ref):
        @pl.when(pl.program_id(0) == 0)
        def _():
            offset = meta_ref[0] * rows
            t = lax.broadcasted_iota(jnp.int32, (rows, rows), 0)
            s = lax.broadcasted_iota(jnp.int32, (rows, rows), 1)
            pos = lax.broadcasted_iota(jnp.int32, (rows, 1), 0)
            first = jnp.zeros((rows, 1), jnp.int32)
            bound = -offset
            for d in range(doc_count):
                bound = bound + meta_ref[LENS + d]
                first = jnp.where(bound <= pos, bound, first)
            mask_ref[...] = jnp.where((s <= t) & (s >= first), 1.0, 0.0).astype(BF16)

        for h in range(part // DH):
            cols = slice(h * DH, (h + 1) * DH)
            for i in range(2):
                r = slice(i * tile, (i + 1) * tile)
                seen = (i + 1) * tile
                scores = lax.dot_general(
                    q_ref[r, cols], k_ref[:seen, cols], (((1,), (1,)), ((), ())), preferred_element_type=F32
                )
                scores = scores.astype(BF16) * mask_ref[r, :seen]
                o_ref[r, cols] = jnp.dot(scores, v_ref[:seen, cols], preferred_element_type=F32)

    spec = pl.BlockSpec((rows, part), lambda g, m: (0, g))
    return call(
        kernel,
        (width // part,),
        [spec] * 3,
        spec,
        jax.ShapeDtypeStruct((rows, width), F32),
        3 * rows * rows * width,
        10 * rows * width,
        [pltpu.VMEM((rows, rows), BF16)],
    )(meta, query, key, value)


def norm_heads(meta, query, within, carry, gain, doc_count, slot):
    rows, width = query.shape
    part = carry.shape[0]

    def kernel(meta_ref, q_ref, w_ref, c_ref, g_ref, o_ref):
        offset = meta_ref[0] * rows
        begins = doc_start(meta_ref, doc_count, offset)
        bound = jnp.int32(0)
        end = jnp.int32(0)
        for d in range(doc_count):
            previous = bound
            bound = bound + meta_ref[LENS + d]
            end = jnp.where(previous <= offset, bound, end)
        stop = jnp.where(begins < offset, end - offset, 0)
        cross = lax.broadcasted_iota(jnp.int32, (rows, DH), 0) < stop
        for h in range(part // DH):
            cols = slice(h * DH, (h + 1) * DH)
            term = jnp.dot(q_ref[:, cols], c_ref[cols, :], preferred_element_type=F32)
            mixture = w_ref[:, cols] + jnp.where(cross, term, 0.0)
            mean = jnp.mean(mixture * mixture, axis=-1, keepdims=True)
            o_ref[:, cols] = (mixture * lax.rsqrt(mean + 1e-06) * g_ref[:, cols]).astype(BF16)

    def block(i, m):
        return (0, 0) if slot is None else (0, m[1] ^ slot)

    spec = pl.BlockSpec((rows, part), block)
    return call(
        kernel,
        (1,),
        [spec, spec, pl.BlockSpec((part, DH), lambda i, m: (0, 0)), pl.BlockSpec((1, part), block)],
        pl.BlockSpec((rows, part), lambda i, m: (0, 0)),
        jax.ShapeDtypeStruct((rows, part), BF16),
        2 * rows * part * DH,
        8 * rows * part,
    )(meta, query, within, carry, gain.reshape(1, width))


def project_own(meta, pieces, weight, columns):
    rows, part = pieces[0].shape
    tile = columns // 4
    count = len(pieces)

    def kernel(meta_ref, *refs):
        ns, ws, o_ref = refs[:count], refs[count : 2 * count], refs[-1]
        total = jnp.dot(ns[0][...], ws[0][...], preferred_element_type=F32)
        for n, w in zip(ns[1:], ws[1:]):
            total = total + jnp.dot(n[...], w[...], preferred_element_type=F32)
        o_ref[...] = total

    return call(
        kernel,
        (4,),
        [pl.BlockSpec((rows, part), lambda n, m: (0, 0))] * count
        + [pl.BlockSpec((part, tile), lambda n, m, s=s: (m[1] ^ s, m[2] * 4 + n)) for s in range(count)],
        pl.BlockSpec((rows, tile), lambda n, m: (0, n)),
        jax.ShapeDtypeStruct((rows, columns), F32),
        2 * rows * part * count * columns,
        2 * part * count * columns + 4 * rows * columns,
    )(meta, *pieces, *[weight] * count)


def project_more(meta, total, pieces, weights, dtype):
    rows, columns = total.shape
    part = pieces[0].shape[1]
    count, ranges = len(pieces), len(weights[0])
    steps = 2
    tile = columns // (ranges * steps)
    flat = [w for ws in weights for w in ws]

    def kernel(meta_ref, t_ref, *refs):
        ns, ws, o_ref = refs[:count], refs[count:-1], refs[-1]
        for c in range(ranges):

            @pl.when(pl.program_id(0) == c)
            def _():
                out = t_ref[...]
                for s in range(count):
                    out = out + jnp.dot(ns[s][...], ws[s * ranges + c][...], preferred_element_type=F32)
                o_ref[...] = out.astype(dtype)

    def column(c):
        return lambda g, n, m: (0, jnp.where(g < c, 0, jnp.where(g > c, steps - 1, n)))

    out_spec = pl.BlockSpec((rows, tile), lambda g, n, m: (0, g * steps + n))
    return call(
        kernel,
        (ranges, steps),
        [out_spec]
        + [pl.BlockSpec((rows, part), lambda g, n, m: (0, 0))] * count
        + [pl.BlockSpec((part, tile), column(c)) for _ in range(count) for c in range(ranges)],
        out_spec,
        jax.ShapeDtypeStruct((rows, columns), dtype),
        2 * rows * part * count * columns,
        2 * part * count * columns + 6 * rows * columns,
    )(meta, total, *pieces, *flat)


def body(n_seq, n_head, query, key, value, doc_lengths, gain, weight):
    rows, width = query.shape
    doc_count = doc_lengths.shape[0]
    plane = n_seq // PLANES
    columns = weight.shape[1] // n_head
    block = lax.axis_index("seq").astype(jnp.int32)
    group = lax.axis_index("head").astype(jnp.int32)
    member = block % plane
    meta = jnp.concatenate([
        jnp.stack([block, member, group]), jnp.zeros((LENS - 3,), jnp.int32), doc_lengths
    ])

    bounds = jnp.cumsum(doc_lengths)

    def first_block(token):
        starts = jnp.max(jnp.where(bounds <= token, bounds, 0))
        return starts // rows

    def weigh(condition):
        return condition.astype(F32)

    def swap(x, bit):
        return lax.ppermute(x, "seq", [(i, i ^ bit) for i in range(n_seq)])

    def flip(x):
        return lax.ppermute(x, "head", [(0, 1), (1, 0)])

    by_slot = (width // DH) % plane == 0
    steps = plane if by_slot else 1
    states = block_states(meta, key, value, doc_count, steps)
    if not by_slot:
        states = states.reshape(plane, width // plane, DH)[jnp.arange(plane, dtype=jnp.int32) ^ member]
    slots = [states[s] for s in range(plane)]

    pair = n_head == 2 and by_slot and plane == 4
    part = width // plane
    if pair:
        far_weight = lax.dynamic_slice(weight, (member * part, (1 - group) * columns), (part, columns))
        half = columns // 2
        w0 = [flip(far_weight[:, c * half : (c + 1) * half]) for c in range(2)]

    kept = []
    bit = 1
    while bit < plane:
        mine, send = slots[0::2], slots[1::2]
        got = swap(jnp.stack(send), bit)
        got = [got[i] for i in range(len(send))]
        upper = (member & bit) != 0
        unit = block & ~(2 * bit - 1)
        joined = weigh(first_block((unit + 2 * bit) * rows - 1) < unit + bit)
        own_factor = jnp.where(upper, 1.0, joined)
        got_factor = jnp.where(upper, joined, 1.0)
        kept.append((mine, got, bit, upper, unit))
        slots = [
            (own_factor * a.astype(F32) + got_factor * b.astype(F32)).astype(BF16) for a, b in zip(mine, got)
        ]
        bit *= 2
    base = block - member
    begins = first_block(base * rows)
    carry = jnp.zeros(slots[0].shape, F32)
    for d in range(PLANES - 1, 0, -1):
        shift = d * plane
        got = lax.ppermute(slots[0], "seq", [(i, i + shift) for i in range(n_seq - shift)])
        carry = carry + weigh((base - shift + plane - 1 >= begins) & (base >= shift)) * got.astype(F32)
    carries = [carry]

    for mine, got, bit, upper, unit in reversed(kept):
        middle = unit + bit
        begins = first_block(middle * rows)
        through, joined = weigh(begins < unit), weigh(begins < middle)
        ours, theirs = [], []
        for carry, a, b in zip(carries, mine, got):
            lower_state = jnp.where(upper, b, a).astype(F32)
            after = through * carry + joined * lower_state
            ours.append(jnp.where(upper, after, carry))
            theirs.append(jnp.where(upper, carry, after).astype(BF16))
        back = swap(jnp.stack(theirs), bit)
        carries = [x for i, c in enumerate(ours) for x in (c, back[i])]
    carries = [c.astype(BF16) for c in carries]

    within = within_block(meta, query, key, value, doc_count)
    if not pair:
        natural = jnp.stack(carries)[jnp.arange(plane, dtype=jnp.int32) ^ member].reshape(width, DH)
        normed = norm_heads(meta, query, within, natural, gain, doc_count, None)
        partial_sum = jnp.dot(normed, weight, preferred_element_type=F32)
        return lax.psum_scatter(partial_sum.astype(BF16), "head", scatter_dimension=1, tiled=True)

    order = (0, 2, 1, 3)
    normed = {s: norm_heads(meta, query, within, carries[s], gain, doc_count, s) for s in order}
    far = {s: flip(normed[s]) for s in order}
    w0 = list(lax.optimization_barrier((*w0, carries[2])))[:2]
    w2 = [swap(w, 2) for w in w0]
    w1 = [swap(w, 1) for w in w0]
    w3 = [swap(w, 1) for w in w2]
    weights = {0: w0, 1: w1, 2: w2, 3: w3}
    total = project_own(meta, [normed[s] for s in range(plane)], weight, columns)
    total = project_more(meta, total, [far[s] for s in order[:3]], [weights[s] for s in order[:3]], F32)
    return project_more(meta, total, [far[3]], [weights[3]], BF16)


def solution(mesh):
    return jax.shard_map(
        functools.partial(body, mesh.shape["seq"], mesh.shape["head"]),
        mesh=mesh,
        in_specs=(
            P("seq", "head"),
            P("seq", "head"),
            P("seq", "head"),
            P(),
            P("head"),
            P("head", None),
        ),
        out_specs=P("seq", "head"),
        check_vma=False,
    )
```

```python
import functools

import jax
import jax.numpy as jnp
from jax import lax
from jax.experimental import pallas as pl
from jax.experimental.pallas import tpu as pltpu
from jax.sharding import PartitionSpec as P

DH = 128
PLANES = 4
F32, BF16 = jnp.float32, jnp.bfloat16
LENS = 8
VMEM_LIMIT = 60 * 1024 * 1024


def doc_start(meta, doc_count, token):
    bound = jnp.int32(0)
    start = jnp.int32(0)
    for d in range(doc_count):
        bound = bound + meta[LENS + d]
        start = jnp.where(bound <= token, bound, start)
    return start


def call(kernel, grid, in_specs, out_specs, out_shape, flops, bytes_accessed, scratch=()):
    return pl.pallas_call(
        kernel,
        grid_spec=pltpu.PrefetchScalarGridSpec(
            num_scalar_prefetch=1,
            grid=grid,
            in_specs=in_specs,
            out_specs=out_specs,
            scratch_shapes=scratch,
        ),
        out_shape=out_shape,
        compiler_params=pltpu.CompilerParams(vmem_limit_bytes=VMEM_LIMIT),
        cost_estimate=pl.CostEstimate(flops=flops, bytes_accessed=bytes_accessed, transcendentals=0),
    )


def block_states(meta, key, value, doc_count, steps):
    rows, width = key.shape
    part = width // steps

    def kernel(meta_ref, k_ref, v_ref, o_ref):
        offset = meta_ref[0] * rows
        first = doc_start(meta_ref, doc_count, offset + rows - 1) - offset
        live = lax.broadcasted_iota(jnp.int32, (rows, DH), 0) >= first
        for h in range(part // DH):
            cols = slice(h * DH, (h + 1) * DH)
            k = jnp.where(live, k_ref[:, cols], jnp.zeros((), BF16))
            s = lax.dot_general(k, v_ref[:, cols], (((0,), (0,)), ((), ())), preferred_element_type=F32)
            o_ref[0, cols, :] = s.astype(BF16)

    def slot(g, m):
        return (g ^ m[1], 0, 0) if steps > 1 else (0, 0, 0)

    return call(
        kernel,
        (steps,),
        [pl.BlockSpec((rows, part), lambda g, m: (0, g))] * 2,
        pl.BlockSpec((1, part, DH), slot),
        jax.ShapeDtypeStruct((steps, part, DH), BF16),
        2 * rows * width * DH,
        2 * 2 * rows * width,
    )(meta, key, value)


def within_block(meta, query, key, value, doc_count):
    rows, width = query.shape
    part = DH
    for heads in (4, 3, 2):
        if width % (heads * DH) == 0:
            part = heads * DH
            break
    tile = rows // 2

    def kernel(meta_ref, q_ref, k_ref, v_ref, o_ref, mask_ref):
        @pl.when(pl.program_id(0) == 0)
        def _():
            offset = meta_ref[0] * rows
            t = lax.broadcasted_iota(jnp.int32, (rows, rows), 0)
            s = lax.broadcasted_iota(jnp.int32, (rows, rows), 1)
            pos = lax.broadcasted_iota(jnp.int32, (rows, 1), 0)
            first = jnp.zeros((rows, 1), jnp.int32)
            bound = -offset
            for d in range(doc_count):
                bound = bound + meta_ref[LENS + d]
                first = jnp.where(bound <= pos, bound, first)
            mask_ref[...] = jnp.where((s <= t) & (s >= first), 1.0, 0.0).astype(BF16)

        for h in range(part // DH):
            cols = slice(h * DH, (h + 1) * DH)
            for i in range(2):
                r = slice(i * tile, (i + 1) * tile)
                seen = (i + 1) * tile
                scores = lax.dot_general(
                    q_ref[r, cols], k_ref[:seen, cols], (((1,), (1,)), ((), ())), preferred_element_type=F32
                )
                scores = scores.astype(BF16) * mask_ref[r, :seen]
                o_ref[r, cols] = jnp.dot(scores, v_ref[:seen, cols], preferred_element_type=F32)

    spec = pl.BlockSpec((rows, part), lambda g, m: (0, g))
    return call(
        kernel,
        (width // part,),
        [spec] * 3,
        spec,
        jax.ShapeDtypeStruct((rows, width), F32),
        3 * rows * rows * width,
        10 * rows * width,
        [pltpu.VMEM((rows, rows), BF16)],
    )(meta, query, key, value)


def whole(shape):
    return pl.BlockSpec(shape, lambda *_: (0,) * len(shape))


def after(meta, *arrays):
    return lax.optimization_barrier((meta, *arrays))[0]


def factor(condition):
    return jnp.where(condition, 1.0, 0.0)


def split_states(meta, key, value, doc_count):
    rows, width = key.shape
    part = width // 4

    def slot(g):
        return jnp.where(g < 2, 2 * g + 1, 2 * g - 4)

    def kernel(meta_ref, k_ref, v_ref, send_ref, keep_ref):
        offset = meta_ref[0] * rows
        first = doc_start(meta_ref, doc_count, offset + rows - 1) - offset
        live = lax.broadcasted_iota(jnp.int32, (rows, DH), 0) >= first
        for h in range(part // DH):
            cols = slice(h * DH, (h + 1) * DH)
            k = jnp.where(live, k_ref[:, cols], jnp.zeros((), BF16))
            s = lax.dot_general(k, v_ref[:, cols], (((0,), (0,)), ((), ())), preferred_element_type=F32)
            s = s.astype(BF16)

            @pl.when(pl.program_id(0) < 2)
            def _():
                send_ref[0, cols, :] = s

            @pl.when(pl.program_id(0) >= 2)
            def _():
                keep_ref[0, cols, :] = s

    return call(
        kernel,
        (4,),
        [pl.BlockSpec((rows, part), lambda g, m: (0, slot(g) ^ m[1]))] * 2,
        [
            pl.BlockSpec((1, part, DH), lambda g, m: (jnp.minimum(g, 1), 0, 0)),
            pl.BlockSpec((1, part, DH), lambda g, m: (jnp.maximum(g - 2, 0), 0, 0)),
        ],
        [jax.ShapeDtypeStruct((2, part, DH), BF16)] * 2,
        2 * rows * width * DH,
        2 * 2 * rows * width,
    )(meta, key, value)


def within_slots(meta, query, key, value, doc_count, slots, dtype, with_query):
    rows, width = query.shape
    part = width // 4
    tile = rows // 2

    def kernel(meta_ref, q_ref, k_ref, v_ref, o_ref, *rest):
        mask_ref = rest[-1]

        @pl.when(pl.program_id(0) == 0)
        def _():
            offset = meta_ref[0] * rows
            t = lax.broadcasted_iota(jnp.int32, (rows, rows), 0)
            s = lax.broadcasted_iota(jnp.int32, (rows, rows), 1)
            pos = lax.broadcasted_iota(jnp.int32, (rows, 1), 0)
            first = jnp.zeros((rows, 1), jnp.int32)
            bound = -offset
            for d in range(doc_count):
                bound = bound + meta_ref[LENS + d]
                first = jnp.where(bound <= pos, bound, first)
            mask_ref[...] = jnp.where((s <= t) & (s >= first), 1.0, 0.0).astype(BF16)

        for h in range(part // DH):
            cols = slice(h * DH, (h + 1) * DH)
            for i in range(2):
                r = slice(i * tile, (i + 1) * tile)
                seen = (i + 1) * tile
                scores = lax.dot_general(
                    q_ref[r, cols], k_ref[:seen, cols], (((1,), (1,)), ((), ())), preferred_element_type=F32
                )
                scores = scores.astype(BF16) * mask_ref[r, :seen]
                o_ref[r, cols] = jnp.dot(scores, v_ref[:seen, cols], preferred_element_type=F32).astype(dtype)
        if with_query:
            rest[0][...] = q_ref[...]

    count = len(slots)
    spec = pl.BlockSpec((rows, part), lambda g, m: (0, (g + slots[0]) ^ m[1]))
    out = pl.BlockSpec((rows, part), lambda g, m: (0, g))
    shape = (rows, part * count)
    return call(
        kernel,
        (count,),
        [spec] * 3,
        [out] * (1 + with_query),
        [jax.ShapeDtypeStruct(shape, dtype)] + [jax.ShapeDtypeStruct(shape, BF16)] * with_query,
        3 * rows * rows * part * count,
        10 * rows * part * count,
        [pltpu.VMEM((rows, rows), BF16)],
    )(meta, query, key, value)


def small(kernel, meta, arrays, shape, count):
    return call(
        kernel,
        (1,),
        [whole(a.shape) for a in arrays],
        [whole(shape)] * count,
        [jax.ShapeDtypeStruct(shape, BF16)] * count,
        shape[0] * shape[1],
        2 * shape[0] * shape[1] * (len(arrays) + count),
    )(meta, *arrays)


def join_core(meta, keep, got, rows, doc_count):
    def kernel(meta_ref, keep_ref, got_ref, a_ref, b_ref):
        low = meta_ref[0] & -2
        joined = factor(doc_start(meta_ref, doc_count, (low + 2) * rows - 1) < (low + 1) * rows)
        upper = (meta_ref[1] & 1) != 0
        own, other = jnp.where(upper, 1.0, joined), jnp.where(upper, joined, 1.0)
        for i, o_ref in enumerate((a_ref, b_ref)):
            o_ref[...] = (own * keep_ref[i].astype(F32) + other * got_ref[i].astype(F32)).astype(BF16)

    return small(kernel, meta, (keep, got), keep.shape[1:], 2)


def join_chips(meta, mine, got, rows, doc_count):
    def kernel(meta_ref, a_ref, b_ref, o_ref):
        low = meta_ref[0] & -4
        joined = factor(doc_start(meta_ref, doc_count, (low + 4) * rows - 1) < (low + 2) * rows)
        upper = (meta_ref[1] & 2) != 0
        own, other = jnp.where(upper, 1.0, joined), jnp.where(upper, joined, 1.0)
        o_ref[...] = (own * a_ref[...].astype(F32) + other * b_ref[...].astype(F32)).astype(BF16)

    return small(kernel, meta, (mine, got), mine.shape, 1)[0]


def join_planes(meta, plane_sum, previous, rows, doc_count):
    def kernel(meta_ref, a_ref, b_ref, o_ref):
        low = meta_ref[0] & -4
        joined = factor(doc_start(meta_ref, doc_count, (low + 4) * rows - 1) < low * rows)
        o_ref[...] = (a_ref[...].astype(F32) + joined * b_ref[...].astype(F32)).astype(BF16)

    return small(kernel, meta, (plane_sum, previous), plane_sum.shape, 1)[0]


def carry_in_chip(meta_ref, chip, keep, got, rows, doc_count):
    low = meta_ref[0] & -2
    begins = doc_start(meta_ref, doc_count, (low + 1) * rows)
    through, joined = factor(begins < low * rows), factor(begins < (low + 1) * rows)
    upper = (meta_ref[1] & 1) != 0
    later = through * chip + joined * jnp.where(upper, got, keep).astype(F32)
    return jnp.where(upper, later, chip), jnp.where(upper, chip, later)


def carry_first(meta, near, far, mine, got, keep, core_got, rows, doc_count):
    def kernel(meta_ref, near_ref, far_ref, a_ref, b_ref, keep_ref, got_ref, o_ref, core_ref, chip_ref):
        low = meta_ref[0] & -4
        begins = doc_start(meta_ref, doc_count, low * rows)
        first = factor(begins < low * rows) * near_ref[...].astype(F32)
        first = first + factor(begins < (low - 4) * rows) * far_ref[...].astype(F32)
        begins = doc_start(meta_ref, doc_count, (low + 2) * rows)
        through, joined = factor(begins < low * rows), factor(begins < (low + 2) * rows)
        upper = (meta_ref[1] & 2) != 0
        later = through * first + joined * jnp.where(upper, b_ref[...], a_ref[...]).astype(F32)
        chip_ref[...] = jnp.where(upper, first, later).astype(BF16)
        chip = jnp.where(upper, later, first)
        ours, theirs = carry_in_chip(meta_ref, chip, keep_ref[0], got_ref[0], rows, doc_count)
        o_ref[...] = ours.astype(BF16)
        core_ref[...] = theirs.astype(BF16)

    return small(kernel, meta, (near, far, mine, got, keep, core_got), mine.shape, 3)


def carry_second(meta, chip, keep, core_got, rows, doc_count):
    def kernel(meta_ref, chip_ref, keep_ref, got_ref, o_ref, core_ref):
        ours, theirs = carry_in_chip(
            meta_ref, chip_ref[...].astype(F32), keep_ref[1], got_ref[1], rows, doc_count
        )
        o_ref[...] = ours.astype(BF16)
        core_ref[...] = theirs.astype(BF16)

    return small(kernel, meta, (chip, keep, core_got), chip.shape, 2)


def norm_heads(meta, query, within, carry, gain, doc_count, slots=(None, None, None)):
    rows = query.shape[0]
    part = carry.shape[0]

    def kernel(meta_ref, q_ref, w_ref, c_ref, g_ref, o_ref):
        offset = meta_ref[0] * rows
        begins = doc_start(meta_ref, doc_count, offset)
        bound = jnp.int32(0)
        end = jnp.int32(0)
        for d in range(doc_count):
            previous = bound
            bound = bound + meta_ref[LENS + d]
            end = jnp.where(previous <= offset, bound, end)
        stop = jnp.where(begins < offset, end - offset, 0)
        cross = lax.broadcasted_iota(jnp.int32, (rows, DH), 0) < stop
        for h in range(part // DH):
            cols = slice(h * DH, (h + 1) * DH)
            term = jnp.dot(q_ref[:, cols], c_ref[cols, :], preferred_element_type=F32)
            mixture = w_ref[:, cols].astype(F32) + jnp.where(cross, term, 0.0)
            mean = jnp.mean(mixture * mixture, axis=-1, keepdims=True)
            o_ref[:, cols] = (mixture * lax.rsqrt(mean + 1e-06) * g_ref[:, cols]).astype(BF16)

    def block(place):
        if place is None:
            return lambda i, m: (0, 0)
        if isinstance(place, int):
            return lambda i, m: (0, place)
        return lambda i, m: (0, m[1] ^ place[1])

    return call(
        kernel,
        (1,),
        [
            pl.BlockSpec((rows, part), block(slots[0])),
            pl.BlockSpec((rows, part), block(slots[1])),
            whole((part, DH)),
            pl.BlockSpec((1, part), block(slots[2])),
        ],
        whole((rows, part)),
        jax.ShapeDtypeStruct((rows, part), BF16),
        2 * rows * part * DH,
        8 * rows * part,
    )(meta, query, within, carry, gain.reshape(1, -1))


TILES = 4


def project_own(meta, pieces, weight, columns):
    rows, part = pieces[0].shape
    tile = columns // TILES
    count = len(pieces)

    def kernel(meta_ref, *refs):
        ns, ws, o_ref = refs[:count], refs[count : 2 * count], refs[-1]
        n = jnp.concatenate([r[...] for r in ns], axis=1)
        w = jnp.concatenate([r[...] for r in ws], axis=0)
        o_ref[...] = jnp.dot(n, w, preferred_element_type=F32)

    return call(
        kernel,
        (TILES,),
        [whole((rows, part))] * count
        + [pl.BlockSpec((part, tile), lambda n, m, s=s: (m[1] ^ s, m[2] * TILES + n)) for s in range(count)],
        pl.BlockSpec((rows, tile), lambda n, m: (0, n)),
        jax.ShapeDtypeStruct((rows, columns), F32),
        2 * rows * part * count * columns,
        2 * part * count * columns + 4 * rows * columns,
    )(meta, *pieces, *[weight] * count)


def project_more(meta, total, pieces, weights, dtype):
    rows, columns = total.shape
    part = pieces[0].shape[1]
    tile = columns // TILES
    count = len(pieces)
    flat = []
    for ws in weights:
        start = 0
        for w in ws:
            tiles = w.shape[1] // tile
            flat.append((w, start, tiles))
            start += tiles

    def kernel(meta_ref, t_ref, *refs):
        ns, ws, o_ref = refs[:count], refs[count:-1], refs[-1]
        n = jnp.concatenate([r[...] for r in ns], axis=1)
        for c in range(TILES):

            @pl.when(pl.program_id(0) == c)
            def _():
                held = [r[...] for r, (_, start, tiles) in zip(ws, flat) if start <= c < start + tiles]
                w = jnp.concatenate(held, axis=0)
                o_ref[...] = (t_ref[...] + jnp.dot(n, w, preferred_element_type=F32)).astype(dtype)

    def column(start, tiles):
        return lambda n, m: (0, jnp.clip(n - start, 0, tiles - 1))

    out_spec = pl.BlockSpec((rows, tile), lambda n, m: (0, n ^ (m[3] * (TILES // 2))))
    return call(
        kernel,
        (TILES,),
        [out_spec]
        + [whole((rows, part))] * count
        + [pl.BlockSpec((part, tile), column(start, tiles)) for _, start, tiles in flat],
        out_spec,
        jax.ShapeDtypeStruct((rows, columns), dtype),
        2 * rows * part * count * columns,
        2 * part * count * columns + 6 * rows * columns,
    )(meta, total, *pieces, *[w for w, _, _ in flat])


def pair_body(n_seq, query, key, value, doc_lengths, gain, weight):
    rows, width = query.shape
    docs = doc_lengths.shape[0]
    plane, part = 4, width // 4
    columns = weight.shape[1] // 2
    half = columns // 2
    block = lax.axis_index("seq").astype(jnp.int32)
    group = lax.axis_index("head").astype(jnp.int32)
    member = block % plane
    side = (block // plane) % 2
    meta = jnp.concatenate([
        jnp.stack([block, member, group, side]), jnp.zeros((LENS - 4,), jnp.int32), doc_lengths
    ])

    def swap(x, bit):
        return lax.ppermute(x, "seq", [(i, i ^ bit) for i in range(n_seq)])

    def shift(x, count):
        return lax.ppermute(x, "seq", [(i, i + count) for i in range(n_seq - count)])

    def flip(x):
        return lax.ppermute(x, "head", [(0, 1), (1, 0)])

    def behind(x, *arrays):
        return lax.optimization_barrier((x, *arrays))[0]

    sent_weight = lax.dynamic_slice(
        weight, (member * part, (1 - group) * columns + side * half), (part, half)
    )
    far_gain = flip(lax.dynamic_slice(gain, ((member ^ 3) * part,), (part,)))
    w0 = [flip(sent_weight), None]

    send, keep = split_states(after(meta, sent_weight), key, value, docs)
    core_got = swap(send, 1)
    within3, query3 = within_slots(after(meta, send), query, key, value, docs, (3,), BF16, True)
    far_query, far_within = flip(query3), flip(within3)
    chip0, chip2 = join_core(after(meta, within3), keep, core_got, rows, docs)
    chip_got = swap(chip2, 2)
    (within,) = within_slots(after(meta, chip0), query, key, value, docs, (0, 1, 2), F32, False)
    plane_sum = join_chips(after(meta, within), chip0, chip_got, rows, docs)
    near = shift(plane_sum, plane)
    both = join_planes(after(meta, w0[0]), plane_sum, near, rows, docs)
    far = shift(both, 2 * plane)
    carry0, core_carry0, chip_carry = carry_first(
        meta, near, far, chip0, chip_got, keep, core_got, rows, docs
    )
    carry1 = swap(core_carry0, 1)
    chip_carry2 = swap(chip_carry, 2)

    def norm(slot, carry):
        return norm_heads(
            meta,
            query,
            within3 if slot == 3 else within,
            carry,
            gain,
            docs,
            (("slot", slot), None if slot == 3 else slot, ("slot", slot)),
        )

    normed0 = norm(0, carry0)
    far0 = flip(normed0)
    normed1 = norm(1, carry1)
    far1 = flip(normed1)
    carry2, core_carry2 = carry_second(meta, chip_carry2, keep, core_got, rows, docs)
    carry3 = swap(core_carry2, 1)
    far_carry3 = flip(carry3)
    normed2 = norm(2, carry2)
    far2 = flip(behind(normed2, carry3))
    normed3 = norm(3, carry3)

    w0[1] = swap(behind(w0[0], far), plane)
    quarter = half // 2
    w2 = [swap(w0[0], 2)]
    w2.append(swap(w0[1][:, :quarter], 2))
    w2.append(swap(w2[0][:, quarter:], plane))
    w1 = [swap(w, 1) for w in w0]
    w3 = [swap(w, 1) for w in w2]

    total = project_own(meta, [normed0, normed1, normed2, normed3], weight, columns)
    total = project_more(meta, total, [far0, far1], [w0, w1], F32)
    far3 = norm_heads(meta, far_query, far_within, far_carry3, far_gain, docs)
    return project_more(meta, total, [far2, far3], [w2, w3], BF16)


def body(n_seq, n_head, query, key, value, doc_lengths, gain, weight):
    rows, width = query.shape
    doc_count = doc_lengths.shape[0]
    plane = n_seq // PLANES
    if n_head == 2 and plane == 4 and width % (4 * DH) == 0:
        return pair_body(n_seq, query, key, value, doc_lengths, gain, weight)
    block = lax.axis_index("seq").astype(jnp.int32)
    group = lax.axis_index("head").astype(jnp.int32)
    member = block % plane
    meta = jnp.concatenate([
        jnp.stack([block, member, group]), jnp.zeros((LENS - 3,), jnp.int32), doc_lengths
    ])

    bounds = jnp.cumsum(doc_lengths)

    def first_block(token):
        starts = jnp.max(jnp.where(bounds <= token, bounds, 0))
        return starts // rows

    def weigh(condition):
        return condition.astype(F32)

    def swap(x, bit):
        return lax.ppermute(x, "seq", [(i, i ^ bit) for i in range(n_seq)])

    by_slot = (width // DH) % plane == 0
    steps = plane if by_slot else 1
    states = block_states(meta, key, value, doc_count, steps)
    if not by_slot:
        states = states.reshape(plane, width // plane, DH)[jnp.arange(plane, dtype=jnp.int32) ^ member]
    slots = [states[s] for s in range(plane)]

    kept = []
    bit = 1
    while bit < plane:
        mine, send = slots[0::2], slots[1::2]
        got = swap(jnp.stack(send), bit)
        got = [got[i] for i in range(len(send))]
        upper = (member & bit) != 0
        unit = block & ~(2 * bit - 1)
        joined = weigh(first_block((unit + 2 * bit) * rows - 1) < unit + bit)
        own_factor = jnp.where(upper, 1.0, joined)
        got_factor = jnp.where(upper, joined, 1.0)
        kept.append((mine, got, bit, upper, unit))
        slots = [
            (own_factor * a.astype(F32) + got_factor * b.astype(F32)).astype(BF16) for a, b in zip(mine, got)
        ]
        bit *= 2
    base = block - member
    begins = first_block(base * rows)
    carry = jnp.zeros(slots[0].shape, F32)
    for d in range(PLANES - 1, 0, -1):
        shift = d * plane
        got = lax.ppermute(slots[0], "seq", [(i, i + shift) for i in range(n_seq - shift)])
        carry = carry + weigh((base - shift + plane - 1 >= begins) & (base >= shift)) * got.astype(F32)
    carries = [carry]

    for mine, got, bit, upper, unit in reversed(kept):
        middle = unit + bit
        begins = first_block(middle * rows)
        through, joined = weigh(begins < unit), weigh(begins < middle)
        ours, theirs = [], []
        for carry, a, b in zip(carries, mine, got):
            lower_state = jnp.where(upper, b, a).astype(F32)
            after = through * carry + joined * lower_state
            ours.append(jnp.where(upper, after, carry))
            theirs.append(jnp.where(upper, carry, after).astype(BF16))
        back = swap(jnp.stack(theirs), bit)
        carries = [x for i, c in enumerate(ours) for x in (c, back[i])]
    carries = [c.astype(BF16) for c in carries]

    within = within_block(meta, query, key, value, doc_count)
    natural = jnp.stack(carries)[jnp.arange(plane, dtype=jnp.int32) ^ member].reshape(width, DH)
    normed = norm_heads(meta, query, within, natural, gain, doc_count)
    partial_sum = jnp.dot(normed, weight, preferred_element_type=F32)
    return lax.psum_scatter(partial_sum.astype(BF16), "head", scatter_dimension=1, tiled=True)


def solution(mesh):
    return jax.shard_map(
        functools.partial(body, mesh.shape["seq"], mesh.shape["head"]),
        mesh=mesh,
        in_specs=(
            P("seq", "head"),
            P("seq", "head"),
            P("seq", "head"),
            P(),
            P("head"),
            P("head", None),
        ),
        out_specs=P("seq", "head"),
        check_vma=False,
    )
```

```python
import functools

import jax
import jax.numpy as jnp
from jax import lax
from jax.experimental import pallas as pl
from jax.experimental.pallas import tpu as pltpu
from jax.sharding import PartitionSpec as P

DH = 128
PLANES = 4
F32, BF16 = jnp.float32, jnp.bfloat16
LENS = 8
VMEM_LIMIT = 16 * 1024 * 1024


def doc_start(meta, doc_count, token):
    bound = jnp.int32(0)
    start = jnp.int32(0)
    for d in range(doc_count):
        bound = bound + meta[LENS + d]
        start = jnp.where(bound <= token, bound, start)
    return start


def call(kernel, grid, in_specs, out_specs, out_shape, flops, bytes_accessed, scratch=()):
    return pl.pallas_call(
        kernel,
        grid_spec=pltpu.PrefetchScalarGridSpec(
            num_scalar_prefetch=1,
            grid=grid,
            in_specs=in_specs,
            out_specs=out_specs,
            scratch_shapes=scratch,
        ),
        out_shape=out_shape,
        compiler_params=pltpu.CompilerParams(vmem_limit_bytes=VMEM_LIMIT),
        cost_estimate=pl.CostEstimate(flops=flops, bytes_accessed=bytes_accessed, transcendentals=0),
    )


def block_states(meta, key, value, doc_count, steps):
    rows, width = key.shape
    part = width // steps

    def kernel(meta_ref, k_ref, v_ref, o_ref):
        offset = meta_ref[0] * rows
        first = doc_start(meta_ref, doc_count, offset + rows - 1) - offset
        live = lax.broadcasted_iota(jnp.int32, (rows, DH), 0) >= first
        for h in range(part // DH):
            cols = slice(h * DH, (h + 1) * DH)
            k = jnp.where(live, k_ref[:, cols], jnp.zeros((), BF16))
            s = lax.dot_general(k, v_ref[:, cols], (((0,), (0,)), ((), ())), preferred_element_type=F32)
            o_ref[0, cols, :] = s.astype(BF16)

    def slot(g, m):
        return (g ^ m[1], 0, 0) if steps > 1 else (0, 0, 0)

    return call(
        kernel,
        (steps,),
        [pl.BlockSpec((rows, part), lambda g, m: (0, g))] * 2,
        pl.BlockSpec((1, part, DH), slot),
        jax.ShapeDtypeStruct((steps, part, DH), BF16),
        2 * rows * width * DH,
        2 * 2 * rows * width,
    )(meta, key, value)


def within_block(meta, query, key, value, doc_count):
    rows, width = query.shape
    part = DH
    for heads in (4, 3, 2):
        if width % (heads * DH) == 0:
            part = heads * DH
            break
    tile = rows // 2

    def kernel(meta_ref, q_ref, k_ref, v_ref, o_ref, mask_ref):
        @pl.when(pl.program_id(0) == 0)
        def _():
            offset = meta_ref[0] * rows
            t = lax.broadcasted_iota(jnp.int32, (rows, rows), 0)
            s = lax.broadcasted_iota(jnp.int32, (rows, rows), 1)
            pos = lax.broadcasted_iota(jnp.int32, (rows, 1), 0)
            first = jnp.zeros((rows, 1), jnp.int32)
            bound = -offset
            for d in range(doc_count):
                bound = bound + meta_ref[LENS + d]
                first = jnp.where(bound <= pos, bound, first)
            mask_ref[...] = jnp.where((s <= t) & (s >= first), 1.0, 0.0).astype(BF16)

        for h in range(part // DH):
            cols = slice(h * DH, (h + 1) * DH)
            for i in range(2):
                r = slice(i * tile, (i + 1) * tile)
                seen = (i + 1) * tile
                scores = lax.dot_general(
                    q_ref[r, cols], k_ref[:seen, cols], (((1,), (1,)), ((), ())), preferred_element_type=F32
                )
                scores = scores.astype(BF16) * mask_ref[r, :seen]
                o_ref[r, cols] = jnp.dot(scores, v_ref[:seen, cols], preferred_element_type=F32)

    spec = pl.BlockSpec((rows, part), lambda g, m: (0, g))
    return call(
        kernel,
        (width // part,),
        [spec] * 3,
        spec,
        jax.ShapeDtypeStruct((rows, width), F32),
        3 * rows * rows * width,
        10 * rows * width,
        [pltpu.VMEM((rows, rows), BF16)],
    )(meta, query, key, value)


def whole(shape):
    return pl.BlockSpec(shape, lambda *_: (0,) * len(shape))


def after(meta, *arrays):
    return lax.optimization_barrier((meta, *arrays))[0]


def factor(condition):
    return jnp.where(condition, 1.0, 0.0)


def split_states(meta, key, value, doc_count):
    rows, width = key.shape
    part = width // 4

    def slot(g):
        return jnp.where(g < 2, 2 * g + 1, 2 * g - 4)

    def kernel(meta_ref, k_ref, v_ref, send_ref, keep_ref):
        offset = meta_ref[0] * rows
        first = doc_start(meta_ref, doc_count, offset + rows - 1) - offset
        live = lax.broadcasted_iota(jnp.int32, (rows, DH), 0) >= first
        for h in range(part // DH):
            cols = slice(h * DH, (h + 1) * DH)
            k = jnp.where(live, k_ref[:, cols], jnp.zeros((), BF16))
            s = lax.dot_general(k, v_ref[:, cols], (((0,), (0,)), ((), ())), preferred_element_type=F32)
            s = s.astype(BF16)

            @pl.when(pl.program_id(0) < 2)
            def _():
                send_ref[0, cols, :] = s

            @pl.when(pl.program_id(0) >= 2)
            def _():
                keep_ref[0, cols, :] = s

    return call(
        kernel,
        (4,),
        [pl.BlockSpec((rows, part), lambda g, m: (0, slot(g) ^ m[1]))] * 2,
        [
            pl.BlockSpec((1, part, DH), lambda g, m: (jnp.minimum(g, 1), 0, 0)),
            pl.BlockSpec((1, part, DH), lambda g, m: (jnp.maximum(g - 2, 0), 0, 0)),
        ],
        [jax.ShapeDtypeStruct((2, part, DH), BF16)] * 2,
        2 * rows * width * DH,
        2 * 2 * rows * width,
    )(meta, key, value)


def within_slots(meta, query, key, value, doc_count, slots, dtype, with_query):
    rows, width = query.shape
    part = width // 4
    tile = rows // 2

    def kernel(meta_ref, q_ref, k_ref, v_ref, o_ref, *rest):
        mask_ref = rest[-1]

        @pl.when(pl.program_id(0) == 0)
        def _():
            offset = meta_ref[0] * rows
            t = lax.broadcasted_iota(jnp.int32, (rows, rows), 0)
            s = lax.broadcasted_iota(jnp.int32, (rows, rows), 1)
            pos = lax.broadcasted_iota(jnp.int32, (rows, 1), 0)
            first = jnp.zeros((rows, 1), jnp.int32)
            bound = -offset
            for d in range(doc_count):
                bound = bound + meta_ref[LENS + d]
                first = jnp.where(bound <= pos, bound, first)
            mask_ref[...] = jnp.where((s <= t) & (s >= first), 1.0, 0.0).astype(BF16)

        for h in range(part // DH):
            cols = slice(h * DH, (h + 1) * DH)
            for i in range(2):
                r = slice(i * tile, (i + 1) * tile)
                seen = (i + 1) * tile
                scores = lax.dot_general(
                    q_ref[r, cols], k_ref[:seen, cols], (((1,), (1,)), ((), ())), preferred_element_type=F32
                )
                scores = scores.astype(BF16) * mask_ref[r, :seen]
                o_ref[r, cols] = jnp.dot(scores, v_ref[:seen, cols], preferred_element_type=F32).astype(dtype)
        if with_query:
            rest[0][...] = q_ref[...]

    count = len(slots)
    spec = pl.BlockSpec((rows, part), lambda g, m: (0, (g + slots[0]) ^ m[1]))
    out = pl.BlockSpec((rows, part), lambda g, m: (0, g))
    shape = (rows, part * count)
    return call(
        kernel,
        (count,),
        [spec] * 3,
        [out] * (1 + with_query),
        [jax.ShapeDtypeStruct(shape, dtype)] + [jax.ShapeDtypeStruct(shape, BF16)] * with_query,
        3 * rows * rows * part * count,
        10 * rows * part * count,
        [pltpu.VMEM((rows, rows), BF16)],
    )(meta, query, key, value)


def small(kernel, meta, arrays, shape, count):
    return call(
        kernel,
        (1,),
        [whole(a.shape) for a in arrays],
        [whole(shape)] * count,
        [jax.ShapeDtypeStruct(shape, BF16)] * count,
        shape[0] * shape[1],
        2 * shape[0] * shape[1] * (len(arrays) + count),
    )(meta, *arrays)


def join_core(meta, keep, got, rows, doc_count):
    def kernel(meta_ref, keep_ref, got_ref, a_ref, b_ref):
        low = meta_ref[0] & -2
        joined = factor(doc_start(meta_ref, doc_count, (low + 2) * rows - 1) < (low + 1) * rows)
        upper = (meta_ref[1] & 1) != 0
        own, other = jnp.where(upper, 1.0, joined), jnp.where(upper, joined, 1.0)
        for i, o_ref in enumerate((a_ref, b_ref)):
            o_ref[...] = (own * keep_ref[i].astype(F32) + other * got_ref[i].astype(F32)).astype(BF16)

    return small(kernel, meta, (keep, got), keep.shape[1:], 2)


def join_chips(meta, mine, got, rows, doc_count):
    def kernel(meta_ref, a_ref, b_ref, o_ref):
        low = meta_ref[0] & -4
        joined = factor(doc_start(meta_ref, doc_count, (low + 4) * rows - 1) < (low + 2) * rows)
        upper = (meta_ref[1] & 2) != 0
        own, other = jnp.where(upper, 1.0, joined), jnp.where(upper, joined, 1.0)
        o_ref[...] = (own * a_ref[...].astype(F32) + other * b_ref[...].astype(F32)).astype(BF16)

    return small(kernel, meta, (mine, got), mine.shape, 1)[0]


def join_planes(meta, plane_sum, previous, rows, doc_count):
    def kernel(meta_ref, a_ref, b_ref, o_ref):
        low = meta_ref[0] & -4
        joined = factor(doc_start(meta_ref, doc_count, (low + 4) * rows - 1) < low * rows)
        o_ref[...] = (a_ref[...].astype(F32) + joined * b_ref[...].astype(F32)).astype(BF16)

    return small(kernel, meta, (plane_sum, previous), plane_sum.shape, 1)[0]


def carry_in_chip(meta_ref, chip, keep, got, rows, doc_count):
    low = meta_ref[0] & -2
    begins = doc_start(meta_ref, doc_count, (low + 1) * rows)
    through, joined = factor(begins < low * rows), factor(begins < (low + 1) * rows)
    upper = (meta_ref[1] & 1) != 0
    later = through * chip + joined * jnp.where(upper, got, keep).astype(F32)
    return jnp.where(upper, later, chip), jnp.where(upper, chip, later)


def carry_first(meta, near, far, mine, got, keep, core_got, rows, doc_count):
    def kernel(meta_ref, near_ref, far_ref, a_ref, b_ref, keep_ref, got_ref, o_ref, core_ref, chip_ref):
        low = meta_ref[0] & -4
        begins = doc_start(meta_ref, doc_count, low * rows)
        first = factor(begins < low * rows) * near_ref[...].astype(F32)
        first = first + factor(begins < (low - 4) * rows) * far_ref[...].astype(F32)
        begins = doc_start(meta_ref, doc_count, (low + 2) * rows)
        through, joined = factor(begins < low * rows), factor(begins < (low + 2) * rows)
        upper = (meta_ref[1] & 2) != 0
        later = through * first + joined * jnp.where(upper, b_ref[...], a_ref[...]).astype(F32)
        chip_ref[...] = jnp.where(upper, first, later).astype(BF16)
        chip = jnp.where(upper, later, first)
        ours, theirs = carry_in_chip(meta_ref, chip, keep_ref[0], got_ref[0], rows, doc_count)
        o_ref[...] = ours.astype(BF16)
        core_ref[...] = theirs.astype(BF16)

    return small(kernel, meta, (near, far, mine, got, keep, core_got), mine.shape, 3)


def carry_second(meta, chip, keep, core_got, rows, doc_count):
    def kernel(meta_ref, chip_ref, keep_ref, got_ref, o_ref, core_ref):
        ours, theirs = carry_in_chip(
            meta_ref, chip_ref[...].astype(F32), keep_ref[1], got_ref[1], rows, doc_count
        )
        o_ref[...] = ours.astype(BF16)
        core_ref[...] = theirs.astype(BF16)

    return small(kernel, meta, (chip, keep, core_got), chip.shape, 2)


def norm_heads(meta, query, within, carry, gain, doc_count, slots=(None, None, None)):
    rows = query.shape[0]
    part = carry.shape[0]

    def kernel(meta_ref, q_ref, w_ref, c_ref, g_ref, o_ref):
        offset = meta_ref[0] * rows
        begins = doc_start(meta_ref, doc_count, offset)
        bound = jnp.int32(0)
        end = jnp.int32(0)
        for d in range(doc_count):
            previous = bound
            bound = bound + meta_ref[LENS + d]
            end = jnp.where(previous <= offset, bound, end)
        stop = jnp.where(begins < offset, end - offset, 0)
        cross = lax.broadcasted_iota(jnp.int32, (rows, DH), 0) < stop
        for h in range(part // DH):
            cols = slice(h * DH, (h + 1) * DH)
            term = jnp.dot(q_ref[:, cols], c_ref[cols, :], preferred_element_type=F32)
            mixture = w_ref[:, cols].astype(F32) + jnp.where(cross, term, 0.0)
            mean = jnp.mean(mixture * mixture, axis=-1, keepdims=True)
            o_ref[:, cols] = (mixture * lax.rsqrt(mean + 1e-06) * g_ref[:, cols]).astype(BF16)

    def block(place):
        if place is None:
            return lambda i, m: (0, 0)
        if isinstance(place, int):
            return lambda i, m: (0, place)
        return lambda i, m: (0, m[1] ^ place[1])

    return call(
        kernel,
        (1,),
        [
            pl.BlockSpec((rows, part), block(slots[0])),
            pl.BlockSpec((rows, part), block(slots[1])),
            whole((part, DH)),
            pl.BlockSpec((1, part), block(slots[2])),
        ],
        whole((rows, part)),
        jax.ShapeDtypeStruct((rows, part), BF16),
        2 * rows * part * DH,
        8 * rows * part,
    )(meta, query, within, carry, gain.reshape(1, -1))


TILES = 4


def project_own(meta, pieces, weight, columns):
    rows, part = pieces[0].shape
    tile = columns // TILES
    count = len(pieces)

    def kernel(meta_ref, *refs):
        ns, ws, o_ref = refs[:count], refs[count : 2 * count], refs[-1]
        n = jnp.concatenate([r[...] for r in ns], axis=1)
        w = jnp.concatenate([r[...] for r in ws], axis=0)
        o_ref[...] = jnp.dot(n, w, preferred_element_type=F32)

    return call(
        kernel,
        (TILES,),
        [whole((rows, part))] * count
        + [pl.BlockSpec((part, tile), lambda n, m, s=s: (m[1] ^ s, m[2] * TILES + n)) for s in range(count)],
        pl.BlockSpec((rows, tile), lambda n, m: (0, n)),
        jax.ShapeDtypeStruct((rows, columns), F32),
        2 * rows * part * count * columns,
        2 * part * count * columns + 4 * rows * columns,
    )(meta, *pieces, *[weight] * count)


def project_more(meta, total, pieces, weights, dtype):
    rows, columns = total.shape
    part = pieces[0].shape[1]
    tile = columns // TILES
    count = len(pieces)
    flat = []
    for ws in weights:
        start = 0
        for w in ws:
            tiles = w.shape[1] // tile
            flat.append((w, start, tiles))
            start += tiles

    def kernel(meta_ref, t_ref, *refs):
        ns, ws, o_ref = refs[:count], refs[count:-1], refs[-1]
        n = jnp.concatenate([r[...] for r in ns], axis=1)
        for c in range(TILES):

            @pl.when(pl.program_id(0) == c)
            def _():
                held = [r[...] for r, (_, start, tiles) in zip(ws, flat) if start <= c < start + tiles]
                w = jnp.concatenate(held, axis=0)
                o_ref[...] = (t_ref[...] + jnp.dot(n, w, preferred_element_type=F32)).astype(dtype)

    def column(start, tiles):
        return lambda n, m: (0, jnp.clip(n - start, 0, tiles - 1))

    out_spec = pl.BlockSpec((rows, tile), lambda n, m: (0, n ^ (m[3] * (TILES // 2))))
    return call(
        kernel,
        (TILES,),
        [out_spec]
        + [whole((rows, part))] * count
        + [pl.BlockSpec((part, tile), column(start, tiles)) for _, start, tiles in flat],
        out_spec,
        jax.ShapeDtypeStruct((rows, columns), dtype),
        2 * rows * part * count * columns,
        2 * part * count * columns + 6 * rows * columns,
    )(meta, total, *pieces, *[w for w, _, _ in flat])


def pair_body(n_seq, query, key, value, doc_lengths, gain, weight):
    rows, width = query.shape
    docs = doc_lengths.shape[0]
    plane, part = 4, width // 4
    columns = weight.shape[1] // 2
    half = columns // 2
    block = lax.axis_index("seq").astype(jnp.int32)
    group = lax.axis_index("head").astype(jnp.int32)
    member = block % plane
    side = (block // plane) % 2
    meta = jnp.concatenate([
        jnp.stack([block, member, group, side]), jnp.zeros((LENS - 4,), jnp.int32), doc_lengths
    ])

    def swap(x, bit):
        return lax.ppermute(x, "seq", [(i, i ^ bit) for i in range(n_seq)])

    def shift(x, count):
        return lax.ppermute(x, "seq", [(i, i + count) for i in range(n_seq - count)])

    def flip(x):
        return lax.ppermute(x, "head", [(0, 1), (1, 0)])

    def behind(x, *arrays):
        return lax.optimization_barrier((x, *arrays))[0]

    sent_weight = lax.dynamic_slice(
        weight, (member * part, (1 - group) * columns + side * half), (part, half)
    )
    far_gain = flip(lax.dynamic_slice(gain, ((member ^ 3) * part,), (part,)))
    w0 = [flip(sent_weight), None]

    send, keep = split_states(after(meta, sent_weight), key, value, docs)
    core_got = swap(send, 1)
    within3, query3 = within_slots(after(meta, send), query, key, value, docs, (3,), BF16, True)
    far_query, far_within = flip(query3), flip(within3)
    chip0, chip2 = join_core(after(meta, within3, far_gain), keep, core_got, rows, docs)
    chip_got = swap(chip2, 2)
    (within,) = within_slots(after(meta, chip0), query, key, value, docs, (0, 1, 2), F32, False)
    plane_sum = join_chips(after(meta, within, w0[0]), chip0, chip_got, rows, docs)
    near = shift(plane_sum, plane)
    both = join_planes(after(meta, far_query), plane_sum, near, rows, docs)
    w2 = [swap(w0[0], 2)]
    far = shift(both, 2 * plane)
    carry0, core_carry0, chip_carry = carry_first(
        after(meta, far_within, w2[0]), near, far, chip0, chip_got, keep, core_got, rows, docs
    )
    carry1 = swap(core_carry0, 1)
    chip_carry2 = swap(chip_carry, 2)

    def norm(slot, carry):
        return norm_heads(
            meta,
            query,
            within3 if slot == 3 else within,
            carry,
            gain,
            docs,
            (("slot", slot), None if slot == 3 else slot, ("slot", slot)),
        )

    normed0 = norm(0, carry0)
    far0 = flip(normed0)
    normed1 = norm(1, carry1)
    far1 = flip(normed1)
    carry2, core_carry2 = carry_second(meta, chip_carry2, keep, core_got, rows, docs)
    carry3 = swap(core_carry2, 1)
    far_carry3 = flip(carry3)
    normed2 = norm(2, carry2)
    far2 = flip(behind(normed2, carry3))
    normed3 = norm(3, carry3)

    w0[1] = swap(behind(w0[0], far), plane)
    quarter = half // 2
    w2.append(swap(w0[1][:, :quarter], 2))
    w2.append(swap(w2[0][:, quarter:], plane))
    w1 = [swap(w, 1) for w in w0]
    w3 = [swap(w, 1) for w in w2]

    total = project_own(meta, [normed0, normed1, normed2, normed3], weight, columns)
    total = project_more(meta, total, [far0, far1], [w0, w1], F32)
    far3 = norm_heads(meta, far_query, far_within, far_carry3, far_gain, docs)
    return project_more(meta, total, [far2, far3], [w2, w3], BF16)


def body(n_seq, n_head, query, key, value, doc_lengths, gain, weight):
    rows, width = query.shape
    doc_count = doc_lengths.shape[0]
    plane = n_seq // PLANES
    if n_head == 2 and plane == 4 and width % (4 * DH) == 0:
        return pair_body(n_seq, query, key, value, doc_lengths, gain, weight)
    block = lax.axis_index("seq").astype(jnp.int32)
    group = lax.axis_index("head").astype(jnp.int32)
    member = block % plane
    meta = jnp.concatenate([
        jnp.stack([block, member, group]), jnp.zeros((LENS - 3,), jnp.int32), doc_lengths
    ])

    bounds = jnp.cumsum(doc_lengths)

    def first_block(token):
        starts = jnp.max(jnp.where(bounds <= token, bounds, 0))
        return starts // rows

    def weigh(condition):
        return condition.astype(F32)

    def swap(x, bit):
        return lax.ppermute(x, "seq", [(i, i ^ bit) for i in range(n_seq)])

    by_slot = (width // DH) % plane == 0
    steps = plane if by_slot else 1
    states = block_states(meta, key, value, doc_count, steps)
    if not by_slot:
        states = states.reshape(plane, width // plane, DH)[jnp.arange(plane, dtype=jnp.int32) ^ member]
    slots = [states[s] for s in range(plane)]

    kept = []
    bit = 1
    while bit < plane:
        mine, send = slots[0::2], slots[1::2]
        got = swap(jnp.stack(send), bit)
        got = [got[i] for i in range(len(send))]
        upper = (member & bit) != 0
        unit = block & ~(2 * bit - 1)
        joined = weigh(first_block((unit + 2 * bit) * rows - 1) < unit + bit)
        own_factor = jnp.where(upper, 1.0, joined)
        got_factor = jnp.where(upper, joined, 1.0)
        kept.append((mine, got, bit, upper, unit))
        slots = [
            (own_factor * a.astype(F32) + got_factor * b.astype(F32)).astype(BF16) for a, b in zip(mine, got)
        ]
        bit *= 2
    base = block - member
    begins = first_block(base * rows)
    carry = jnp.zeros(slots[0].shape, F32)
    for d in range(PLANES - 1, 0, -1):
        shift = d * plane
        got = lax.ppermute(slots[0], "seq", [(i, i + shift) for i in range(n_seq - shift)])
        carry = carry + weigh((base - shift + plane - 1 >= begins) & (base >= shift)) * got.astype(F32)
    carries = [carry]

    for mine, got, bit, upper, unit in reversed(kept):
        middle = unit + bit
        begins = first_block(middle * rows)
        through, joined = weigh(begins < unit), weigh(begins < middle)
        ours, theirs = [], []
        for carry, a, b in zip(carries, mine, got):
            lower_state = jnp.where(upper, b, a).astype(F32)
            after = through * carry + joined * lower_state
            ours.append(jnp.where(upper, after, carry))
            theirs.append(jnp.where(upper, carry, after).astype(BF16))
        back = swap(jnp.stack(theirs), bit)
        carries = [x for i, c in enumerate(ours) for x in (c, back[i])]
    carries = [c.astype(BF16) for c in carries]

    within = within_block(meta, query, key, value, doc_count)
    natural = jnp.stack(carries)[jnp.arange(plane, dtype=jnp.int32) ^ member].reshape(width, DH)
    normed = norm_heads(meta, query, within, natural, gain, doc_count)
    partial_sum = jnp.dot(normed, weight, preferred_element_type=F32)
    return lax.psum_scatter(partial_sum.astype(BF16), "head", scatter_dimension=1, tiled=True)


def solution(mesh):
    return jax.shard_map(
        functools.partial(body, mesh.shape["seq"], mesh.shape["head"]),
        mesh=mesh,
        in_specs=(
            P("seq", "head"),
            P("seq", "head"),
            P("seq", "head"),
            P(),
            P("head"),
            P("head", None),
        ),
        out_specs=P("seq", "head"),
        check_vma=False,
    )
```

```python
import functools

import jax
import jax.numpy as jnp
from jax import lax
from jax.experimental import pallas as pl
from jax.experimental.pallas import tpu as pltpu
from jax.sharding import PartitionSpec as P

DH = 128
PLANES = 4
F32, BF16 = jnp.float32, jnp.bfloat16
LENS = 8
VMEM_LIMIT = 16 * 1024 * 1024


def doc_start(meta, doc_count, token):
    bound = jnp.int32(0)
    start = jnp.int32(0)
    for d in range(doc_count):
        bound = bound + meta[LENS + d]
        start = jnp.where(bound <= token, bound, start)
    return start


def call(kernel, grid, in_specs, out_specs, out_shape, flops, bytes_accessed, scratch=()):
    return pl.pallas_call(
        kernel,
        grid_spec=pltpu.PrefetchScalarGridSpec(
            num_scalar_prefetch=1,
            grid=grid,
            in_specs=in_specs,
            out_specs=out_specs,
            scratch_shapes=scratch,
        ),
        out_shape=out_shape,
        compiler_params=pltpu.CompilerParams(vmem_limit_bytes=VMEM_LIMIT),
        cost_estimate=pl.CostEstimate(flops=flops, bytes_accessed=bytes_accessed, transcendentals=0),
    )


def block_states(meta, key, value, doc_count, steps):
    rows, width = key.shape
    part = width // steps

    def kernel(meta_ref, k_ref, v_ref, o_ref):
        offset = meta_ref[0] * rows
        first = doc_start(meta_ref, doc_count, offset + rows - 1) - offset
        live = lax.broadcasted_iota(jnp.int32, (rows, DH), 0) >= first
        for h in range(part // DH):
            cols = slice(h * DH, (h + 1) * DH)
            k = jnp.where(live, k_ref[:, cols], jnp.zeros((), BF16))
            s = lax.dot_general(k, v_ref[:, cols], (((0,), (0,)), ((), ())), preferred_element_type=F32)
            o_ref[0, cols, :] = s.astype(BF16)

    def slot(g, m):
        return (g ^ m[1], 0, 0) if steps > 1 else (0, 0, 0)

    return call(
        kernel,
        (steps,),
        [pl.BlockSpec((rows, part), lambda g, m: (0, g))] * 2,
        pl.BlockSpec((1, part, DH), slot),
        jax.ShapeDtypeStruct((steps, part, DH), BF16),
        2 * rows * width * DH,
        2 * 2 * rows * width,
    )(meta, key, value)


def within_block(meta, query, key, value, doc_count):
    rows, width = query.shape
    part = DH
    for heads in (4, 3, 2):
        if width % (heads * DH) == 0:
            part = heads * DH
            break
    tile = rows // 2

    def kernel(meta_ref, q_ref, k_ref, v_ref, o_ref, mask_ref):
        @pl.when(pl.program_id(0) == 0)
        def _():
            offset = meta_ref[0] * rows
            t = lax.broadcasted_iota(jnp.int32, (rows, rows), 0)
            s = lax.broadcasted_iota(jnp.int32, (rows, rows), 1)
            pos = lax.broadcasted_iota(jnp.int32, (rows, 1), 0)
            first = jnp.zeros((rows, 1), jnp.int32)
            bound = -offset
            for d in range(doc_count):
                bound = bound + meta_ref[LENS + d]
                first = jnp.where(bound <= pos, bound, first)
            mask_ref[...] = jnp.where((s <= t) & (s >= first), 1.0, 0.0).astype(BF16)

        for h in range(part // DH):
            cols = slice(h * DH, (h + 1) * DH)
            for i in range(2):
                r = slice(i * tile, (i + 1) * tile)
                seen = (i + 1) * tile
                scores = lax.dot_general(
                    q_ref[r, cols], k_ref[:seen, cols], (((1,), (1,)), ((), ())), preferred_element_type=F32
                )
                scores = scores.astype(BF16) * mask_ref[r, :seen]
                o_ref[r, cols] = jnp.dot(scores, v_ref[:seen, cols], preferred_element_type=F32)

    spec = pl.BlockSpec((rows, part), lambda g, m: (0, g))
    return call(
        kernel,
        (width // part,),
        [spec] * 3,
        spec,
        jax.ShapeDtypeStruct((rows, width), F32),
        3 * rows * rows * width,
        10 * rows * width,
        [pltpu.VMEM((rows, rows), BF16)],
    )(meta, query, key, value)


def whole(shape):
    return pl.BlockSpec(shape, lambda *_: (0,) * len(shape))


def after(meta, *arrays):
    return lax.optimization_barrier((meta, *arrays))[0]


def factor(condition):
    return jnp.where(condition, 1.0, 0.0)


def split_states(meta, key, value, doc_count, slots):
    rows, width = key.shape
    part = width // 4
    count = len(slots)

    def kernel(meta_ref, k_hbm, v_hbm, o_ref, k_ref, v_ref, sems):
        copies = []
        for i, s in enumerate(slots):
            cols = pl.ds(pl.multiple_of((meta_ref[1] ^ s) * part, DH), part)
            for n, (source, target) in enumerate(((k_hbm, k_ref), (v_hbm, v_ref))):
                copies.append(pltpu.make_async_copy(source.at[:, cols], target.at[i], sems.at[i, n]))
                copies[-1].start()
        offset = meta_ref[0] * rows
        first = doc_start(meta_ref, doc_count, offset + rows - 1) - offset
        live = lax.broadcasted_iota(jnp.int32, (rows, DH), 0) >= first
        for i in range(count):
            copies[2 * i].wait()
            copies[2 * i + 1].wait()
            for h in range(part // DH):
                cols = slice(h * DH, (h + 1) * DH)
                k = jnp.where(live, k_ref[i, :, cols], jnp.zeros((), BF16))
                state = lax.dot_general(
                    k, v_ref[i, :, cols], (((0,), (0,)), ((), ())), preferred_element_type=F32
                )
                o_ref[i, cols, :] = state.astype(BF16)

    return call(
        kernel,
        (1,),
        [pl.BlockSpec(memory_space=pltpu.HBM)] * 2,
        whole((count, part, DH)),
        jax.ShapeDtypeStruct((count, part, DH), BF16),
        2 * rows * part * count * DH,
        2 * 2 * rows * part * count,
        [
            pltpu.VMEM((count, rows, part), BF16),
            pltpu.VMEM((count, rows, part), BF16),
            pltpu.SemaphoreType.DMA((count, 2)),
        ],
    )(meta, key, value)


def seen_mask(meta_ref, rows, doc_count):
    offset = meta_ref[0] * rows
    t = lax.broadcasted_iota(jnp.int32, (rows, rows), 0)
    s = lax.broadcasted_iota(jnp.int32, (rows, rows), 1)
    pos = lax.broadcasted_iota(jnp.int32, (rows, 1), 0)
    first = jnp.zeros((rows, 1), jnp.int32)
    bound = -offset
    for d in range(doc_count):
        bound = bound + meta_ref[LENS + d]
        first = jnp.where(bound <= pos, bound, first)
    return jnp.where((s <= t) & (s >= first), 1.0, 0.0).astype(BF16)


def within_slots(meta, query, key, value, doc_count, slots, mask=None):
    rows, width = query.shape
    part = width // 4
    tile = rows // 2
    make = mask is None

    def kernel(meta_ref, q_ref, k_ref, v_ref, *rest):
        if make:
            o_ref, mask_ref = rest

            @pl.when(pl.program_id(0) == 0)
            def _():
                mask_ref[...] = seen_mask(meta_ref, rows, doc_count)
        else:
            mask_ref, o_ref = rest
        for h in range(part // DH):
            cols = slice(h * DH, (h + 1) * DH)
            for i in range(2):
                r = slice(i * tile, (i + 1) * tile)
                seen = (i + 1) * tile
                scores = lax.dot_general(
                    q_ref[r, cols], k_ref[:seen, cols], (((1,), (1,)), ((), ())), preferred_element_type=F32
                )
                scores = scores.astype(BF16) * mask_ref[r, :seen]
                o_ref[r, cols] = jnp.dot(scores, v_ref[:seen, cols], preferred_element_type=F32)

    count = len(slots)
    spec = pl.BlockSpec((rows, part), lambda g, m: (0, (g + slots[0]) ^ m[1]))
    out = pl.BlockSpec((rows, part), lambda g, m: (0, g))
    shape = jax.ShapeDtypeStruct((rows, part * count), F32)
    square = whole((rows, rows))
    return call(
        kernel,
        (count,),
        [spec] * 3 + [square] * (not make),
        [out, square] if make else out,
        [shape, jax.ShapeDtypeStruct((rows, rows), BF16)] if make else shape,
        3 * rows * rows * part * count,
        10 * rows * part * count,
    )(meta, query, key, value, *([] if make else [mask]))


def small(kernel, meta, arrays, shape, count):
    return call(
        kernel,
        (1,),
        [whole(a.shape) for a in arrays],
        [whole(shape)] * count,
        [jax.ShapeDtypeStruct(shape, BF16)] * count,
        shape[0] * shape[1],
        2 * shape[0] * shape[1] * (len(arrays) + count),
    )(meta, *arrays)


def join_core(meta, keep, got, rows, doc_count):
    def kernel(meta_ref, keep_ref, got_ref, a_ref, b_ref):
        low = meta_ref[0] & -2
        joined = factor(doc_start(meta_ref, doc_count, (low + 2) * rows - 1) < (low + 1) * rows)
        upper = (meta_ref[1] & 1) != 0
        own, other = jnp.where(upper, 1.0, joined), jnp.where(upper, joined, 1.0)
        for i, o_ref in enumerate((a_ref, b_ref)):
            o_ref[...] = (own * keep_ref[i].astype(F32) + other * got_ref[i].astype(F32)).astype(BF16)

    return small(kernel, meta, (keep, got), keep.shape[1:], 2)


def join_chips(meta, mine, got, rows, doc_count):
    def kernel(meta_ref, a_ref, b_ref, o_ref):
        low = meta_ref[0] & -4
        joined = factor(doc_start(meta_ref, doc_count, (low + 4) * rows - 1) < (low + 2) * rows)
        upper = (meta_ref[1] & 2) != 0
        own, other = jnp.where(upper, 1.0, joined), jnp.where(upper, joined, 1.0)
        o_ref[...] = (own * a_ref[...].astype(F32) + other * b_ref[...].astype(F32)).astype(BF16)

    return small(kernel, meta, (mine, got), mine.shape, 1)[0]


def join_planes(meta, plane_sum, previous, rows, doc_count):
    def kernel(meta_ref, a_ref, b_ref, o_ref):
        low = meta_ref[0] & -4
        joined = factor(doc_start(meta_ref, doc_count, (low + 4) * rows - 1) < low * rows)
        o_ref[...] = (a_ref[...].astype(F32) + joined * b_ref[...].astype(F32)).astype(BF16)

    return small(kernel, meta, (plane_sum, previous), plane_sum.shape, 1)[0]


def carry_in_chip(meta_ref, chip, keep, got, rows, doc_count):
    low = meta_ref[0] & -2
    begins = doc_start(meta_ref, doc_count, (low + 1) * rows)
    through, joined = factor(begins < low * rows), factor(begins < (low + 1) * rows)
    upper = (meta_ref[1] & 1) != 0
    later = through * chip + joined * jnp.where(upper, got, keep).astype(F32)
    return jnp.where(upper, later, chip), jnp.where(upper, chip, later)


def carry_first(meta, near, far, mine, got, keep, core_got, rows, doc_count):
    def kernel(meta_ref, near_ref, far_ref, a_ref, b_ref, keep_ref, got_ref, o_ref, core_ref, chip_ref):
        low = meta_ref[0] & -4
        begins = doc_start(meta_ref, doc_count, low * rows)
        first = factor(begins < low * rows) * near_ref[...].astype(F32)
        first = first + factor(begins < (low - 4) * rows) * far_ref[...].astype(F32)
        begins = doc_start(meta_ref, doc_count, (low + 2) * rows)
        through, joined = factor(begins < low * rows), factor(begins < (low + 2) * rows)
        upper = (meta_ref[1] & 2) != 0
        later = through * first + joined * jnp.where(upper, b_ref[...], a_ref[...]).astype(F32)
        chip_ref[...] = jnp.where(upper, first, later).astype(BF16)
        chip = jnp.where(upper, later, first)
        ours, theirs = carry_in_chip(meta_ref, chip, keep_ref[0], got_ref[0], rows, doc_count)
        o_ref[...] = ours.astype(BF16)
        core_ref[...] = theirs.astype(BF16)

    return small(kernel, meta, (near, far, mine, got, keep, core_got), mine.shape, 3)


def carry_second(meta, chip, keep, core_got, rows, doc_count):
    def kernel(meta_ref, chip_ref, keep_ref, got_ref, o_ref, core_ref):
        ours, theirs = carry_in_chip(
            meta_ref, chip_ref[...].astype(F32), keep_ref[1], got_ref[1], rows, doc_count
        )
        o_ref[...] = ours.astype(BF16)
        core_ref[...] = theirs.astype(BF16)

    return small(kernel, meta, (chip, keep, core_got), chip.shape, 2)


def norm_heads(meta, query, within, carry, gain, doc_count, slots=(None, None, None)):
    rows = query.shape[0]
    part = carry.shape[0]

    def kernel(meta_ref, q_ref, w_ref, c_ref, g_ref, o_ref):
        offset = meta_ref[0] * rows
        begins = doc_start(meta_ref, doc_count, offset)
        bound = jnp.int32(0)
        end = jnp.int32(0)
        for d in range(doc_count):
            previous = bound
            bound = bound + meta_ref[LENS + d]
            end = jnp.where(previous <= offset, bound, end)
        stop = jnp.where(begins < offset, end - offset, 0)
        cross = lax.broadcasted_iota(jnp.int32, (rows, DH), 0) < stop
        for h in range(part // DH):
            cols = slice(h * DH, (h + 1) * DH)
            term = jnp.dot(q_ref[:, cols], c_ref[cols, :], preferred_element_type=F32)
            mixture = w_ref[:, cols].astype(F32) + jnp.where(cross, term, 0.0)
            mean = jnp.mean(mixture * mixture, axis=-1, keepdims=True)
            o_ref[:, cols] = (mixture * lax.rsqrt(mean + 1e-06) * g_ref[:, cols]).astype(BF16)

    def block(place):
        if place is None:
            return lambda i, m: (0, 0)
        if isinstance(place, int):
            return lambda i, m: (0, place)
        return lambda i, m: (0, m[1] ^ place[1])

    return call(
        kernel,
        (1,),
        [
            pl.BlockSpec((rows, part), block(slots[0])),
            pl.BlockSpec((rows, part), block(slots[1])),
            whole((part, DH)),
            pl.BlockSpec((1, part), block(slots[2])),
        ],
        whole((rows, part)),
        jax.ShapeDtypeStruct((rows, part), BF16),
        2 * rows * part * DH,
        8 * rows * part,
    )(meta, query, within, carry, gain.reshape(1, -1))


TILES = 4


def project_own(meta, pieces, weight, columns):
    rows, part = pieces[0].shape
    tile = columns // TILES
    count = len(pieces)

    def kernel(meta_ref, *refs):
        ns, ws, o_ref = refs[:count], refs[count : 2 * count], refs[-1]
        n = jnp.concatenate([r[...] for r in ns], axis=1)
        w = jnp.concatenate([r[...] for r in ws], axis=0)
        o_ref[...] = jnp.dot(n, w, preferred_element_type=F32)

    return call(
        kernel,
        (TILES,),
        [whole((rows, part))] * count
        + [pl.BlockSpec((part, tile), lambda n, m, s=s: (m[1] ^ s, m[2] * TILES + n)) for s in range(count)],
        pl.BlockSpec((rows, tile), lambda n, m: (0, n)),
        jax.ShapeDtypeStruct((rows, columns), F32),
        2 * rows * part * count * columns,
        2 * part * count * columns + 4 * rows * columns,
    )(meta, *pieces, *[weight] * count)


def project_more(meta, total, pieces, weights, dtype):
    rows, columns = total.shape
    part = pieces[0].shape[1]
    tile = columns // TILES
    count = len(pieces)
    flat = []
    for ws in weights:
        start = 0
        for w in ws:
            tiles = w.shape[1] // tile
            flat.append((w, start, tiles))
            start += tiles

    def kernel(meta_ref, t_ref, *refs):
        ns, ws, o_ref = refs[:count], refs[count:-1], refs[-1]
        n = jnp.concatenate([r[...] for r in ns], axis=1)
        for c in range(TILES):

            @pl.when(pl.program_id(0) == c)
            def _():
                held = [r[...] for r, (_, start, tiles) in zip(ws, flat) if start <= c < start + tiles]
                w = jnp.concatenate(held, axis=0)
                o_ref[...] = (t_ref[...] + jnp.dot(n, w, preferred_element_type=F32)).astype(dtype)

    def column(start, tiles):
        return lambda n, m: (0, jnp.clip(n - start, 0, tiles - 1))

    out_spec = pl.BlockSpec((rows, tile), lambda n, m: (0, n ^ (m[3] * (TILES // 2))))
    return call(
        kernel,
        (TILES,),
        [out_spec]
        + [whole((rows, part))] * count
        + [pl.BlockSpec((part, tile), column(start, tiles)) for _, start, tiles in flat],
        out_spec,
        jax.ShapeDtypeStruct((rows, columns), dtype),
        2 * rows * part * count * columns,
        2 * part * count * columns + 6 * rows * columns,
    )(meta, total, *pieces, *[w for w, _, _ in flat])


def pair_body(n_seq, query, key, value, doc_lengths, gain, weight):
    rows, width = query.shape
    docs = doc_lengths.shape[0]
    plane, part = 4, width // 4
    columns = weight.shape[1] // 2
    half = columns // 2
    block = lax.axis_index("seq").astype(jnp.int32)
    group = lax.axis_index("head").astype(jnp.int32)
    member = block % plane
    side = (block // plane) % 2
    meta = jnp.concatenate([
        jnp.stack([block, member, group, side]), jnp.zeros((LENS - 4,), jnp.int32), doc_lengths
    ])

    def swap(x, bit):
        return lax.ppermute(x, "seq", [(i, i ^ bit) for i in range(n_seq)])

    def shift(x, count):
        return lax.ppermute(x, "seq", [(i, i + count) for i in range(n_seq - count)])

    def flip(x):
        return lax.ppermute(x, "head", [(0, 1), (1, 0)])

    def behind(x, *arrays):
        return lax.optimization_barrier((x, *arrays))[0]

    send = split_states(meta, key, value, docs, (1, 3))
    core_got = swap(send, 1)
    keep = split_states(after(meta, send), key, value, docs, (0, 2))
    chip0, chip2 = join_core(meta, keep, core_got, rows, docs)
    chip_got = swap(chip2, 2)

    sent_weight = lax.dynamic_slice(
        weight, (member * part, (1 - group) * columns + side * half), (part, half)
    )
    w0 = [flip(behind(sent_weight, chip2))]
    within0, mask = within_slots(after(meta, chip0), query, key, value, docs, (0,))
    plane_sum = join_chips(after(meta, within0), chip0, chip_got, rows, docs)
    near = shift(plane_sum, plane)
    within1 = within_slots(after(meta, plane_sum), query, key, value, docs, (1,), mask)
    both = join_planes(after(meta, within1, w0[0]), plane_sum, near, rows, docs)
    w2 = [swap(w0[0], 2)]
    far = shift(both, 2 * plane)
    carry0, core_carry0, chip_carry = carry_first(
        meta, near, far, chip0, chip_got, keep, core_got, rows, docs
    )
    carry1 = swap(core_carry0, 1)
    chip_carry2 = swap(chip_carry, 2)

    def norm(slot, within, carry):
        return norm_heads(
            meta, query, within, carry, gain, docs, (("slot", slot), None, ("slot", slot))
        )

    normed0 = norm(0, within0, carry0)
    far0 = flip(normed0)
    normed1 = norm(1, within1, carry1)
    far1 = flip(normed1)
    within2 = within_slots(after(meta, normed1), query, key, value, docs, (2,), mask)
    within3 = within_slots(after(meta, within2), query, key, value, docs, (3,), mask)
    carry2, core_carry2 = carry_second(meta, chip_carry2, keep, core_got, rows, docs)
    carry3 = swap(core_carry2, 1)
    normed2 = norm(2, within2, carry2)
    far2 = flip(normed2)
    normed3 = norm(3, within3, carry3)
    far3 = flip(normed3)

    w0.append(swap(behind(w0[0], far), plane))
    quarter = half // 2
    w2.append(swap(w0[1][:, :quarter], 2))
    w2.append(swap(w2[0][:, quarter:], plane))
    w1 = [swap(w, 1) for w in w0]
    w3 = [swap(w, 1) for w in w2]

    total = project_own(meta, [normed0, normed1, normed2, normed3], weight, columns)
    total = project_more(meta, total, [far0, far1], [w0, w1], F32)
    total = project_more(meta, total, [far2], [w2], F32)
    return project_more(meta, total, [far3], [w3], BF16)


def body(n_seq, n_head, query, key, value, doc_lengths, gain, weight):
    rows, width = query.shape
    doc_count = doc_lengths.shape[0]
    plane = n_seq // PLANES
    if n_head == 2 and plane == 4 and width % (4 * DH) == 0:
        return pair_body(n_seq, query, key, value, doc_lengths, gain, weight)
    block = lax.axis_index("seq").astype(jnp.int32)
    group = lax.axis_index("head").astype(jnp.int32)
    member = block % plane
    meta = jnp.concatenate([
        jnp.stack([block, member, group]), jnp.zeros((LENS - 3,), jnp.int32), doc_lengths
    ])

    bounds = jnp.cumsum(doc_lengths)

    def first_block(token):
        starts = jnp.max(jnp.where(bounds <= token, bounds, 0))
        return starts // rows

    def weigh(condition):
        return condition.astype(F32)

    def swap(x, bit):
        return lax.ppermute(x, "seq", [(i, i ^ bit) for i in range(n_seq)])

    by_slot = (width // DH) % plane == 0
    steps = plane if by_slot else 1
    states = block_states(meta, key, value, doc_count, steps)
    if not by_slot:
        states = states.reshape(plane, width // plane, DH)[jnp.arange(plane, dtype=jnp.int32) ^ member]
    slots = [states[s] for s in range(plane)]

    kept = []
    bit = 1
    while bit < plane:
        mine, send = slots[0::2], slots[1::2]
        got = swap(jnp.stack(send), bit)
        got = [got[i] for i in range(len(send))]
        upper = (member & bit) != 0
        unit = block & ~(2 * bit - 1)
        joined = weigh(first_block((unit + 2 * bit) * rows - 1) < unit + bit)
        own_factor = jnp.where(upper, 1.0, joined)
        got_factor = jnp.where(upper, joined, 1.0)
        kept.append((mine, got, bit, upper, unit))
        slots = [
            (own_factor * a.astype(F32) + got_factor * b.astype(F32)).astype(BF16) for a, b in zip(mine, got)
        ]
        bit *= 2
    base = block - member
    begins = first_block(base * rows)
    carry = jnp.zeros(slots[0].shape, F32)
    for d in range(PLANES - 1, 0, -1):
        shift = d * plane
        got = lax.ppermute(slots[0], "seq", [(i, i + shift) for i in range(n_seq - shift)])
        carry = carry + weigh((base - shift + plane - 1 >= begins) & (base >= shift)) * got.astype(F32)
    carries = [carry]

    for mine, got, bit, upper, unit in reversed(kept):
        middle = unit + bit
        begins = first_block(middle * rows)
        through, joined = weigh(begins < unit), weigh(begins < middle)
        ours, theirs = [], []
        for carry, a, b in zip(carries, mine, got):
            lower_state = jnp.where(upper, b, a).astype(F32)
            after = through * carry + joined * lower_state
            ours.append(jnp.where(upper, after, carry))
            theirs.append(jnp.where(upper, carry, after).astype(BF16))
        back = swap(jnp.stack(theirs), bit)
        carries = [x for i, c in enumerate(ours) for x in (c, back[i])]
    carries = [c.astype(BF16) for c in carries]

    within = within_block(meta, query, key, value, doc_count)
    natural = jnp.stack(carries)[jnp.arange(plane, dtype=jnp.int32) ^ member].reshape(width, DH)
    normed = norm_heads(meta, query, within, natural, gain, doc_count)
    partial_sum = jnp.dot(normed, weight, preferred_element_type=F32)
    return lax.psum_scatter(partial_sum.astype(BF16), "head", scatter_dimension=1, tiled=True)


def solution(mesh):
    return jax.shard_map(
        functools.partial(body, mesh.shape["seq"], mesh.shape["head"]),
        mesh=mesh,
        in_specs=(
            P("seq", "head"),
            P("seq", "head"),
            P("seq", "head"),
            P(),
            P("head"),
            P("head", None),
        ),
        out_specs=P("seq", "head"),
        check_vma=False,
    )
```

```python
import functools

import jax
import jax.numpy as jnp
from jax import lax
from jax.experimental import pallas as pl
from jax.experimental.pallas import tpu as pltpu
from jax.sharding import PartitionSpec as P

DH = 128
PLANES = 4
F32, BF16 = jnp.float32, jnp.bfloat16
LENS = 8
VMEM_LIMIT = 16 * 1024 * 1024
VMEM_MOST = 60 * 1024 * 1024


def doc_start(meta, doc_count, token):
    bound = jnp.int32(0)
    start = jnp.int32(0)
    for d in range(doc_count):
        bound = bound + meta[LENS + d]
        start = jnp.where(bound <= token, bound, start)
    return start


def call(kernel, grid, in_specs, out_specs, out_shape, flops, bytes_accessed, scratch=(), vmem=VMEM_LIMIT):
    return pl.pallas_call(
        kernel,
        grid_spec=pltpu.PrefetchScalarGridSpec(
            num_scalar_prefetch=1,
            grid=grid,
            in_specs=in_specs,
            out_specs=out_specs,
            scratch_shapes=scratch,
        ),
        out_shape=out_shape,
        compiler_params=pltpu.CompilerParams(vmem_limit_bytes=vmem),
        cost_estimate=pl.CostEstimate(flops=flops, bytes_accessed=bytes_accessed, transcendentals=0),
    )


def block_states(meta, key, value, doc_count, steps):
    rows, width = key.shape
    part = width // steps

    def kernel(meta_ref, k_ref, v_ref, o_ref):
        offset = meta_ref[0] * rows
        first = doc_start(meta_ref, doc_count, offset + rows - 1) - offset
        live = lax.broadcasted_iota(jnp.int32, (rows, DH), 0) >= first
        for h in range(part // DH):
            cols = slice(h * DH, (h + 1) * DH)
            k = jnp.where(live, k_ref[:, cols], jnp.zeros((), BF16))
            s = lax.dot_general(k, v_ref[:, cols], (((0,), (0,)), ((), ())), preferred_element_type=F32)
            o_ref[0, cols, :] = s.astype(BF16)

    def slot(g, m):
        return (g ^ m[1], 0, 0) if steps > 1 else (0, 0, 0)

    return call(
        kernel,
        (steps,),
        [pl.BlockSpec((rows, part), lambda g, m: (0, g))] * 2,
        pl.BlockSpec((1, part, DH), slot),
        jax.ShapeDtypeStruct((steps, part, DH), BF16),
        2 * rows * width * DH,
        2 * 2 * rows * width,
    )(meta, key, value)


def within_block(meta, query, key, value, doc_count):
    rows, width = query.shape
    part = DH
    for heads in (4, 3, 2):
        if width % (heads * DH) == 0:
            part = heads * DH
            break
    tile = rows // 2

    def kernel(meta_ref, q_ref, k_ref, v_ref, o_ref, mask_ref):
        @pl.when(pl.program_id(0) == 0)
        def _():
            offset = meta_ref[0] * rows
            t = lax.broadcasted_iota(jnp.int32, (rows, rows), 0)
            s = lax.broadcasted_iota(jnp.int32, (rows, rows), 1)
            pos = lax.broadcasted_iota(jnp.int32, (rows, 1), 0)
            first = jnp.zeros((rows, 1), jnp.int32)
            bound = -offset
            for d in range(doc_count):
                bound = bound + meta_ref[LENS + d]
                first = jnp.where(bound <= pos, bound, first)
            mask_ref[...] = jnp.where((s <= t) & (s >= first), 1.0, 0.0).astype(BF16)

        for h in range(part // DH):
            cols = slice(h * DH, (h + 1) * DH)
            for i in range(2):
                r = slice(i * tile, (i + 1) * tile)
                seen = (i + 1) * tile
                scores = lax.dot_general(
                    q_ref[r, cols], k_ref[:seen, cols], (((1,), (1,)), ((), ())), preferred_element_type=F32
                )
                scores = scores.astype(BF16) * mask_ref[r, :seen]
                o_ref[r, cols] = jnp.dot(scores, v_ref[:seen, cols], preferred_element_type=F32)

    spec = pl.BlockSpec((rows, part), lambda g, m: (0, g))
    return call(
        kernel,
        (width // part,),
        [spec] * 3,
        spec,
        jax.ShapeDtypeStruct((rows, width), F32),
        3 * rows * rows * width,
        10 * rows * width,
        [pltpu.VMEM((rows, rows), BF16)],
    )(meta, query, key, value)


def whole(shape):
    return pl.BlockSpec(shape, lambda *_: (0,) * len(shape))


def after(meta, *arrays):
    return lax.optimization_barrier((meta, *arrays))[0]


def factor(condition):
    return jnp.where(condition, 1.0, 0.0)


def split_states(meta, key, value, doc_count, slots):
    rows, width = key.shape
    part = width // 4
    count = len(slots)

    def kernel(meta_ref, k_hbm, v_hbm, o_ref, k_ref, v_ref, sems):
        copies = []
        for i, s in enumerate(slots):
            cols = pl.ds(pl.multiple_of((meta_ref[1] ^ s) * part, DH), part)
            for n, (source, target) in enumerate(((k_hbm, k_ref), (v_hbm, v_ref))):
                copies.append(pltpu.make_async_copy(source.at[:, cols], target.at[i], sems.at[i, n]))
                copies[-1].start()
        offset = meta_ref[0] * rows
        first = doc_start(meta_ref, doc_count, offset + rows - 1) - offset
        live = lax.broadcasted_iota(jnp.int32, (rows, DH), 0) >= first
        for i in range(count):
            copies[2 * i].wait()
            copies[2 * i + 1].wait()
            for h in range(part // DH):
                cols = slice(h * DH, (h + 1) * DH)
                k = jnp.where(live, k_ref[i, :, cols], jnp.zeros((), BF16))
                state = lax.dot_general(
                    k, v_ref[i, :, cols], (((0,), (0,)), ((), ())), preferred_element_type=F32
                )
                o_ref[i, cols, :] = state.astype(BF16)

    return call(
        kernel,
        (1,),
        [pl.BlockSpec(memory_space=pltpu.HBM)] * 2,
        whole((count, part, DH)),
        jax.ShapeDtypeStruct((count, part, DH), BF16),
        2 * rows * part * count * DH,
        2 * 2 * rows * part * count,
        [
            pltpu.VMEM((count, rows, part), BF16),
            pltpu.VMEM((count, rows, part), BF16),
            pltpu.SemaphoreType.DMA((count, 2)),
        ],
        VMEM_MOST,
    )(meta, key, value)


def seen_mask(meta_ref, rows, doc_count):
    offset = meta_ref[0] * rows
    t = lax.broadcasted_iota(jnp.int32, (rows, rows), 0)
    s = lax.broadcasted_iota(jnp.int32, (rows, rows), 1)
    pos = lax.broadcasted_iota(jnp.int32, (rows, 1), 0)
    first = jnp.zeros((rows, 1), jnp.int32)
    bound = -offset
    for d in range(doc_count):
        bound = bound + meta_ref[LENS + d]
        first = jnp.where(bound <= pos, bound, first)
    return jnp.where((s <= t) & (s >= first), 1.0, 0.0).astype(BF16)


def within_slots(meta, query, key, value, doc_count, slots, mask=None):
    rows, width = query.shape
    part = width // 4
    tile = rows // 2
    make = mask is None

    def kernel(meta_ref, q_ref, k_ref, v_ref, *rest):
        if make:
            o_ref, mask_ref = rest

            @pl.when(pl.program_id(0) == 0)
            def _():
                mask_ref[...] = seen_mask(meta_ref, rows, doc_count)
        else:
            mask_ref, o_ref = rest
        for h in range(part // DH):
            cols = slice(h * DH, (h + 1) * DH)
            for i in range(2):
                r = slice(i * tile, (i + 1) * tile)
                seen = (i + 1) * tile
                scores = lax.dot_general(
                    q_ref[r, cols], k_ref[:seen, cols], (((1,), (1,)), ((), ())), preferred_element_type=F32
                )
                scores = scores.astype(BF16) * mask_ref[r, :seen]
                o_ref[r, cols] = jnp.dot(scores, v_ref[:seen, cols], preferred_element_type=F32)

    count = len(slots)
    spec = pl.BlockSpec((rows, part), lambda g, m: (0, (g + slots[0]) ^ m[1]))
    out = pl.BlockSpec((rows, part), lambda g, m: (0, g))
    shape = jax.ShapeDtypeStruct((rows, part * count), F32)
    square = whole((rows, rows))
    return call(
        kernel,
        (count,),
        [spec] * 3 + [square] * (not make),
        [out, square] if make else out,
        [shape, jax.ShapeDtypeStruct((rows, rows), BF16)] if make else shape,
        3 * rows * rows * part * count,
        10 * rows * part * count,
    )(meta, query, key, value, *([] if make else [mask]))


def small(kernel, meta, arrays, shape, count):
    return call(
        kernel,
        (1,),
        [whole(a.shape) for a in arrays],
        [whole(shape)] * count,
        [jax.ShapeDtypeStruct(shape, BF16)] * count,
        shape[0] * shape[1],
        2 * shape[0] * shape[1] * (len(arrays) + count),
    )(meta, *arrays)


def join_core(meta, keep, got, rows, doc_count):
    def kernel(meta_ref, keep_ref, got_ref, a_ref, b_ref):
        low = meta_ref[0] & -2
        joined = factor(doc_start(meta_ref, doc_count, (low + 2) * rows - 1) < (low + 1) * rows)
        upper = (meta_ref[1] & 1) != 0
        own, other = jnp.where(upper, 1.0, joined), jnp.where(upper, joined, 1.0)
        for i, o_ref in enumerate((a_ref, b_ref)):
            o_ref[...] = (own * keep_ref[i].astype(F32) + other * got_ref[i].astype(F32)).astype(BF16)

    return small(kernel, meta, (keep, got), keep.shape[1:], 2)


def join_chips(meta, mine, got, rows, doc_count):
    def kernel(meta_ref, a_ref, b_ref, o_ref):
        low = meta_ref[0] & -4
        joined = factor(doc_start(meta_ref, doc_count, (low + 4) * rows - 1) < (low + 2) * rows)
        upper = (meta_ref[1] & 2) != 0
        own, other = jnp.where(upper, 1.0, joined), jnp.where(upper, joined, 1.0)
        o_ref[...] = (own * a_ref[...].astype(F32) + other * b_ref[...].astype(F32)).astype(BF16)

    return small(kernel, meta, (mine, got), mine.shape, 1)[0]


def join_planes(meta, plane_sum, previous, rows, doc_count):
    def kernel(meta_ref, a_ref, b_ref, o_ref):
        low = meta_ref[0] & -4
        joined = factor(doc_start(meta_ref, doc_count, (low + 4) * rows - 1) < low * rows)
        o_ref[...] = (a_ref[...].astype(F32) + joined * b_ref[...].astype(F32)).astype(BF16)

    return small(kernel, meta, (plane_sum, previous), plane_sum.shape, 1)[0]


def carry_in_chip(meta_ref, chip, keep, got, rows, doc_count):
    low = meta_ref[0] & -2
    begins = doc_start(meta_ref, doc_count, (low + 1) * rows)
    through, joined = factor(begins < low * rows), factor(begins < (low + 1) * rows)
    upper = (meta_ref[1] & 1) != 0
    later = through * chip + joined * jnp.where(upper, got, keep).astype(F32)
    return jnp.where(upper, later, chip), jnp.where(upper, chip, later)


def carry_first(meta, near, far, mine, got, keep, core_got, rows, doc_count):
    def kernel(meta_ref, near_ref, far_ref, a_ref, b_ref, keep_ref, got_ref, o_ref, core_ref, chip_ref):
        low = meta_ref[0] & -4
        begins = doc_start(meta_ref, doc_count, low * rows)
        first = factor(begins < low * rows) * near_ref[...].astype(F32)
        first = first + factor(begins < (low - 4) * rows) * far_ref[...].astype(F32)
        begins = doc_start(meta_ref, doc_count, (low + 2) * rows)
        through, joined = factor(begins < low * rows), factor(begins < (low + 2) * rows)
        upper = (meta_ref[1] & 2) != 0
        later = through * first + joined * jnp.where(upper, b_ref[...], a_ref[...]).astype(F32)
        chip_ref[...] = jnp.where(upper, first, later).astype(BF16)
        chip = jnp.where(upper, later, first)
        ours, theirs = carry_in_chip(meta_ref, chip, keep_ref[0], got_ref[0], rows, doc_count)
        o_ref[...] = ours.astype(BF16)
        core_ref[...] = theirs.astype(BF16)

    return small(kernel, meta, (near, far, mine, got, keep, core_got), mine.shape, 3)


def carry_second(meta, chip, keep, core_got, rows, doc_count):
    def kernel(meta_ref, chip_ref, keep_ref, got_ref, o_ref, core_ref):
        ours, theirs = carry_in_chip(
            meta_ref, chip_ref[...].astype(F32), keep_ref[1], got_ref[1], rows, doc_count
        )
        o_ref[...] = ours.astype(BF16)
        core_ref[...] = theirs.astype(BF16)

    return small(kernel, meta, (chip, keep, core_got), chip.shape, 2)


def norm_heads(meta, query, within, carry, gain, doc_count, slots=(None, None, None)):
    rows = query.shape[0]
    part = carry.shape[0]

    def kernel(meta_ref, q_ref, w_ref, c_ref, g_ref, o_ref):
        offset = meta_ref[0] * rows
        begins = doc_start(meta_ref, doc_count, offset)
        bound = jnp.int32(0)
        end = jnp.int32(0)
        for d in range(doc_count):
            previous = bound
            bound = bound + meta_ref[LENS + d]
            end = jnp.where(previous <= offset, bound, end)
        stop = jnp.where(begins < offset, end - offset, 0)
        cross = lax.broadcasted_iota(jnp.int32, (rows, DH), 0) < stop
        for h in range(part // DH):
            cols = slice(h * DH, (h + 1) * DH)
            term = jnp.dot(q_ref[:, cols], c_ref[cols, :], preferred_element_type=F32)
            mixture = w_ref[:, cols].astype(F32) + jnp.where(cross, term, 0.0)
            mean = jnp.mean(mixture * mixture, axis=-1, keepdims=True)
            o_ref[:, cols] = (mixture * lax.rsqrt(mean + 1e-06) * g_ref[:, cols]).astype(BF16)

    def block(place):
        if place is None:
            return lambda i, m: (0, 0)
        if isinstance(place, int):
            return lambda i, m: (0, place)
        return lambda i, m: (0, m[1] ^ place[1])

    return call(
        kernel,
        (1,),
        [
            pl.BlockSpec((rows, part), block(slots[0])),
            pl.BlockSpec((rows, part), block(slots[1])),
            whole((part, DH)),
            pl.BlockSpec((1, part), block(slots[2])),
        ],
        whole((rows, part)),
        jax.ShapeDtypeStruct((rows, part), BF16),
        2 * rows * part * DH,
        8 * rows * part,
    )(meta, query, within, carry, gain.reshape(1, -1))


TILES = 4


def project_own(meta, pieces, weight, columns):
    rows, part = pieces[0].shape
    tile = columns // TILES
    count = len(pieces)

    def kernel(meta_ref, *refs):
        ns, ws, o_ref = refs[:count], refs[count : 2 * count], refs[-1]
        n = jnp.concatenate([r[...] for r in ns], axis=1)
        w = jnp.concatenate([r[...] for r in ws], axis=0)
        o_ref[...] = jnp.dot(n, w, preferred_element_type=F32)

    return call(
        kernel,
        (TILES,),
        [whole((rows, part))] * count
        + [pl.BlockSpec((part, tile), lambda n, m, s=s: (m[1] ^ s, m[2] * TILES + n)) for s in range(count)],
        pl.BlockSpec((rows, tile), lambda n, m: (0, n)),
        jax.ShapeDtypeStruct((rows, columns), F32),
        2 * rows * part * count * columns,
        2 * part * count * columns + 4 * rows * columns,
    )(meta, *pieces, *[weight] * count)


def project_more(meta, total, pieces, weights, dtype):
    rows, columns = total.shape
    part = pieces[0].shape[1]
    tile = columns // TILES
    count = len(pieces)
    flat = []
    for ws in weights:
        start = 0
        for w in ws:
            tiles = w.shape[1] // tile
            flat.append((w, start, tiles))
            start += tiles

    def kernel(meta_ref, t_ref, *refs):
        ns, ws, o_ref = refs[:count], refs[count:-1], refs[-1]
        n = jnp.concatenate([r[...] for r in ns], axis=1)
        for c in range(TILES):

            @pl.when(pl.program_id(0) == c)
            def _():
                held = [r[...] for r, (_, start, tiles) in zip(ws, flat) if start <= c < start + tiles]
                w = jnp.concatenate(held, axis=0)
                o_ref[...] = (t_ref[...] + jnp.dot(n, w, preferred_element_type=F32)).astype(dtype)

    def column(start, tiles):
        return lambda n, m: (0, jnp.clip(n - start, 0, tiles - 1))

    out_spec = pl.BlockSpec((rows, tile), lambda n, m: (0, n ^ (m[3] * (TILES // 2))))
    return call(
        kernel,
        (TILES,),
        [out_spec]
        + [whole((rows, part))] * count
        + [pl.BlockSpec((part, tile), column(start, tiles)) for _, start, tiles in flat],
        out_spec,
        jax.ShapeDtypeStruct((rows, columns), dtype),
        2 * rows * part * count * columns,
        2 * part * count * columns + 6 * rows * columns,
    )(meta, total, *pieces, *[w for w, _, _ in flat])


def pair_body(n_seq, query, key, value, doc_lengths, gain, weight):
    rows, width = query.shape
    docs = doc_lengths.shape[0]
    plane, part = 4, width // 4
    columns = weight.shape[1] // 2
    half = columns // 2
    block = lax.axis_index("seq").astype(jnp.int32)
    group = lax.axis_index("head").astype(jnp.int32)
    member = block % plane
    side = (block // plane) % 2
    meta = jnp.concatenate([
        jnp.stack([block, member, group, side]), jnp.zeros((LENS - 4,), jnp.int32), doc_lengths
    ])

    def swap(x, bit):
        return lax.ppermute(x, "seq", [(i, i ^ bit) for i in range(n_seq)])

    def shift(x, count):
        return lax.ppermute(x, "seq", [(i, i + count) for i in range(n_seq - count)])

    def flip(x):
        return lax.ppermute(x, "head", [(0, 1), (1, 0)])

    def behind(x, *arrays):
        return lax.optimization_barrier((x, *arrays))[0]

    send = split_states(meta, key, value, docs, (1, 3))
    core_got = swap(send, 1)
    keep = split_states(after(meta, send), key, value, docs, (0, 2))
    chip0, chip2 = join_core(meta, keep, core_got, rows, docs)
    chip_got = swap(chip2, 2)

    sent_weight = lax.dynamic_slice(
        weight, (member * part, (1 - group) * columns + side * half), (part, half)
    )
    within0, mask = within_slots(after(meta, chip0), query, key, value, docs, (0,))
    w0 = [flip(behind(sent_weight, within0))]
    plane_sum = join_chips(after(meta, within0), chip0, chip_got, rows, docs)
    near = shift(plane_sum, plane)
    within1 = within_slots(after(meta, plane_sum), query, key, value, docs, (1,), mask)
    both = join_planes(after(meta, within1), plane_sum, near, rows, docs)
    far = shift(both, 2 * plane)
    carry0, core_carry0, chip_carry = carry_first(
        after(meta, w0[0]), near, far, chip0, chip_got, keep, core_got, rows, docs
    )
    carry1 = swap(core_carry0, 1)
    chip_carry2 = swap(chip_carry, 2)

    def norm(slot, within, carry):
        return norm_heads(
            meta, query, within, carry, gain, docs, (("slot", slot), None, ("slot", slot))
        )

    normed0 = norm(0, within0, carry0)
    far0 = flip(normed0)
    normed1 = norm(1, within1, carry1)
    far1 = flip(normed1)
    within2 = within_slots(after(meta, normed1), query, key, value, docs, (2,), mask)
    within3 = within_slots(after(meta, within2), query, key, value, docs, (3,), mask)
    carry2, core_carry2 = carry_second(meta, chip_carry2, keep, core_got, rows, docs)
    carry3 = swap(core_carry2, 1)
    normed2 = norm(2, within2, carry2)
    far2 = flip(normed2)
    normed3 = norm(3, within3, carry3)
    far3 = flip(normed3)

    held = behind(w0[0], normed0)
    w0.append(behind(swap(held, plane), normed3))
    w2 = [behind(swap(behind(w0[0], chip_carry2), 2), normed3)]
    quarter = half // 2
    w2.append(swap(w0[1][:, :quarter], 2))
    w2.append(swap(w2[0][:, quarter:], plane))
    w1 = [swap(held, 1), swap(w0[1], 1)]
    w3 = [swap(w, 1) for w in w2]

    total = project_own(meta, [normed0, normed1, normed2, normed3], weight, columns)
    total = project_more(meta, total, [far0, far1], [w0, w1], F32)
    total = project_more(meta, total, [far2], [w2], F32)
    return project_more(meta, total, [far3], [w3], BF16)


def body(n_seq, n_head, query, key, value, doc_lengths, gain, weight):
    rows, width = query.shape
    doc_count = doc_lengths.shape[0]
    plane = n_seq // PLANES
    if n_head == 2 and plane == 4 and width % (4 * DH) == 0:
        return pair_body(n_seq, query, key, value, doc_lengths, gain, weight)
    block = lax.axis_index("seq").astype(jnp.int32)
    group = lax.axis_index("head").astype(jnp.int32)
    member = block % plane
    meta = jnp.concatenate([
        jnp.stack([block, member, group]), jnp.zeros((LENS - 3,), jnp.int32), doc_lengths
    ])

    bounds = jnp.cumsum(doc_lengths)

    def first_block(token):
        starts = jnp.max(jnp.where(bounds <= token, bounds, 0))
        return starts // rows

    def weigh(condition):
        return condition.astype(F32)

    def swap(x, bit):
        return lax.ppermute(x, "seq", [(i, i ^ bit) for i in range(n_seq)])

    by_slot = (width // DH) % plane == 0
    steps = plane if by_slot else 1
    states = block_states(meta, key, value, doc_count, steps)
    if not by_slot:
        states = states.reshape(plane, width // plane, DH)[jnp.arange(plane, dtype=jnp.int32) ^ member]
    slots = [states[s] for s in range(plane)]

    kept = []
    bit = 1
    while bit < plane:
        mine, send = slots[0::2], slots[1::2]
        got = swap(jnp.stack(send), bit)
        got = [got[i] for i in range(len(send))]
        upper = (member & bit) != 0
        unit = block & ~(2 * bit - 1)
        joined = weigh(first_block((unit + 2 * bit) * rows - 1) < unit + bit)
        own_factor = jnp.where(upper, 1.0, joined)
        got_factor = jnp.where(upper, joined, 1.0)
        kept.append((mine, got, bit, upper, unit))
        slots = [
            (own_factor * a.astype(F32) + got_factor * b.astype(F32)).astype(BF16) for a, b in zip(mine, got)
        ]
        bit *= 2
    base = block - member
    begins = first_block(base * rows)
    carry = jnp.zeros(slots[0].shape, F32)
    for d in range(PLANES - 1, 0, -1):
        shift = d * plane
        got = lax.ppermute(slots[0], "seq", [(i, i + shift) for i in range(n_seq - shift)])
        carry = carry + weigh((base - shift + plane - 1 >= begins) & (base >= shift)) * got.astype(F32)
    carries = [carry]

    for mine, got, bit, upper, unit in reversed(kept):
        middle = unit + bit
        begins = first_block(middle * rows)
        through, joined = weigh(begins < unit), weigh(begins < middle)
        ours, theirs = [], []
        for carry, a, b in zip(carries, mine, got):
            lower_state = jnp.where(upper, b, a).astype(F32)
            after = through * carry + joined * lower_state
            ours.append(jnp.where(upper, after, carry))
            theirs.append(jnp.where(upper, carry, after).astype(BF16))
        back = swap(jnp.stack(theirs), bit)
        carries = [x for i, c in enumerate(ours) for x in (c, back[i])]
    carries = [c.astype(BF16) for c in carries]

    within = within_block(meta, query, key, value, doc_count)
    natural = jnp.stack(carries)[jnp.arange(plane, dtype=jnp.int32) ^ member].reshape(width, DH)
    normed = norm_heads(meta, query, within, natural, gain, doc_count)
    partial_sum = jnp.dot(normed, weight, preferred_element_type=F32)
    return lax.psum_scatter(partial_sum.astype(BF16), "head", scatter_dimension=1, tiled=True)


def solution(mesh):
    return jax.shard_map(
        functools.partial(body, mesh.shape["seq"], mesh.shape["head"]),
        mesh=mesh,
        in_specs=(
            P("seq", "head"),
            P("seq", "head"),
            P("seq", "head"),
            P(),
            P("head"),
            P("head", None),
        ),
        out_specs=P("seq", "head"),
        check_vma=False,
    )
```

```python
import functools

import jax
import jax.numpy as jnp
from jax import lax
from jax.experimental import pallas as pl
from jax.experimental.pallas import tpu as pltpu
from jax.sharding import PartitionSpec as P

DH = 128
PLANES = 4
F32, BF16 = jnp.float32, jnp.bfloat16
LENS = 8
VMEM_LIMIT = 16 * 1024 * 1024
VMEM_MOST = 62 * 1024 * 1024


def doc_start(meta, doc_count, token):
    bound = jnp.int32(0)
    start = jnp.int32(0)
    for d in range(doc_count):
        bound = bound + meta[LENS + d]
        start = jnp.where(bound <= token, bound, start)
    return start


def call(kernel, grid, in_specs, out_specs, out_shape, flops, bytes_accessed, scratch=(), vmem=VMEM_LIMIT):
    return pl.pallas_call(
        kernel,
        grid_spec=pltpu.PrefetchScalarGridSpec(
            num_scalar_prefetch=1,
            grid=grid,
            in_specs=in_specs,
            out_specs=out_specs,
            scratch_shapes=scratch,
        ),
        out_shape=out_shape,
        compiler_params=pltpu.CompilerParams(vmem_limit_bytes=vmem),
        cost_estimate=pl.CostEstimate(flops=flops, bytes_accessed=bytes_accessed, transcendentals=0),
    )


def block_states(meta, key, value, doc_count, steps):
    rows, width = key.shape
    part = width // steps

    def kernel(meta_ref, k_ref, v_ref, o_ref):
        offset = meta_ref[0] * rows
        first = doc_start(meta_ref, doc_count, offset + rows - 1) - offset
        live = lax.broadcasted_iota(jnp.int32, (rows, DH), 0) >= first
        for h in range(part // DH):
            cols = slice(h * DH, (h + 1) * DH)
            k = jnp.where(live, k_ref[:, cols], jnp.zeros((), BF16))
            s = lax.dot_general(k, v_ref[:, cols], (((0,), (0,)), ((), ())), preferred_element_type=F32)
            o_ref[0, cols, :] = s.astype(BF16)

    def slot(g, m):
        return (g ^ m[1], 0, 0) if steps > 1 else (0, 0, 0)

    return call(
        kernel,
        (steps,),
        [pl.BlockSpec((rows, part), lambda g, m: (0, g))] * 2,
        pl.BlockSpec((1, part, DH), slot),
        jax.ShapeDtypeStruct((steps, part, DH), BF16),
        2 * rows * width * DH,
        2 * 2 * rows * width,
    )(meta, key, value)


def within_block(meta, query, key, value, doc_count):
    rows, width = query.shape
    part = DH
    for heads in (4, 3, 2):
        if width % (heads * DH) == 0:
            part = heads * DH
            break
    tile = rows // 2

    def kernel(meta_ref, q_ref, k_ref, v_ref, o_ref, mask_ref):
        @pl.when(pl.program_id(0) == 0)
        def _():
            offset = meta_ref[0] * rows
            t = lax.broadcasted_iota(jnp.int32, (rows, rows), 0)
            s = lax.broadcasted_iota(jnp.int32, (rows, rows), 1)
            pos = lax.broadcasted_iota(jnp.int32, (rows, 1), 0)
            first = jnp.zeros((rows, 1), jnp.int32)
            bound = -offset
            for d in range(doc_count):
                bound = bound + meta_ref[LENS + d]
                first = jnp.where(bound <= pos, bound, first)
            mask_ref[...] = jnp.where((s <= t) & (s >= first), 1.0, 0.0).astype(BF16)

        for h in range(part // DH):
            cols = slice(h * DH, (h + 1) * DH)
            for i in range(2):
                r = slice(i * tile, (i + 1) * tile)
                seen = (i + 1) * tile
                scores = lax.dot_general(
                    q_ref[r, cols], k_ref[:seen, cols], (((1,), (1,)), ((), ())), preferred_element_type=F32
                )
                scores = scores.astype(BF16) * mask_ref[r, :seen]
                o_ref[r, cols] = jnp.dot(scores, v_ref[:seen, cols], preferred_element_type=F32)

    spec = pl.BlockSpec((rows, part), lambda g, m: (0, g))
    return call(
        kernel,
        (width // part,),
        [spec] * 3,
        spec,
        jax.ShapeDtypeStruct((rows, width), F32),
        3 * rows * rows * width,
        10 * rows * width,
        [pltpu.VMEM((rows, rows), BF16)],
    )(meta, query, key, value)


def whole(shape):
    return pl.BlockSpec(shape, lambda *_: (0,) * len(shape))


def after(meta, *arrays):
    return lax.optimization_barrier((meta, *arrays))[0]


def factor(condition):
    return jnp.where(condition, 1.0, 0.0)


def split_states(meta, key, value, doc_count):
    rows, width = key.shape
    part = width // 4

    def kernel(meta_ref, k_hbm, v_hbm, send_ref, keep_ref, k_ref, v_ref, sems):
        copies = []
        for i, s in enumerate((1, 3, 0, 2)):
            cols = pl.ds(pl.multiple_of((meta_ref[1] ^ s) * part, DH), part)
            for n, (source, target) in enumerate(((k_hbm, k_ref), (v_hbm, v_ref))):
                copies.append(pltpu.make_async_copy(source.at[:, cols], target.at[i], sems.at[i, n]))
                copies[-1].start()
        offset = meta_ref[0] * rows
        first = doc_start(meta_ref, doc_count, offset + rows - 1) - offset
        live = lax.broadcasted_iota(jnp.int32, (rows, DH), 0) >= first
        for i in range(4):
            copies[2 * i].wait()
            copies[2 * i + 1].wait()
            o_ref = (send_ref, keep_ref)[i // 2]
            for h in range(part // DH):
                cols = slice(h * DH, (h + 1) * DH)
                k = jnp.where(live, k_ref[i, :, cols], jnp.zeros((), BF16))
                state = lax.dot_general(
                    k, v_ref[i, :, cols], (((0,), (0,)), ((), ())), preferred_element_type=F32
                )
                o_ref[i % 2, cols, :] = state.astype(BF16)

    return call(
        kernel,
        (1,),
        [pl.BlockSpec(memory_space=pltpu.HBM)] * 2,
        [whole((2, part, DH))] * 2,
        [jax.ShapeDtypeStruct((2, part, DH), BF16)] * 2,
        2 * rows * width * DH,
        2 * 2 * rows * width,
        [
            pltpu.VMEM((4, rows, part), BF16),
            pltpu.VMEM((4, rows, part), BF16),
            pltpu.SemaphoreType.DMA((4, 2)),
        ],
        VMEM_MOST,
    )(meta, key, value)


def seen_mask(meta_ref, rows, doc_count):
    offset = meta_ref[0] * rows
    t = lax.broadcasted_iota(jnp.int32, (rows, rows), 0)
    s = lax.broadcasted_iota(jnp.int32, (rows, rows), 1)
    pos = lax.broadcasted_iota(jnp.int32, (rows, 1), 0)
    first = jnp.zeros((rows, 1), jnp.int32)
    bound = -offset
    for d in range(doc_count):
        bound = bound + meta_ref[LENS + d]
        first = jnp.where(bound <= pos, bound, first)
    return jnp.where((s <= t) & (s >= first), 1.0, 0.0).astype(BF16)


def within_slots(meta, query, key, value, doc_count, slots, mask=None):
    rows, width = query.shape
    part = width // 4
    tile = rows // 2
    make = mask is None

    def kernel(meta_ref, q_ref, k_ref, v_ref, *rest):
        if make:
            o_ref, mask_ref = rest

            @pl.when(pl.program_id(0) == 0)
            def _():
                mask_ref[...] = seen_mask(meta_ref, rows, doc_count)
        else:
            mask_ref, o_ref = rest
        for h in range(part // DH):
            cols = slice(h * DH, (h + 1) * DH)
            for i in range(2):
                r = slice(i * tile, (i + 1) * tile)
                seen = (i + 1) * tile
                scores = lax.dot_general(
                    q_ref[r, cols], k_ref[:seen, cols], (((1,), (1,)), ((), ())), preferred_element_type=F32
                )
                scores = scores.astype(BF16) * mask_ref[r, :seen]
                o_ref[r, cols] = jnp.dot(scores, v_ref[:seen, cols], preferred_element_type=F32)

    count = len(slots)
    spec = pl.BlockSpec((rows, part), lambda g, m: (0, (g + slots[0]) ^ m[1]))
    out = pl.BlockSpec((rows, part), lambda g, m: (0, g))
    shape = jax.ShapeDtypeStruct((rows, part * count), F32)
    square = whole((rows, rows))
    return call(
        kernel,
        (count,),
        [spec] * 3 + [square] * (not make),
        [out, square] if make else out,
        [shape, jax.ShapeDtypeStruct((rows, rows), BF16)] if make else shape,
        3 * rows * rows * part * count,
        10 * rows * part * count,
    )(meta, query, key, value, *([] if make else [mask]))


def small(kernel, meta, arrays, shape, count):
    return call(
        kernel,
        (1,),
        [whole(a.shape) for a in arrays],
        [whole(shape)] * count,
        [jax.ShapeDtypeStruct(shape, BF16)] * count,
        shape[0] * shape[1],
        2 * shape[0] * shape[1] * (len(arrays) + count),
    )(meta, *arrays)


def join_core(meta, keep, got, rows, doc_count):
    def kernel(meta_ref, keep_ref, got_ref, a_ref, b_ref):
        low = meta_ref[0] & -2
        joined = factor(doc_start(meta_ref, doc_count, (low + 2) * rows - 1) < (low + 1) * rows)
        upper = (meta_ref[1] & 1) != 0
        own, other = jnp.where(upper, 1.0, joined), jnp.where(upper, joined, 1.0)
        for i, o_ref in enumerate((a_ref, b_ref)):
            o_ref[...] = (own * keep_ref[i].astype(F32) + other * got_ref[i].astype(F32)).astype(BF16)

    return small(kernel, meta, (keep, got), keep.shape[1:], 2)


def join_chips(meta, mine, got, rows, doc_count):
    def kernel(meta_ref, a_ref, b_ref, o_ref):
        low = meta_ref[0] & -4
        joined = factor(doc_start(meta_ref, doc_count, (low + 4) * rows - 1) < (low + 2) * rows)
        upper = (meta_ref[1] & 2) != 0
        own, other = jnp.where(upper, 1.0, joined), jnp.where(upper, joined, 1.0)
        o_ref[...] = (own * a_ref[...].astype(F32) + other * b_ref[...].astype(F32)).astype(BF16)

    return small(kernel, meta, (mine, got), mine.shape, 1)[0]


def join_planes(meta, plane_sum, previous, rows, doc_count):
    def kernel(meta_ref, a_ref, b_ref, o_ref):
        low = meta_ref[0] & -4
        joined = factor(doc_start(meta_ref, doc_count, (low + 4) * rows - 1) < low * rows)
        o_ref[...] = (a_ref[...].astype(F32) + joined * b_ref[...].astype(F32)).astype(BF16)

    return small(kernel, meta, (plane_sum, previous), plane_sum.shape, 1)[0]


def carry_in_chip(meta_ref, chip, keep, got, rows, doc_count):
    low = meta_ref[0] & -2
    begins = doc_start(meta_ref, doc_count, (low + 1) * rows)
    through, joined = factor(begins < low * rows), factor(begins < (low + 1) * rows)
    upper = (meta_ref[1] & 1) != 0
    later = through * chip + joined * jnp.where(upper, got, keep).astype(F32)
    return jnp.where(upper, later, chip), jnp.where(upper, chip, later)


def carry_first(meta, near, far, mine, got, keep, core_got, rows, doc_count):
    def kernel(meta_ref, near_ref, far_ref, a_ref, b_ref, keep_ref, got_ref, o_ref, core_ref, chip_ref):
        low = meta_ref[0] & -4
        begins = doc_start(meta_ref, doc_count, low * rows)
        first = factor(begins < low * rows) * near_ref[...].astype(F32)
        first = first + factor(begins < (low - 4) * rows) * far_ref[...].astype(F32)
        begins = doc_start(meta_ref, doc_count, (low + 2) * rows)
        through, joined = factor(begins < low * rows), factor(begins < (low + 2) * rows)
        upper = (meta_ref[1] & 2) != 0
        later = through * first + joined * jnp.where(upper, b_ref[...], a_ref[...]).astype(F32)
        chip_ref[...] = jnp.where(upper, first, later).astype(BF16)
        chip = jnp.where(upper, later, first)
        ours, theirs = carry_in_chip(meta_ref, chip, keep_ref[0], got_ref[0], rows, doc_count)
        o_ref[...] = ours.astype(BF16)
        core_ref[...] = theirs.astype(BF16)

    return small(kernel, meta, (near, far, mine, got, keep, core_got), mine.shape, 3)


def carry_second(meta, chip, keep, core_got, rows, doc_count):
    def kernel(meta_ref, chip_ref, keep_ref, got_ref, o_ref, core_ref):
        ours, theirs = carry_in_chip(
            meta_ref, chip_ref[...].astype(F32), keep_ref[1], got_ref[1], rows, doc_count
        )
        o_ref[...] = ours.astype(BF16)
        core_ref[...] = theirs.astype(BF16)

    return small(kernel, meta, (chip, keep, core_got), chip.shape, 2)


def norm_heads(meta, query, within, carry, gain, doc_count, slots=(None, None, None)):
    rows = query.shape[0]
    part = carry.shape[0]

    def kernel(meta_ref, q_ref, w_ref, c_ref, g_ref, o_ref):
        offset = meta_ref[0] * rows
        begins = doc_start(meta_ref, doc_count, offset)
        bound = jnp.int32(0)
        end = jnp.int32(0)
        for d in range(doc_count):
            previous = bound
            bound = bound + meta_ref[LENS + d]
            end = jnp.where(previous <= offset, bound, end)
        stop = jnp.where(begins < offset, end - offset, 0)
        cross = lax.broadcasted_iota(jnp.int32, (rows, DH), 0) < stop
        for h in range(part // DH):
            cols = slice(h * DH, (h + 1) * DH)
            term = jnp.dot(q_ref[:, cols], c_ref[cols, :], preferred_element_type=F32)
            mixture = w_ref[:, cols].astype(F32) + jnp.where(cross, term, 0.0)
            mean = jnp.mean(mixture * mixture, axis=-1, keepdims=True)
            o_ref[:, cols] = (mixture * lax.rsqrt(mean + 1e-06) * g_ref[:, cols]).astype(BF16)

    def block(place):
        if place is None:
            return lambda i, m: (0, 0)
        if isinstance(place, int):
            return lambda i, m: (0, place)
        return lambda i, m: (0, m[1] ^ place[1])

    return call(
        kernel,
        (1,),
        [
            pl.BlockSpec((rows, part), block(slots[0])),
            pl.BlockSpec((rows, part), block(slots[1])),
            whole((part, DH)),
            pl.BlockSpec((1, part), block(slots[2])),
        ],
        whole((rows, part)),
        jax.ShapeDtypeStruct((rows, part), BF16),
        2 * rows * part * DH,
        8 * rows * part,
    )(meta, query, within, carry, gain.reshape(1, -1))


TILES = 4


def project_own(meta, pieces, weight, columns):
    rows, part = pieces[0].shape
    tile = columns // TILES
    count = len(pieces)

    def kernel(meta_ref, *refs):
        ns, ws, o_ref = refs[:count], refs[count : 2 * count], refs[-1]
        n = jnp.concatenate([r[...] for r in ns], axis=1)
        w = jnp.concatenate([r[...] for r in ws], axis=0)
        o_ref[...] = jnp.dot(n, w, preferred_element_type=F32)

    return call(
        kernel,
        (TILES,),
        [whole((rows, part))] * count
        + [pl.BlockSpec((part, tile), lambda n, m, s=s: (m[1] ^ s, m[2] * TILES + n)) for s in range(count)],
        pl.BlockSpec((rows, tile), lambda n, m: (0, n)),
        jax.ShapeDtypeStruct((rows, columns), F32),
        2 * rows * part * count * columns,
        2 * part * count * columns + 4 * rows * columns,
    )(meta, *pieces, *[weight] * count)


def project_more(meta, total, pieces, weights, dtype):
    rows, columns = total.shape
    part = pieces[0].shape[1]
    tile = columns // TILES
    count = len(pieces)
    flat = []
    for ws in weights:
        start = 0
        for w in ws:
            tiles = w.shape[1] // tile
            flat.append((w, start, tiles))
            start += tiles

    def kernel(meta_ref, t_ref, *refs):
        ns, ws, o_ref = refs[:count], refs[count:-1], refs[-1]
        n = jnp.concatenate([r[...] for r in ns], axis=1)
        for c in range(TILES):

            @pl.when(pl.program_id(0) == c)
            def _():
                held = [r[...] for r, (_, start, tiles) in zip(ws, flat) if start <= c < start + tiles]
                w = jnp.concatenate(held, axis=0)
                o_ref[...] = (t_ref[...] + jnp.dot(n, w, preferred_element_type=F32)).astype(dtype)

    def column(start, tiles):
        return lambda n, m: (0, jnp.clip(n - start, 0, tiles - 1))

    out_spec = pl.BlockSpec((rows, tile), lambda n, m: (0, n ^ (m[3] * (TILES // 2))))
    return call(
        kernel,
        (TILES,),
        [out_spec]
        + [whole((rows, part))] * count
        + [pl.BlockSpec((part, tile), column(start, tiles)) for _, start, tiles in flat],
        out_spec,
        jax.ShapeDtypeStruct((rows, columns), dtype),
        2 * rows * part * count * columns,
        2 * part * count * columns + 6 * rows * columns,
    )(meta, total, *pieces, *[w for w, _, _ in flat])


def pair_body(n_seq, query, key, value, doc_lengths, gain, weight):
    rows, width = query.shape
    docs = doc_lengths.shape[0]
    plane, part = 4, width // 4
    columns = weight.shape[1] // 2
    half = columns // 2
    block = lax.axis_index("seq").astype(jnp.int32)
    group = lax.axis_index("head").astype(jnp.int32)
    member = block % plane
    side = (block // plane) % 2
    meta = jnp.concatenate([
        jnp.stack([block, member, group, side]), jnp.zeros((LENS - 4,), jnp.int32), doc_lengths
    ])

    def swap(x, bit):
        return lax.ppermute(x, "seq", [(i, i ^ bit) for i in range(n_seq)])

    def shift(x, count):
        return lax.ppermute(x, "seq", [(i, i + count) for i in range(n_seq - count)])

    def flip(x):
        return lax.ppermute(x, "head", [(0, 1), (1, 0)])

    def behind(x, *arrays):
        return lax.optimization_barrier((x, *arrays))[0]

    quarter = half // 2
    sent = [(side * half, half), ((1 - side) * half, quarter)]
    sent = [
        lax.dynamic_slice(weight, (member * part, (1 - group) * columns + at), (part, size))
        for at, size in sent
    ]

    send, keep = split_states(meta, key, value, docs)
    core_got = swap(send, 1)
    w0 = [flip(behind(sent[0], send))]
    chip0, chip2 = join_core(meta, keep, core_got, rows, docs)
    chip_got = swap(chip2, 2)
    within0, mask = within_slots(after(meta, chip0), query, key, value, docs, (0,))
    within1 = within_slots(after(meta, within0), query, key, value, docs, (1,), mask)
    plane_sum = join_chips(after(meta, within1), chip0, chip_got, rows, docs)
    near = shift(plane_sum, plane)
    within2 = within_slots(after(meta, plane_sum), query, key, value, docs, (2,), mask)
    both = join_planes(after(meta, within2), plane_sum, near, rows, docs)
    far = shift(both, 2 * plane)
    w0.append(flip(behind(sent[1], both)))
    within3 = within_slots(after(meta, both), query, key, value, docs, (3,), mask)
    carry0, core_carry0, chip_carry = carry_first(
        after(meta, within3), near, far, chip0, chip_got, keep, core_got, rows, docs
    )
    carry1 = swap(core_carry0, 1)
    chip_carry2 = swap(chip_carry, 2)

    def norm(slot, within, carry):
        return norm_heads(
            meta, query, within, carry, gain, docs, (("slot", slot), None, ("slot", slot))
        )

    normed0 = norm(0, within0, carry0)
    far0 = flip(normed0)
    normed1 = norm(1, within1, carry1)
    far1 = flip(normed1)
    carry2, core_carry2 = carry_second(meta, chip_carry2, keep, core_got, rows, docs)
    carry3 = swap(core_carry2, 1)
    normed2 = norm(2, within2, carry2)
    far2 = flip(normed2)
    normed3 = norm(3, within3, carry3)
    far3 = flip(normed3)

    first, second = lax.optimization_barrier((*w0, chip_carry2, normed1))[:2]
    w2 = [swap(first, 2), swap(second, 2)]
    w0.append(swap(first[:, quarter:], plane))
    w2.append(swap(w2[0][:, quarter:], plane))
    w1 = [swap(w, 1) for w in w0]
    w3 = [swap(w, 1) for w in w2]

    total = project_own(after(meta, far1), [normed0, normed1, normed2, normed3], weight, columns)
    total = project_more(meta, total, [far0, far1], [w0, w1], F32)
    total = project_more(meta, total, [far2], [w2], F32)
    return project_more(meta, total, [far3], [w3], BF16)


def body(n_seq, n_head, query, key, value, doc_lengths, gain, weight):
    rows, width = query.shape
    doc_count = doc_lengths.shape[0]
    plane = n_seq // PLANES
    if n_head == 2 and plane == 4 and width % (4 * DH) == 0:
        return pair_body(n_seq, query, key, value, doc_lengths, gain, weight)
    block = lax.axis_index("seq").astype(jnp.int32)
    group = lax.axis_index("head").astype(jnp.int32)
    member = block % plane
    meta = jnp.concatenate([
        jnp.stack([block, member, group]), jnp.zeros((LENS - 3,), jnp.int32), doc_lengths
    ])

    bounds = jnp.cumsum(doc_lengths)

    def first_block(token):
        starts = jnp.max(jnp.where(bounds <= token, bounds, 0))
        return starts // rows

    def weigh(condition):
        return condition.astype(F32)

    def swap(x, bit):
        return lax.ppermute(x, "seq", [(i, i ^ bit) for i in range(n_seq)])

    by_slot = (width // DH) % plane == 0
    steps = plane if by_slot else 1
    states = block_states(meta, key, value, doc_count, steps)
    if not by_slot:
        states = states.reshape(plane, width // plane, DH)[jnp.arange(plane, dtype=jnp.int32) ^ member]
    slots = [states[s] for s in range(plane)]

    kept = []
    bit = 1
    while bit < plane:
        mine, send = slots[0::2], slots[1::2]
        got = swap(jnp.stack(send), bit)
        got = [got[i] for i in range(len(send))]
        upper = (member & bit) != 0
        unit = block & ~(2 * bit - 1)
        joined = weigh(first_block((unit + 2 * bit) * rows - 1) < unit + bit)
        own_factor = jnp.where(upper, 1.0, joined)
        got_factor = jnp.where(upper, joined, 1.0)
        kept.append((mine, got, bit, upper, unit))
        slots = [
            (own_factor * a.astype(F32) + got_factor * b.astype(F32)).astype(BF16) for a, b in zip(mine, got)
        ]
        bit *= 2
    base = block - member
    begins = first_block(base * rows)
    carry = jnp.zeros(slots[0].shape, F32)
    for d in range(PLANES - 1, 0, -1):
        shift = d * plane
        got = lax.ppermute(slots[0], "seq", [(i, i + shift) for i in range(n_seq - shift)])
        carry = carry + weigh((base - shift + plane - 1 >= begins) & (base >= shift)) * got.astype(F32)
    carries = [carry]

    for mine, got, bit, upper, unit in reversed(kept):
        middle = unit + bit
        begins = first_block(middle * rows)
        through, joined = weigh(begins < unit), weigh(begins < middle)
        ours, theirs = [], []
        for carry, a, b in zip(carries, mine, got):
            lower_state = jnp.where(upper, b, a).astype(F32)
            after = through * carry + joined * lower_state
            ours.append(jnp.where(upper, after, carry))
            theirs.append(jnp.where(upper, carry, after).astype(BF16))
        back = swap(jnp.stack(theirs), bit)
        carries = [x for i, c in enumerate(ours) for x in (c, back[i])]
    carries = [c.astype(BF16) for c in carries]

    within = within_block(meta, query, key, value, doc_count)
    natural = jnp.stack(carries)[jnp.arange(plane, dtype=jnp.int32) ^ member].reshape(width, DH)
    normed = norm_heads(meta, query, within, natural, gain, doc_count)
    partial_sum = jnp.dot(normed, weight, preferred_element_type=F32)
    return lax.psum_scatter(partial_sum.astype(BF16), "head", scatter_dimension=1, tiled=True)


def solution(mesh):
    return jax.shard_map(
        functools.partial(body, mesh.shape["seq"], mesh.shape["head"]),
        mesh=mesh,
        in_specs=(
            P("seq", "head"),
            P("seq", "head"),
            P("seq", "head"),
            P(),
            P("head"),
            P("head", None),
        ),
        out_specs=P("seq", "head"),
        check_vma=False,
    )
```

```python
import functools

import jax
import jax.numpy as jnp
from jax import lax
from jax.experimental import pallas as pl
from jax.experimental.pallas import tpu as pltpu
from jax.sharding import PartitionSpec as P

DH = 128
PLANES = 4
F32, BF16 = jnp.float32, jnp.bfloat16
LENS = 8
VMEM_LIMIT = 16 * 1024 * 1024
VMEM_MOST = 62 * 1024 * 1024


def doc_start(meta, doc_count, token):
    bound = jnp.int32(0)
    start = jnp.int32(0)
    for d in range(doc_count):
        bound = bound + meta[LENS + d]
        start = jnp.where(bound <= token, bound, start)
    return start


def call(kernel, grid, in_specs, out_specs, out_shape, flops, bytes_accessed, scratch=(), vmem=VMEM_LIMIT):
    return pl.pallas_call(
        kernel,
        grid_spec=pltpu.PrefetchScalarGridSpec(
            num_scalar_prefetch=1,
            grid=grid,
            in_specs=in_specs,
            out_specs=out_specs,
            scratch_shapes=scratch,
        ),
        out_shape=out_shape,
        compiler_params=pltpu.CompilerParams(vmem_limit_bytes=vmem),
        cost_estimate=pl.CostEstimate(flops=flops, bytes_accessed=bytes_accessed, transcendentals=0),
    )


def block_states(meta, key, value, doc_count, steps):
    rows, width = key.shape
    part = width // steps

    def kernel(meta_ref, k_ref, v_ref, o_ref):
        offset = meta_ref[0] * rows
        first = doc_start(meta_ref, doc_count, offset + rows - 1) - offset
        live = lax.broadcasted_iota(jnp.int32, (rows, DH), 0) >= first
        for h in range(part // DH):
            cols = slice(h * DH, (h + 1) * DH)
            k = jnp.where(live, k_ref[:, cols], jnp.zeros((), BF16))
            s = lax.dot_general(k, v_ref[:, cols], (((0,), (0,)), ((), ())), preferred_element_type=F32)
            o_ref[0, cols, :] = s.astype(BF16)

    def slot(g, m):
        return (g ^ m[1], 0, 0) if steps > 1 else (0, 0, 0)

    return call(
        kernel,
        (steps,),
        [pl.BlockSpec((rows, part), lambda g, m: (0, g))] * 2,
        pl.BlockSpec((1, part, DH), slot),
        jax.ShapeDtypeStruct((steps, part, DH), BF16),
        2 * rows * width * DH,
        2 * 2 * rows * width,
    )(meta, key, value)


def within_block(meta, query, key, value, doc_count):
    rows, width = query.shape
    part = DH
    for heads in (4, 3, 2):
        if width % (heads * DH) == 0:
            part = heads * DH
            break
    tile = rows // 2

    def kernel(meta_ref, q_ref, k_ref, v_ref, o_ref, mask_ref):
        @pl.when(pl.program_id(0) == 0)
        def _():
            offset = meta_ref[0] * rows
            t = lax.broadcasted_iota(jnp.int32, (rows, rows), 0)
            s = lax.broadcasted_iota(jnp.int32, (rows, rows), 1)
            pos = lax.broadcasted_iota(jnp.int32, (rows, 1), 0)
            first = jnp.zeros((rows, 1), jnp.int32)
            bound = -offset
            for d in range(doc_count):
                bound = bound + meta_ref[LENS + d]
                first = jnp.where(bound <= pos, bound, first)
            mask_ref[...] = jnp.where((s <= t) & (s >= first), 1.0, 0.0).astype(BF16)

        for h in range(part // DH):
            cols = slice(h * DH, (h + 1) * DH)
            for i in range(2):
                r = slice(i * tile, (i + 1) * tile)
                seen = (i + 1) * tile
                scores = lax.dot_general(
                    q_ref[r, cols], k_ref[:seen, cols], (((1,), (1,)), ((), ())), preferred_element_type=F32
                )
                scores = scores.astype(BF16) * mask_ref[r, :seen]
                o_ref[r, cols] = jnp.dot(scores, v_ref[:seen, cols], preferred_element_type=F32)

    spec = pl.BlockSpec((rows, part), lambda g, m: (0, g))
    return call(
        kernel,
        (width // part,),
        [spec] * 3,
        spec,
        jax.ShapeDtypeStruct((rows, width), F32),
        3 * rows * rows * width,
        10 * rows * width,
        [pltpu.VMEM((rows, rows), BF16)],
    )(meta, query, key, value)


def local(kernel, meta, arrays, shapes, micros, limit=4):
    vmem = pl.BlockSpec(memory_space=pltpu.VMEM)
    return pl.pallas_call(
        kernel,
        out_shape=shapes,
        in_specs=[pl.BlockSpec(memory_space=pltpu.SMEM)] + [vmem] * len(arrays),
        out_specs=[vmem] * len(shapes),
        compiler_params=pltpu.CompilerParams(vmem_limit_bytes=limit * 1024 * 1024),
        cost_estimate=pl.CostEstimate(flops=int(micros * 1e9), bytes_accessed=1024, transcendentals=0),
    )(meta, *arrays)


def whole(shape):
    return pl.BlockSpec(shape, lambda *_: (0,) * len(shape))


def after(meta, *arrays):
    return lax.optimization_barrier((meta, *arrays))[0]


def factor(condition):
    return jnp.where(condition, 1.0, 0.0)


def head_columns(meta_ref, slot, part, h):
    return pl.ds(pl.multiple_of((meta_ref[1] ^ slot) * part + h * DH, DH), DH)


def split_states(meta, key, value, doc_count):
    rows, width = key.shape
    part = width // 4

    def kernel(meta_ref, k_ref, v_ref, send_ref, keep_ref):
        offset = meta_ref[0] * rows
        first = doc_start(meta_ref, doc_count, offset + rows - 1) - offset
        live = lax.broadcasted_iota(jnp.int32, (rows, DH), 0) >= first
        for i, s in enumerate((1, 3, 0, 2)):
            o_ref = (send_ref, keep_ref)[i // 2]
            for h in range(part // DH):
                cols = head_columns(meta_ref, s, part, h)
                k = jnp.where(live, k_ref[:, cols], jnp.zeros((), BF16))
                state = lax.dot_general(
                    k, v_ref[:, cols], (((0,), (0,)), ((), ())), preferred_element_type=F32
                )
                o_ref[i % 2, h * DH : (h + 1) * DH, :] = state.astype(BF16)

    return local(kernel, meta, (key, value), [jax.ShapeDtypeStruct((2, part, DH), BF16)] * 2, 2, 8)


def seen_mask(meta_ref, rows, doc_count):
    offset = meta_ref[0] * rows
    t = lax.broadcasted_iota(jnp.int32, (rows, rows), 0)
    s = lax.broadcasted_iota(jnp.int32, (rows, rows), 1)
    pos = lax.broadcasted_iota(jnp.int32, (rows, 1), 0)
    first = jnp.zeros((rows, 1), jnp.int32)
    bound = -offset
    for d in range(doc_count):
        bound = bound + meta_ref[LENS + d]
        first = jnp.where(bound <= pos, bound, first)
    return jnp.where((s <= t) & (s >= first), 1.0, 0.0).astype(BF16)


def within_slot(meta, query, key, value, doc_count, slot, mask=None):
    rows, width = query.shape
    part = width // 4
    tile = rows // 2
    make = mask is None

    def kernel(meta_ref, q_ref, k_ref, v_ref, *rest):
        if make:
            o_ref, mask_ref = rest
            mask_ref[...] = seen_mask(meta_ref, rows, doc_count)
        else:
            mask_ref, o_ref = rest
        for h in range(part // DH):
            cols = head_columns(meta_ref, slot, part, h)
            for i in range(2):
                r = slice(i * tile, (i + 1) * tile)
                seen = (i + 1) * tile
                scores = lax.dot_general(
                    q_ref[r, cols], k_ref[:seen, cols], (((1,), (1,)), ((), ())), preferred_element_type=F32
                )
                scores = scores.astype(BF16) * mask_ref[r, :seen]
                o_ref[r, h * DH : (h + 1) * DH] = jnp.dot(scores, v_ref[:seen, cols], preferred_element_type=F32)

    shapes = [jax.ShapeDtypeStruct((rows, part), F32)]
    arrays = (query, key, value)
    if make:
        return local(kernel, meta, arrays, shapes + [jax.ShapeDtypeStruct((rows, rows), BF16)], 2, 12)
    return local(kernel, meta, (*arrays, mask), shapes, 2, 12)[0]


def small(kernel, meta, arrays, shape, count):
    return local(kernel, meta, arrays, [jax.ShapeDtypeStruct(shape, BF16)] * count, 0.6)


def join_core(meta, keep, got, rows, doc_count):
    def kernel(meta_ref, keep_ref, got_ref, a_ref, b_ref):
        low = meta_ref[0] & -2
        joined = factor(doc_start(meta_ref, doc_count, (low + 2) * rows - 1) < (low + 1) * rows)
        upper = (meta_ref[1] & 1) != 0
        own, other = jnp.where(upper, 1.0, joined), jnp.where(upper, joined, 1.0)
        for i, o_ref in enumerate((a_ref, b_ref)):
            o_ref[...] = (own * keep_ref[i].astype(F32) + other * got_ref[i].astype(F32)).astype(BF16)

    return small(kernel, meta, (keep, got), keep.shape[1:], 2)


def join_chips(meta, mine, got, rows, doc_count):
    def kernel(meta_ref, a_ref, b_ref, o_ref):
        low = meta_ref[0] & -4
        joined = factor(doc_start(meta_ref, doc_count, (low + 4) * rows - 1) < (low + 2) * rows)
        upper = (meta_ref[1] & 2) != 0
        own, other = jnp.where(upper, 1.0, joined), jnp.where(upper, joined, 1.0)
        o_ref[...] = (own * a_ref[...].astype(F32) + other * b_ref[...].astype(F32)).astype(BF16)

    return small(kernel, meta, (mine, got), mine.shape, 1)[0]


def join_planes(meta, plane_sum, previous, rows, doc_count):
    def kernel(meta_ref, a_ref, b_ref, o_ref):
        low = meta_ref[0] & -4
        joined = factor(doc_start(meta_ref, doc_count, (low + 4) * rows - 1) < low * rows)
        o_ref[...] = (a_ref[...].astype(F32) + joined * b_ref[...].astype(F32)).astype(BF16)

    return small(kernel, meta, (plane_sum, previous), plane_sum.shape, 1)[0]


def carry_in_chip(meta_ref, chip, keep, got, rows, doc_count):
    low = meta_ref[0] & -2
    begins = doc_start(meta_ref, doc_count, (low + 1) * rows)
    through, joined = factor(begins < low * rows), factor(begins < (low + 1) * rows)
    upper = (meta_ref[1] & 1) != 0
    later = through * chip + joined * jnp.where(upper, got, keep).astype(F32)
    return jnp.where(upper, later, chip), jnp.where(upper, chip, later)


def carry_first(meta, near, far, mine, got, keep, core_got, rows, doc_count):
    def kernel(meta_ref, near_ref, far_ref, a_ref, b_ref, keep_ref, got_ref, o_ref, core_ref, chip_ref):
        low = meta_ref[0] & -4
        begins = doc_start(meta_ref, doc_count, low * rows)
        first = factor(begins < low * rows) * near_ref[...].astype(F32)
        first = first + factor(begins < (low - 4) * rows) * far_ref[...].astype(F32)
        begins = doc_start(meta_ref, doc_count, (low + 2) * rows)
        through, joined = factor(begins < low * rows), factor(begins < (low + 2) * rows)
        upper = (meta_ref[1] & 2) != 0
        later = through * first + joined * jnp.where(upper, b_ref[...], a_ref[...]).astype(F32)
        chip_ref[...] = jnp.where(upper, first, later).astype(BF16)
        chip = jnp.where(upper, later, first)
        ours, theirs = carry_in_chip(meta_ref, chip, keep_ref[0], got_ref[0], rows, doc_count)
        o_ref[...] = ours.astype(BF16)
        core_ref[...] = theirs.astype(BF16)

    return small(kernel, meta, (near, far, mine, got, keep, core_got), mine.shape, 3)


def carry_second(meta, chip, keep, core_got, rows, doc_count):
    def kernel(meta_ref, chip_ref, keep_ref, got_ref, o_ref, core_ref):
        ours, theirs = carry_in_chip(
            meta_ref, chip_ref[...].astype(F32), keep_ref[1], got_ref[1], rows, doc_count
        )
        o_ref[...] = ours.astype(BF16)
        core_ref[...] = theirs.astype(BF16)

    return small(kernel, meta, (chip, keep, core_got), chip.shape, 2)


def norm_heads(meta, query, within, carry, gain, doc_count, slot=None):
    rows = query.shape[0]
    part = carry.shape[0]

    def kernel(meta_ref, q_ref, w_ref, c_ref, g_ref, o_ref):
        offset = meta_ref[0] * rows
        begins = doc_start(meta_ref, doc_count, offset)
        bound = jnp.int32(0)
        end = jnp.int32(0)
        for d in range(doc_count):
            previous = bound
            bound = bound + meta_ref[LENS + d]
            end = jnp.where(previous <= offset, bound, end)
        stop = jnp.where(begins < offset, end - offset, 0)
        cross = lax.broadcasted_iota(jnp.int32, (rows, DH), 0) < stop
        for h in range(part // DH):
            here = slice(h * DH, (h + 1) * DH)
            cols = here if slot is None else head_columns(meta_ref, slot, part, h)
            term = jnp.dot(q_ref[:, cols], c_ref[here, :], preferred_element_type=F32)
            mixture = w_ref[:, here] + jnp.where(cross, term, 0.0)
            mean = jnp.mean(mixture * mixture, axis=-1, keepdims=True)
            o_ref[:, here] = (mixture * lax.rsqrt(mean + 1e-06) * g_ref[:, cols]).astype(BF16)

    shapes = [jax.ShapeDtypeStruct((rows, part), BF16)]
    return local(kernel, meta, (query, within, carry, gain.reshape(1, -1)), shapes, 1, 8)[0]


TILES = 4


def project_own(meta, pieces, weight, columns):
    rows, part = pieces[0].shape
    tile = columns // TILES
    count = len(pieces)

    def kernel(meta_ref, *refs):
        ns, ws, o_ref = refs[:count], refs[count : 2 * count], refs[-1]
        n = jnp.concatenate([r[...] for r in ns], axis=1)
        w = jnp.concatenate([r[...] for r in ws], axis=0)
        o_ref[...] = jnp.dot(n, w, preferred_element_type=F32)

    return call(
        kernel,
        (TILES,),
        [whole((rows, part))] * count
        + [pl.BlockSpec((part, tile), lambda n, m, s=s: (m[1] ^ s, m[2] * TILES + n)) for s in range(count)],
        pl.BlockSpec((rows, tile), lambda n, m: (0, n)),
        jax.ShapeDtypeStruct((rows, columns), F32),
        5 * 10**9,
        1024,
    )(meta, *pieces, *[weight] * count)


def project_more(meta, total, pieces, weights, dtype):
    rows, columns = total.shape
    part = pieces[0].shape[1]
    tile = columns // TILES
    count = len(pieces)
    flat = []
    for ws in weights:
        start = 0
        for w in ws:
            tiles = w.shape[1] // tile
            flat.append((w, start, tiles))
            start += tiles

    def kernel(meta_ref, t_ref, *refs):
        ns, ws, o_ref = refs[:count], refs[count:-1], refs[-1]
        n = jnp.concatenate([r[...] for r in ns], axis=1)
        for c in range(TILES):

            @pl.when(pl.program_id(0) == c)
            def _():
                held = [r[...] for r, (_, start, tiles) in zip(ws, flat) if start <= c < start + tiles]
                w = jnp.concatenate(held, axis=0)
                o_ref[...] = (t_ref[...] + jnp.dot(n, w, preferred_element_type=F32)).astype(dtype)

    def column(start, tiles):
        return lambda n, m: (0, jnp.clip(n - start, 0, tiles - 1))

    out_spec = pl.BlockSpec((rows, tile), lambda n, m: (0, n ^ (m[3] * (TILES // 2))))
    return call(
        kernel,
        (TILES,),
        [out_spec]
        + [whole((rows, part))] * count
        + [pl.BlockSpec((part, tile), column(start, tiles)) for _, start, tiles in flat],
        out_spec,
        jax.ShapeDtypeStruct((rows, columns), dtype),
        3 * 10**9,
        1024,
    )(meta, total, *pieces, *[w for w, _, _ in flat])


def pair_body(n_seq, query, key, value, doc_lengths, gain, weight):
    rows, width = query.shape
    docs = doc_lengths.shape[0]
    plane, part = 4, width // 4
    columns = weight.shape[1] // 2
    half = columns // 2
    block = lax.axis_index("seq").astype(jnp.int32)
    group = lax.axis_index("head").astype(jnp.int32)
    member = block % plane
    side = (block // plane) % 2
    meta = jnp.concatenate([
        jnp.stack([block, member, group, side]), jnp.zeros((LENS - 4,), jnp.int32), doc_lengths
    ])

    def swap(x, bit):
        return lax.ppermute(x, "seq", [(i, i ^ bit) for i in range(n_seq)])

    def shift(x, count):
        return lax.ppermute(x, "seq", [(i, i + count) for i in range(n_seq - count)])

    def flip(x):
        return lax.ppermute(x, "head", [(0, 1), (1, 0)])

    def behind(x, *arrays):
        return lax.optimization_barrier((x, *arrays))[0]

    quarter = half // 2
    sent = [(side * half, half), ((1 - side) * half, quarter)]
    sent = [
        lax.dynamic_slice(weight, (member * part, (1 - group) * columns + at), (part, size))
        for at, size in sent
    ]
    w0 = [flip(x) for x in sent]

    send, keep = split_states(after(meta, sent[0]), key, value, docs)
    core_got = swap(send, 1)
    query = behind(query, send)
    within0, mask = within_slot(after(meta, send), query, key, value, docs, 0)
    chip0, chip2 = join_core(after(meta, within0), keep, core_got, rows, docs)
    chip_got = swap(chip2, 2)
    within1 = within_slot(after(meta, chip0), query, key, value, docs, 1, mask)
    plane_sum = join_chips(after(meta, within1), chip0, chip_got, rows, docs)
    near = shift(plane_sum, plane)
    within2 = within_slot(after(meta, plane_sum), query, key, value, docs, 2, mask)
    both = join_planes(after(meta, within2), plane_sum, near, rows, docs)
    far = shift(both, 2 * plane)
    within3 = within_slot(after(meta, both), query, key, value, docs, 3, mask)
    carry0, core_carry0, chip_carry = carry_first(
        after(meta, within3), near, far, chip0, chip_got, keep, core_got, rows, docs
    )
    carry1 = swap(core_carry0, 1)
    chip_carry2 = swap(chip_carry, 2)

    def norm(slot, within, carry):
        return norm_heads(meta, query, within, carry, gain, docs, slot)

    normed0 = norm(0, within0, carry0)
    far0 = flip(normed0)
    normed1 = norm(1, within1, carry1)
    far1 = flip(normed1)
    carry2, core_carry2 = carry_second(meta, chip_carry2, keep, core_got, rows, docs)
    carry3 = swap(core_carry2, 1)
    normed2 = norm(2, within2, carry2)
    far2 = flip(normed2)
    normed3 = norm(3, within3, carry3)
    far3 = flip(normed3)

    first, second = lax.optimization_barrier((*w0, chip_carry2, normed0, normed1))[:2]
    total = project_own(after(meta, far0), [normed0, normed1, normed2, normed3], weight, columns)
    w2 = [swap(first, 2), swap(second, 2)]
    w0.append(swap(first[:, quarter:], plane))
    w2.append(swap(behind(w2[0], total)[:, quarter:], plane))
    w1 = [swap(w, 1) for w in w0]
    w3 = [swap(w, 1) for w in w2]

    total = project_more(meta, total, [far0, far1], [w0, w1], F32)
    total = project_more(meta, total, [far2], [w2], F32)
    return project_more(meta, total, [far3], [w3], BF16)


def body(n_seq, n_head, query, key, value, doc_lengths, gain, weight):
    rows, width = query.shape
    doc_count = doc_lengths.shape[0]
    plane = n_seq // PLANES
    if n_head == 2 and plane == 4 and width % (4 * DH) == 0:
        return pair_body(n_seq, query, key, value, doc_lengths, gain, weight)
    block = lax.axis_index("seq").astype(jnp.int32)
    group = lax.axis_index("head").astype(jnp.int32)
    member = block % plane
    meta = jnp.concatenate([
        jnp.stack([block, member, group]), jnp.zeros((LENS - 3,), jnp.int32), doc_lengths
    ])

    bounds = jnp.cumsum(doc_lengths)

    def first_block(token):
        starts = jnp.max(jnp.where(bounds <= token, bounds, 0))
        return starts // rows

    def weigh(condition):
        return condition.astype(F32)

    def swap(x, bit):
        return lax.ppermute(x, "seq", [(i, i ^ bit) for i in range(n_seq)])

    by_slot = (width // DH) % plane == 0
    steps = plane if by_slot else 1
    states = block_states(meta, key, value, doc_count, steps)
    if not by_slot:
        states = states.reshape(plane, width // plane, DH)[jnp.arange(plane, dtype=jnp.int32) ^ member]
    slots = [states[s] for s in range(plane)]

    kept = []
    bit = 1
    while bit < plane:
        mine, send = slots[0::2], slots[1::2]
        got = swap(jnp.stack(send), bit)
        got = [got[i] for i in range(len(send))]
        upper = (member & bit) != 0
        unit = block & ~(2 * bit - 1)
        joined = weigh(first_block((unit + 2 * bit) * rows - 1) < unit + bit)
        own_factor = jnp.where(upper, 1.0, joined)
        got_factor = jnp.where(upper, joined, 1.0)
        kept.append((mine, got, bit, upper, unit))
        slots = [
            (own_factor * a.astype(F32) + got_factor * b.astype(F32)).astype(BF16) for a, b in zip(mine, got)
        ]
        bit *= 2
    base = block - member
    begins = first_block(base * rows)
    carry = jnp.zeros(slots[0].shape, F32)
    for d in range(PLANES - 1, 0, -1):
        shift = d * plane
        got = lax.ppermute(slots[0], "seq", [(i, i + shift) for i in range(n_seq - shift)])
        carry = carry + weigh((base - shift + plane - 1 >= begins) & (base >= shift)) * got.astype(F32)
    carries = [carry]

    for mine, got, bit, upper, unit in reversed(kept):
        middle = unit + bit
        begins = first_block(middle * rows)
        through, joined = weigh(begins < unit), weigh(begins < middle)
        ours, theirs = [], []
        for carry, a, b in zip(carries, mine, got):
            lower_state = jnp.where(upper, b, a).astype(F32)
            after = through * carry + joined * lower_state
            ours.append(jnp.where(upper, after, carry))
            theirs.append(jnp.where(upper, carry, after).astype(BF16))
        back = swap(jnp.stack(theirs), bit)
        carries = [x for i, c in enumerate(ours) for x in (c, back[i])]
    carries = [c.astype(BF16) for c in carries]

    within = within_block(meta, query, key, value, doc_count)
    natural = jnp.stack(carries)[jnp.arange(plane, dtype=jnp.int32) ^ member].reshape(width, DH)
    normed = norm_heads(meta, query, within, natural, gain, doc_count)
    partial_sum = jnp.dot(normed, weight, preferred_element_type=F32)
    return lax.psum_scatter(partial_sum.astype(BF16), "head", scatter_dimension=1, tiled=True)


def solution(mesh):
    return jax.shard_map(
        functools.partial(body, mesh.shape["seq"], mesh.shape["head"]),
        mesh=mesh,
        in_specs=(
            P("seq", "head"),
            P("seq", "head"),
            P("seq", "head"),
            P(),
            P("head"),
            P("head", None),
        ),
        out_specs=P("seq", "head"),
        check_vma=False,
    )
```

```python
import functools

import jax
import jax.numpy as jnp
from jax import lax
from jax.experimental import pallas as pl
from jax.experimental.pallas import tpu as pltpu
from jax.sharding import PartitionSpec as P

DH = 128
PLANES = 4
F32, BF16 = jnp.float32, jnp.bfloat16
LENS = 8
VMEM_LIMIT = 16 * 1024 * 1024


def doc_start(meta, doc_count, token):
    bound = jnp.int32(0)
    start = jnp.int32(0)
    for d in range(doc_count):
        bound = bound + meta[LENS + d]
        start = jnp.where(bound <= token, bound, start)
    return start


def call(kernel, grid, in_specs, out_specs, out_shape, flops, bytes_accessed, scratch=(), vmem=VMEM_LIMIT):
    return pl.pallas_call(
        kernel,
        grid_spec=pltpu.PrefetchScalarGridSpec(
            num_scalar_prefetch=1,
            grid=grid,
            in_specs=in_specs,
            out_specs=out_specs,
            scratch_shapes=scratch,
        ),
        out_shape=out_shape,
        compiler_params=pltpu.CompilerParams(vmem_limit_bytes=vmem),
        cost_estimate=pl.CostEstimate(flops=flops, bytes_accessed=bytes_accessed, transcendentals=0),
    )


def block_states(meta, key, value, doc_count, steps):
    rows, width = key.shape
    part = width // steps

    def kernel(meta_ref, k_ref, v_ref, o_ref):
        offset = meta_ref[0] * rows
        first = doc_start(meta_ref, doc_count, offset + rows - 1) - offset
        live = lax.broadcasted_iota(jnp.int32, (rows, DH), 0) >= first
        for h in range(part // DH):
            cols = slice(h * DH, (h + 1) * DH)
            k = jnp.where(live, k_ref[:, cols], jnp.zeros((), BF16))
            s = lax.dot_general(k, v_ref[:, cols], (((0,), (0,)), ((), ())), preferred_element_type=F32)
            o_ref[0, cols, :] = s.astype(BF16)

    def slot(g, m):
        return (g ^ m[1], 0, 0) if steps > 1 else (0, 0, 0)

    return call(
        kernel,
        (steps,),
        [pl.BlockSpec((rows, part), lambda g, m: (0, g))] * 2,
        pl.BlockSpec((1, part, DH), slot),
        jax.ShapeDtypeStruct((steps, part, DH), BF16),
        2 * rows * width * DH,
        2 * 2 * rows * width,
    )(meta, key, value)


def within_block(meta, query, key, value, doc_count):
    rows, width = query.shape
    part = DH
    for heads in (4, 3, 2):
        if width % (heads * DH) == 0:
            part = heads * DH
            break
    tile = rows // 2

    def kernel(meta_ref, q_ref, k_ref, v_ref, o_ref, mask_ref):
        @pl.when(pl.program_id(0) == 0)
        def _():
            offset = meta_ref[0] * rows
            t = lax.broadcasted_iota(jnp.int32, (rows, rows), 0)
            s = lax.broadcasted_iota(jnp.int32, (rows, rows), 1)
            pos = lax.broadcasted_iota(jnp.int32, (rows, 1), 0)
            first = jnp.zeros((rows, 1), jnp.int32)
            bound = -offset
            for d in range(doc_count):
                bound = bound + meta_ref[LENS + d]
                first = jnp.where(bound <= pos, bound, first)
            mask_ref[...] = jnp.where((s <= t) & (s >= first), 1.0, 0.0).astype(BF16)

        for h in range(part // DH):
            cols = slice(h * DH, (h + 1) * DH)
            for i in range(2):
                r = slice(i * tile, (i + 1) * tile)
                seen = (i + 1) * tile
                scores = lax.dot_general(
                    q_ref[r, cols], k_ref[:seen, cols], (((1,), (1,)), ((), ())), preferred_element_type=F32
                )
                scores = scores.astype(BF16) * mask_ref[r, :seen]
                o_ref[r, cols] = jnp.dot(scores, v_ref[:seen, cols], preferred_element_type=F32)

    spec = pl.BlockSpec((rows, part), lambda g, m: (0, g))
    return call(
        kernel,
        (width // part,),
        [spec] * 3,
        spec,
        jax.ShapeDtypeStruct((rows, width), F32),
        3 * rows * rows * width,
        10 * rows * width,
        [pltpu.VMEM((rows, rows), BF16)],
    )(meta, query, key, value)


def whole(shape):
    return pl.BlockSpec(shape, lambda *_: (0,) * len(shape))


def local(kernel, meta, arrays, shapes, micros, limit=4, specs=None):
    return call(
        kernel,
        (1,),
        specs or [whole(a.shape) for a in arrays],
        [whole(s.shape) for s in shapes],
        shapes,
        int(micros * 1e9),
        1024,
        (),
        limit * 1024 * 1024,
    )(meta, *arrays)


def group(rows, part, slot):
    return pl.BlockSpec((rows, part), lambda i, m: (0, m[1] ^ slot))


def after(meta, *arrays):
    return lax.optimization_barrier((meta, *arrays))[0]


def factor(condition):
    return jnp.where(condition, 1.0, 0.0)


def split_states(meta, key, value, doc_count):
    rows, width = key.shape
    part = width // 4
    order = (1, 3, 0, 2)

    def kernel(meta_ref, *refs):
        offset = meta_ref[0] * rows
        first = doc_start(meta_ref, doc_count, offset + rows - 1) - offset
        live = lax.broadcasted_iota(jnp.int32, (rows, DH), 0) >= first
        for i in range(4):
            k_ref, v_ref, o_ref = refs[i], refs[4 + i], refs[8 + i // 2]
            for h in range(part // DH):
                cols = slice(h * DH, (h + 1) * DH)
                k = jnp.where(live, k_ref[:, cols], jnp.zeros((), BF16))
                state = lax.dot_general(
                    k, v_ref[:, cols], (((0,), (0,)), ((), ())), preferred_element_type=F32
                )
                o_ref[i % 2, cols, :] = state.astype(BF16)

    arrays, specs = [key] * 4 + [value] * 4, [group(rows, part, s) for s in order] * 2
    return local(kernel, meta, arrays, [jax.ShapeDtypeStruct((2, part, DH), BF16)] * 2, 2, 16, specs)


def seen_mask(meta_ref, rows, doc_count):
    offset = meta_ref[0] * rows
    t = lax.broadcasted_iota(jnp.int32, (rows, rows), 0)
    s = lax.broadcasted_iota(jnp.int32, (rows, rows), 1)
    pos = lax.broadcasted_iota(jnp.int32, (rows, 1), 0)
    first = jnp.zeros((rows, 1), jnp.int32)
    bound = -offset
    for d in range(doc_count):
        bound = bound + meta_ref[LENS + d]
        first = jnp.where(bound <= pos, bound, first)
    return jnp.where((s <= t) & (s >= first), 1.0, 0.0).astype(BF16)


def within_slot(meta, query, key, value, doc_count, slot, mask=None):
    rows, width = query.shape
    part = width // 4
    tile = rows // 2
    make = mask is None

    def kernel(meta_ref, q_ref, k_ref, v_ref, *rest):
        if make:
            o_ref, mask_ref = rest
            mask_ref[...] = seen_mask(meta_ref, rows, doc_count)
        else:
            mask_ref, o_ref = rest
        for h in range(part // DH):
            cols = slice(h * DH, (h + 1) * DH)
            for i in range(2):
                r = slice(i * tile, (i + 1) * tile)
                seen = (i + 1) * tile
                scores = lax.dot_general(
                    q_ref[r, cols], k_ref[:seen, cols], (((1,), (1,)), ((), ())), preferred_element_type=F32
                )
                scores = scores.astype(BF16) * mask_ref[r, :seen]
                o_ref[r, cols] = jnp.dot(scores, v_ref[:seen, cols], preferred_element_type=F32)

    shapes = [jax.ShapeDtypeStruct((rows, part), F32)]
    arrays, specs = [query, key, value], [group(rows, part, slot)] * 3
    if make:
        shapes = shapes + [jax.ShapeDtypeStruct((rows, rows), BF16)]
        return local(kernel, meta, arrays, shapes, 2, 16, specs)
    return local(kernel, meta, [*arrays, mask], shapes, 2, 16, [*specs, whole(mask.shape)])[0]


def small(kernel, meta, arrays, shape, count):
    return local(kernel, meta, arrays, [jax.ShapeDtypeStruct(shape, BF16)] * count, 0.6)


def join_core(meta, keep, got, rows, doc_count):
    def kernel(meta_ref, keep_ref, got_ref, a_ref, b_ref):
        low = meta_ref[0] & -2
        joined = factor(doc_start(meta_ref, doc_count, (low + 2) * rows - 1) < (low + 1) * rows)
        upper = (meta_ref[1] & 1) != 0
        own, other = jnp.where(upper, 1.0, joined), jnp.where(upper, joined, 1.0)
        for i, o_ref in enumerate((a_ref, b_ref)):
            o_ref[...] = (own * keep_ref[i].astype(F32) + other * got_ref[i].astype(F32)).astype(BF16)

    return small(kernel, meta, (keep, got), keep.shape[1:], 2)


def join_chips(meta, mine, got, rows, doc_count):
    def kernel(meta_ref, a_ref, b_ref, o_ref):
        low = meta_ref[0] & -4
        joined = factor(doc_start(meta_ref, doc_count, (low + 4) * rows - 1) < (low + 2) * rows)
        upper = (meta_ref[1] & 2) != 0
        own, other = jnp.where(upper, 1.0, joined), jnp.where(upper, joined, 1.0)
        o_ref[...] = (own * a_ref[...].astype(F32) + other * b_ref[...].astype(F32)).astype(BF16)

    return small(kernel, meta, (mine, got), mine.shape, 1)[0]


def join_planes(meta, plane_sum, previous, rows, doc_count):
    def kernel(meta_ref, a_ref, b_ref, o_ref):
        low = meta_ref[0] & -4
        joined = factor(doc_start(meta_ref, doc_count, (low + 4) * rows - 1) < low * rows)
        o_ref[...] = (a_ref[...].astype(F32) + joined * b_ref[...].astype(F32)).astype(BF16)

    return small(kernel, meta, (plane_sum, previous), plane_sum.shape, 1)[0]


def carry_in_chip(meta_ref, chip, keep, got, rows, doc_count):
    low = meta_ref[0] & -2
    begins = doc_start(meta_ref, doc_count, (low + 1) * rows)
    through, joined = factor(begins < low * rows), factor(begins < (low + 1) * rows)
    upper = (meta_ref[1] & 1) != 0
    later = through * chip + joined * jnp.where(upper, got, keep).astype(F32)
    return jnp.where(upper, later, chip), jnp.where(upper, chip, later)


def carry_first(meta, near, far, mine, got, keep, core_got, rows, doc_count):
    def kernel(meta_ref, near_ref, far_ref, a_ref, b_ref, keep_ref, got_ref, o_ref, core_ref, chip_ref):
        low = meta_ref[0] & -4
        begins = doc_start(meta_ref, doc_count, low * rows)
        first = factor(begins < low * rows) * near_ref[...].astype(F32)
        first = first + factor(begins < (low - 4) * rows) * far_ref[...].astype(F32)
        begins = doc_start(meta_ref, doc_count, (low + 2) * rows)
        through, joined = factor(begins < low * rows), factor(begins < (low + 2) * rows)
        upper = (meta_ref[1] & 2) != 0
        later = through * first + joined * jnp.where(upper, b_ref[...], a_ref[...]).astype(F32)
        chip_ref[...] = jnp.where(upper, first, later).astype(BF16)
        chip = jnp.where(upper, later, first)
        ours, theirs = carry_in_chip(meta_ref, chip, keep_ref[0], got_ref[0], rows, doc_count)
        o_ref[...] = ours.astype(BF16)
        core_ref[...] = theirs.astype(BF16)

    return small(kernel, meta, (near, far, mine, got, keep, core_got), mine.shape, 3)


def carry_second(meta, chip, keep, core_got, rows, doc_count):
    def kernel(meta_ref, chip_ref, keep_ref, got_ref, o_ref, core_ref):
        ours, theirs = carry_in_chip(
            meta_ref, chip_ref[...].astype(F32), keep_ref[1], got_ref[1], rows, doc_count
        )
        o_ref[...] = ours.astype(BF16)
        core_ref[...] = theirs.astype(BF16)

    return small(kernel, meta, (chip, keep, core_got), chip.shape, 2)


def norm_heads(meta, query, withins, carries, gain, doc_count, slots=None):
    rows = query.shape[0]
    part = carries[0].shape[0]
    count = len(carries)

    def kernel(meta_ref, *refs):
        offset = meta_ref[0] * rows
        begins = doc_start(meta_ref, doc_count, offset)
        bound = jnp.int32(0)
        end = jnp.int32(0)
        for d in range(doc_count):
            previous = bound
            bound = bound + meta_ref[LENS + d]
            end = jnp.where(previous <= offset, bound, end)
        stop = jnp.where(begins < offset, end - offset, 0)
        cross = lax.broadcasted_iota(jnp.int32, (rows, DH), 0) < stop
        o_ref = refs[-1]
        for n in range(count):
            q_ref, w_ref, c_ref, g_ref = refs[4 * n : 4 * n + 4]
            for h in range(part // DH):
                cols = slice(h * DH, (h + 1) * DH)
                term = jnp.dot(q_ref[:, cols], c_ref[cols, :], preferred_element_type=F32)
                mixture = w_ref[:, cols] + jnp.where(cross, term, 0.0)
                mean = jnp.mean(mixture * mixture, axis=-1, keepdims=True)
                o_ref[:, n * part + h * DH : n * part + (h + 1) * DH] = (
                    mixture * lax.rsqrt(mean + 1e-06) * g_ref[:, cols]
                ).astype(BF16)

    gain = gain.reshape(1, -1)
    arrays, specs = [], []
    for n in range(count):
        arrays += [query, withins[n], carries[n], gain]
        wide = [whole((rows, part)), whole((1, part))] if slots is None else [
            group(rows, part, slots[n]), group(1, part, slots[n])
        ]
        specs += [wide[0], whole((rows, part)), whole((part, DH)), wide[1]]
    shapes = [jax.ShapeDtypeStruct((rows, part * count), BF16)]
    return local(kernel, meta, arrays, shapes, count, 16, specs)[0]


TILES = 4


def project_own(meta, pieces, weight, columns):
    rows = pieces[0].shape[0]
    part = weight.shape[0] // 4
    tile = columns // TILES
    count = len(pieces)

    def kernel(meta_ref, *refs):
        ns, ws, o_ref = refs[:count], refs[count:-1], refs[-1]
        n = jnp.concatenate([r[...] for r in ns], axis=1)
        w = jnp.concatenate([r[...] for r in ws], axis=0)
        o_ref[...] = jnp.dot(n, w, preferred_element_type=F32)

    return call(
        kernel,
        (TILES,),
        [whole(p.shape) for p in pieces]
        + [pl.BlockSpec((part, tile), lambda n, m, s=s: (m[1] ^ s, m[2] * TILES + n)) for s in range(4)],
        pl.BlockSpec((rows, tile), lambda n, m: (0, n)),
        jax.ShapeDtypeStruct((rows, columns), F32),
        10**6,
        1024,
    )(meta, *pieces, *[weight] * 4)


def project_more(meta, total, pieces, weights, dtype):
    rows, columns = total.shape
    tile = columns // TILES
    count = len(pieces)
    flat, specs, places = [], [], []
    for ws in weights:
        start = 0
        for w in ws:
            first, last = start // tile, (start + w.shape[1] - 1) // tile
            places.append((first, last))
            flat.append(w)
            specs.append(
                pl.BlockSpec(
                    (w.shape[0], min(tile, w.shape[1])),
                    lambda n, m, first=first, last=last: (0, jnp.clip(n - first, 0, last - first)),
                )
            )
            start += w.shape[1]
    per_slot = [len(ws) for ws in weights]

    def kernel(meta_ref, t_ref, *refs):
        ns, ws, o_ref = refs[:count], refs[count:-1], refs[-1]
        n = jnp.concatenate([r[...] for r in ns], axis=1)
        for c in range(TILES):

            @pl.when(pl.program_id(0) == c)
            def _():
                rows_of, at = [], 0
                for size in per_slot:
                    here = range(at, at + size)
                    held = [ws[i][...] for i in here if places[i][0] <= c <= places[i][1]]
                    rows_of.append(jnp.concatenate(held, axis=1))
                    at += size
                w = jnp.concatenate(rows_of, axis=0)
                o_ref[...] = (t_ref[...] + jnp.dot(n, w, preferred_element_type=F32)).astype(dtype)

    out_spec = pl.BlockSpec((rows, tile), lambda n, m: (0, n ^ (m[3] * (TILES // 2))))
    return call(
        kernel,
        (TILES,),
        [out_spec] + [whole(p.shape) for p in pieces] + specs,
        out_spec,
        jax.ShapeDtypeStruct((rows, columns), dtype),
        10**6,
        1024,
    )(meta, total, *pieces, *flat)


def pair_body(n_seq, query, key, value, doc_lengths, gain, weight):
    rows, width = query.shape
    docs = doc_lengths.shape[0]
    plane, part = 4, width // 4
    columns = weight.shape[1] // 2
    half = columns // 2
    block = lax.axis_index("seq").astype(jnp.int32)
    group = lax.axis_index("head").astype(jnp.int32)
    member = block % plane
    side = (block // plane) % 2
    meta = jnp.concatenate([
        jnp.stack([block, member, group, side]), jnp.zeros((LENS - 4,), jnp.int32), doc_lengths
    ])

    def swap(x, bit):
        return lax.ppermute(x, "seq", [(i, i ^ bit) for i in range(n_seq)])

    def shift(x, count):
        return lax.ppermute(x, "seq", [(i, i + count) for i in range(n_seq - count)])

    def flip(x):
        return lax.ppermute(x, "head", [(0, 1), (1, 0)])

    def behind(x, *arrays):
        return lax.optimization_barrier((x, *arrays))[0]

    quarter = half // 2
    sent = [(side * half, half), ((1 - side) * half, quarter)]
    sent = [
        lax.dynamic_slice(weight, (member * part, (1 - group) * columns + at), (part, size))
        for at, size in sent
    ]
    w0 = [flip(x) for x in sent]

    send, keep = split_states(after(meta, sent[0]), key, value, docs)
    core_got = swap(send, 1)
    query = behind(query, send)
    within0, mask = within_slot(after(meta, send), query, key, value, docs, 0)
    chip0, chip2 = join_core(after(meta, within0), keep, core_got, rows, docs)
    chip_got = swap(chip2, 2)
    within1 = within_slot(after(meta, chip0), query, key, value, docs, 1, mask)
    plane_sum = join_chips(after(meta, within1), chip0, chip_got, rows, docs)
    near = shift(plane_sum, plane)
    within2 = within_slot(after(meta, plane_sum), query, key, value, docs, 2, mask)
    both = join_planes(after(meta, within2), plane_sum, near, rows, docs)
    far = shift(both, 2 * plane)
    within3 = within_slot(after(meta, both), query, key, value, docs, 3, mask)
    carry0, core_carry0, chip_carry = carry_first(
        after(meta, within3), near, far, chip0, chip_got, keep, core_got, rows, docs
    )
    carry1 = swap(core_carry0, 1)
    chip_carry2 = swap(chip_carry, 2)

    def norm(slots, withins, carries):
        return norm_heads(meta, query, withins, carries, gain, docs, slots)

    normed0 = norm((0,), [within0], [carry0])
    far0 = flip(normed0)
    normed1 = norm((1,), [within1], [carry1])
    far1 = flip(normed1)
    carry2, core_carry2 = carry_second(meta, chip_carry2, keep, core_got, rows, docs)
    carry3 = swap(core_carry2, 1)
    normed2 = norm((2, 3), [within2, within3], [carry2, carry3])
    far2 = flip(normed2)

    first, second = lax.optimization_barrier((*w0, chip_carry2, normed0, normed1))[:2]
    total = project_own(after(meta, far0), [normed0, normed1, normed2], weight, columns)
    w2 = [swap(first, 2), swap(second, 2)]
    w0.append(swap(first[:, quarter:], plane))
    w2.append(swap(behind(w2[0], total)[:, quarter:], plane))

    def cut(w, width):
        return [w[:, at : at + width] for at in range(0, w.shape[1], width)]

    w1 = [swap(x, 1) for w in w0 for x in cut(w, quarter)]
    w3 = [swap(x, 1) for w, width in zip(w2, (quarter, quarter // 2, quarter // 2)) for x in cut(w, width)]

    total = project_more(meta, total, [far0, far1], [w0, w1], F32)
    return project_more(meta, total, [far2], [w2, w3], BF16)


def body(n_seq, n_head, query, key, value, doc_lengths, gain, weight):
    rows, width = query.shape
    doc_count = doc_lengths.shape[0]
    plane = n_seq // PLANES
    if n_head == 2 and plane == 4 and width % (4 * DH) == 0:
        return pair_body(n_seq, query, key, value, doc_lengths, gain, weight)
    block = lax.axis_index("seq").astype(jnp.int32)
    group = lax.axis_index("head").astype(jnp.int32)
    member = block % plane
    meta = jnp.concatenate([
        jnp.stack([block, member, group]), jnp.zeros((LENS - 3,), jnp.int32), doc_lengths
    ])

    bounds = jnp.cumsum(doc_lengths)

    def first_block(token):
        starts = jnp.max(jnp.where(bounds <= token, bounds, 0))
        return starts // rows

    def weigh(condition):
        return condition.astype(F32)

    def swap(x, bit):
        return lax.ppermute(x, "seq", [(i, i ^ bit) for i in range(n_seq)])

    by_slot = (width // DH) % plane == 0
    steps = plane if by_slot else 1
    states = block_states(meta, key, value, doc_count, steps)
    if not by_slot:
        states = states.reshape(plane, width // plane, DH)[jnp.arange(plane, dtype=jnp.int32) ^ member]
    slots = [states[s] for s in range(plane)]

    kept = []
    bit = 1
    while bit < plane:
        mine, send = slots[0::2], slots[1::2]
        got = swap(jnp.stack(send), bit)
        got = [got[i] for i in range(len(send))]
        upper = (member & bit) != 0
        unit = block & ~(2 * bit - 1)
        joined = weigh(first_block((unit + 2 * bit) * rows - 1) < unit + bit)
        own_factor = jnp.where(upper, 1.0, joined)
        got_factor = jnp.where(upper, joined, 1.0)
        kept.append((mine, got, bit, upper, unit))
        slots = [
            (own_factor * a.astype(F32) + got_factor * b.astype(F32)).astype(BF16) for a, b in zip(mine, got)
        ]
        bit *= 2
    base = block - member
    begins = first_block(base * rows)
    carry = jnp.zeros(slots[0].shape, F32)
    for d in range(PLANES - 1, 0, -1):
        shift = d * plane
        got = lax.ppermute(slots[0], "seq", [(i, i + shift) for i in range(n_seq - shift)])
        carry = carry + weigh((base - shift + plane - 1 >= begins) & (base >= shift)) * got.astype(F32)
    carries = [carry]

    for mine, got, bit, upper, unit in reversed(kept):
        middle = unit + bit
        begins = first_block(middle * rows)
        through, joined = weigh(begins < unit), weigh(begins < middle)
        ours, theirs = [], []
        for carry, a, b in zip(carries, mine, got):
            lower_state = jnp.where(upper, b, a).astype(F32)
            after = through * carry + joined * lower_state
            ours.append(jnp.where(upper, after, carry))
            theirs.append(jnp.where(upper, carry, after).astype(BF16))
        back = swap(jnp.stack(theirs), bit)
        carries = [x for i, c in enumerate(ours) for x in (c, back[i])]
    carries = [c.astype(BF16) for c in carries]

    within = within_block(meta, query, key, value, doc_count)
    natural = jnp.stack(carries)[jnp.arange(plane, dtype=jnp.int32) ^ member].reshape(width, DH)
    normed = norm_heads(meta, query, [within], [natural], gain, doc_count)
    partial_sum = jnp.dot(normed, weight, preferred_element_type=F32)
    return lax.psum_scatter(partial_sum.astype(BF16), "head", scatter_dimension=1, tiled=True)


def solution(mesh):
    return jax.shard_map(
        functools.partial(body, mesh.shape["seq"], mesh.shape["head"]),
        mesh=mesh,
        in_specs=(
            P("seq", "head"),
            P("seq", "head"),
            P("seq", "head"),
            P(),
            P("head"),
            P("head", None),
        ),
        out_specs=P("seq", "head"),
        check_vma=False,
    )
```

```python
import functools

import jax
import jax.numpy as jnp
from jax import lax
from jax.experimental import pallas as pl
from jax.experimental.pallas import tpu as pltpu
from jax.sharding import PartitionSpec as P

DH = 128
PLANES = 4
F32, BF16 = jnp.float32, jnp.bfloat16
LENS = 8
VMEM_LIMIT = 16 * 1024 * 1024


def doc_start(meta, doc_count, token):
    bound = jnp.int32(0)
    start = jnp.int32(0)
    for d in range(doc_count):
        bound = bound + meta[LENS + d]
        start = jnp.where(bound <= token, bound, start)
    return start


def call(kernel, grid, in_specs, out_specs, out_shape, flops, bytes_accessed, scratch=(), vmem=VMEM_LIMIT):
    return pl.pallas_call(
        kernel,
        grid_spec=pltpu.PrefetchScalarGridSpec(
            num_scalar_prefetch=1,
            grid=grid,
            in_specs=in_specs,
            out_specs=out_specs,
            scratch_shapes=scratch,
        ),
        out_shape=out_shape,
        compiler_params=pltpu.CompilerParams(vmem_limit_bytes=vmem),
        cost_estimate=pl.CostEstimate(flops=flops, bytes_accessed=bytes_accessed, transcendentals=0),
    )


def block_states(meta, key, value, doc_count, steps):
    rows, width = key.shape
    part = width // steps

    def kernel(meta_ref, k_ref, v_ref, o_ref):
        offset = meta_ref[0] * rows
        first = doc_start(meta_ref, doc_count, offset + rows - 1) - offset
        live = lax.broadcasted_iota(jnp.int32, (rows, DH), 0) >= first
        for h in range(part // DH):
            cols = slice(h * DH, (h + 1) * DH)
            k = jnp.where(live, k_ref[:, cols], jnp.zeros((), BF16))
            s = lax.dot_general(k, v_ref[:, cols], (((0,), (0,)), ((), ())), preferred_element_type=F32)
            o_ref[0, cols, :] = s.astype(BF16)

    def slot(g, m):
        return (g ^ m[1], 0, 0) if steps > 1 else (0, 0, 0)

    return call(
        kernel,
        (steps,),
        [pl.BlockSpec((rows, part), lambda g, m: (0, g))] * 2,
        pl.BlockSpec((1, part, DH), slot),
        jax.ShapeDtypeStruct((steps, part, DH), BF16),
        2 * rows * width * DH,
        2 * 2 * rows * width,
    )(meta, key, value)


def within_block(meta, query, key, value, doc_count):
    rows, width = query.shape
    part = DH
    for heads in (4, 3, 2):
        if width % (heads * DH) == 0:
            part = heads * DH
            break
    tile = rows // 2

    def kernel(meta_ref, q_ref, k_ref, v_ref, o_ref, mask_ref):
        @pl.when(pl.program_id(0) == 0)
        def _():
            offset = meta_ref[0] * rows
            t = lax.broadcasted_iota(jnp.int32, (rows, rows), 0)
            s = lax.broadcasted_iota(jnp.int32, (rows, rows), 1)
            pos = lax.broadcasted_iota(jnp.int32, (rows, 1), 0)
            first = jnp.zeros((rows, 1), jnp.int32)
            bound = -offset
            for d in range(doc_count):
                bound = bound + meta_ref[LENS + d]
                first = jnp.where(bound <= pos, bound, first)
            mask_ref[...] = jnp.where((s <= t) & (s >= first), 1.0, 0.0).astype(BF16)

        for h in range(part // DH):
            cols = slice(h * DH, (h + 1) * DH)
            for i in range(2):
                r = slice(i * tile, (i + 1) * tile)
                seen = (i + 1) * tile
                scores = lax.dot_general(
                    q_ref[r, cols], k_ref[:seen, cols], (((1,), (1,)), ((), ())), preferred_element_type=F32
                )
                scores = scores.astype(BF16) * mask_ref[r, :seen]
                o_ref[r, cols] = jnp.dot(scores, v_ref[:seen, cols], preferred_element_type=F32)

    spec = pl.BlockSpec((rows, part), lambda g, m: (0, g))
    return call(
        kernel,
        (width // part,),
        [spec] * 3,
        spec,
        jax.ShapeDtypeStruct((rows, width), F32),
        3 * rows * rows * width,
        10 * rows * width,
        [pltpu.VMEM((rows, rows), BF16)],
    )(meta, query, key, value)


def whole(shape):
    return pl.BlockSpec(shape, lambda *_: (0,) * len(shape))


def local(kernel, meta, arrays, shapes, micros, limit=4, specs=None):
    return call(
        kernel,
        (1,),
        specs or [whole(a.shape) for a in arrays],
        [whole(s.shape) for s in shapes],
        shapes,
        int(micros * 1e9),
        1024,
        (),
        limit * 1024 * 1024,
    )(meta, *arrays)


def group(rows, part, slot):
    return pl.BlockSpec((rows, part), lambda i, m: (0, m[1] ^ slot))


def after(meta, *arrays):
    return lax.optimization_barrier((meta, *arrays))[0]


def factor(condition):
    return jnp.where(condition, 1.0, 0.0)


def split_states(meta, key, value, doc_count):
    rows, width = key.shape
    part = width // 4
    order = (1, 3, 0, 2)

    def kernel(meta_ref, *refs):
        offset = meta_ref[0] * rows
        first = doc_start(meta_ref, doc_count, offset + rows - 1) - offset
        live = lax.broadcasted_iota(jnp.int32, (rows, DH), 0) >= first
        for i in range(4):
            k_ref, v_ref, o_ref = refs[i], refs[4 + i], refs[8 + i // 2]
            for h in range(part // DH):
                cols = slice(h * DH, (h + 1) * DH)
                k = jnp.where(live, k_ref[:, cols], jnp.zeros((), BF16))
                state = lax.dot_general(
                    k, v_ref[:, cols], (((0,), (0,)), ((), ())), preferred_element_type=F32
                )
                o_ref[i % 2, cols, :] = state.astype(BF16)

    arrays, specs = [key] * 4 + [value] * 4, [group(rows, part, s) for s in order] * 2
    return local(kernel, meta, arrays, [jax.ShapeDtypeStruct((2, part, DH), BF16)] * 2, 2, 10, specs)


def seen_mask(meta_ref, rows, doc_count):
    offset = meta_ref[0] * rows
    t = lax.broadcasted_iota(jnp.int32, (rows, rows), 0)
    s = lax.broadcasted_iota(jnp.int32, (rows, rows), 1)
    pos = lax.broadcasted_iota(jnp.int32, (rows, 1), 0)
    first = jnp.zeros((rows, 1), jnp.int32)
    bound = -offset
    for d in range(doc_count):
        bound = bound + meta_ref[LENS + d]
        first = jnp.where(bound <= pos, bound, first)
    return jnp.where((s <= t) & (s >= first), 1.0, 0.0).astype(BF16)


def within_slot(meta, query, key, value, doc_count, slot, mask=None):
    rows, width = query.shape
    part = width // 4
    tile = rows // 2
    make = mask is None

    def kernel(meta_ref, q_ref, k_ref, v_ref, *rest):
        if make:
            o_ref, mask_ref = rest
            mask_ref[...] = seen_mask(meta_ref, rows, doc_count)
        else:
            mask_ref, o_ref = rest
        for h in range(part // DH):
            cols = slice(h * DH, (h + 1) * DH)
            for i in range(2):
                r = slice(i * tile, (i + 1) * tile)
                seen = (i + 1) * tile
                scores = lax.dot_general(
                    q_ref[r, cols], k_ref[:seen, cols], (((1,), (1,)), ((), ())), preferred_element_type=F32
                )
                scores = scores.astype(BF16) * mask_ref[r, :seen]
                o_ref[r, cols] = jnp.dot(scores, v_ref[:seen, cols], preferred_element_type=F32)

    shapes = [jax.ShapeDtypeStruct((rows, part), F32)]
    arrays, specs = [query, key, value], [group(rows, part, slot)] * 3
    if make:
        shapes = shapes + [jax.ShapeDtypeStruct((rows, rows), BF16)]
        return local(kernel, meta, arrays, shapes, 2, 10, specs)
    return local(kernel, meta, [*arrays, mask], shapes, 2, 10, [*specs, whole(mask.shape)])[0]


def small(kernel, meta, arrays, shape, count):
    return local(kernel, meta, arrays, [jax.ShapeDtypeStruct(shape, BF16)] * count, 0.6)


def join_core(meta, keep, got, rows, doc_count):
    def kernel(meta_ref, keep_ref, got_ref, a_ref, b_ref):
        low = meta_ref[0] & -2
        joined = factor(doc_start(meta_ref, doc_count, (low + 2) * rows - 1) < (low + 1) * rows)
        upper = (meta_ref[1] & 1) != 0
        own, other = jnp.where(upper, 1.0, joined), jnp.where(upper, joined, 1.0)
        for i, o_ref in enumerate((a_ref, b_ref)):
            o_ref[...] = (own * keep_ref[i].astype(F32) + other * got_ref[i].astype(F32)).astype(BF16)

    return small(kernel, meta, (keep, got), keep.shape[1:], 2)


def join_chips(meta, mine, got, rows, doc_count):
    def kernel(meta_ref, a_ref, b_ref, o_ref):
        low = meta_ref[0] & -4
        joined = factor(doc_start(meta_ref, doc_count, (low + 4) * rows - 1) < (low + 2) * rows)
        upper = (meta_ref[1] & 2) != 0
        own, other = jnp.where(upper, 1.0, joined), jnp.where(upper, joined, 1.0)
        o_ref[...] = (own * a_ref[...].astype(F32) + other * b_ref[...].astype(F32)).astype(BF16)

    return small(kernel, meta, (mine, got), mine.shape, 1)[0]


def join_planes(meta, plane_sum, previous, rows, doc_count):
    def kernel(meta_ref, a_ref, b_ref, o_ref):
        low = meta_ref[0] & -4
        joined = factor(doc_start(meta_ref, doc_count, (low + 4) * rows - 1) < low * rows)
        o_ref[...] = (a_ref[...].astype(F32) + joined * b_ref[...].astype(F32)).astype(BF16)

    return small(kernel, meta, (plane_sum, previous), plane_sum.shape, 1)[0]


def carry_in_chip(meta_ref, chip, keep, got, rows, doc_count):
    low = meta_ref[0] & -2
    begins = doc_start(meta_ref, doc_count, (low + 1) * rows)
    through, joined = factor(begins < low * rows), factor(begins < (low + 1) * rows)
    upper = (meta_ref[1] & 1) != 0
    later = through * chip + joined * jnp.where(upper, got, keep).astype(F32)
    return jnp.where(upper, later, chip), jnp.where(upper, chip, later)


def carry_first(meta, near, far, mine, got, keep, core_got, rows, doc_count):
    def kernel(meta_ref, near_ref, far_ref, a_ref, b_ref, keep_ref, got_ref, o_ref, core_ref, chip_ref):
        low = meta_ref[0] & -4
        begins = doc_start(meta_ref, doc_count, low * rows)
        first = factor(begins < low * rows) * near_ref[...].astype(F32)
        first = first + factor(begins < (low - 4) * rows) * far_ref[...].astype(F32)
        begins = doc_start(meta_ref, doc_count, (low + 2) * rows)
        through, joined = factor(begins < low * rows), factor(begins < (low + 2) * rows)
        upper = (meta_ref[1] & 2) != 0
        later = through * first + joined * jnp.where(upper, b_ref[...], a_ref[...]).astype(F32)
        chip_ref[...] = jnp.where(upper, first, later).astype(BF16)
        chip = jnp.where(upper, later, first)
        ours, theirs = carry_in_chip(meta_ref, chip, keep_ref[0], got_ref[0], rows, doc_count)
        o_ref[...] = ours.astype(BF16)
        core_ref[...] = theirs.astype(BF16)

    return small(kernel, meta, (near, far, mine, got, keep, core_got), mine.shape, 3)


def carry_second(meta, chip, keep, core_got, rows, doc_count):
    def kernel(meta_ref, chip_ref, keep_ref, got_ref, o_ref, core_ref):
        ours, theirs = carry_in_chip(
            meta_ref, chip_ref[...].astype(F32), keep_ref[1], got_ref[1], rows, doc_count
        )
        o_ref[...] = ours.astype(BF16)
        core_ref[...] = theirs.astype(BF16)

    return small(kernel, meta, (chip, keep, core_got), chip.shape, 2)


def norm_heads(meta, query, withins, carries, gain, doc_count, slots=None):
    rows = query.shape[0]
    part = carries[0].shape[0]
    count = len(carries)

    def kernel(meta_ref, *refs):
        offset = meta_ref[0] * rows
        begins = doc_start(meta_ref, doc_count, offset)
        bound = jnp.int32(0)
        end = jnp.int32(0)
        for d in range(doc_count):
            previous = bound
            bound = bound + meta_ref[LENS + d]
            end = jnp.where(previous <= offset, bound, end)
        stop = jnp.where(begins < offset, end - offset, 0)
        cross = lax.broadcasted_iota(jnp.int32, (rows, DH), 0) < stop
        o_ref = refs[-1]
        for n in range(count):
            q_ref, w_ref, c_ref, g_ref = refs[4 * n : 4 * n + 4]
            for h in range(part // DH):
                cols = slice(h * DH, (h + 1) * DH)
                term = jnp.dot(q_ref[:, cols], c_ref[cols, :], preferred_element_type=F32)
                mixture = w_ref[:, cols] + jnp.where(cross, term, 0.0)
                mean = jnp.mean(mixture * mixture, axis=-1, keepdims=True)
                o_ref[:, n * part + h * DH : n * part + (h + 1) * DH] = (
                    mixture * lax.rsqrt(mean + 1e-06) * g_ref[:, cols]
                ).astype(BF16)

    gain = gain.reshape(1, -1)
    arrays, specs = [], []
    for n in range(count):
        arrays += [query, withins[n], carries[n], gain]
        wide = [whole((rows, part)), whole((1, part))] if slots is None else [
            group(rows, part, slots[n]), group(1, part, slots[n])
        ]
        specs += [wide[0], whole((rows, part)), whole((part, DH)), wide[1]]
    shapes = [jax.ShapeDtypeStruct((rows, part * count), BF16)]
    return local(kernel, meta, arrays, shapes, count, 10, specs)[0]


TILES = 4


def project_own(meta, pieces, weight, columns):
    rows = pieces[0].shape[0]
    part = weight.shape[0] // 4
    tile = columns // TILES
    count = len(pieces)

    def kernel(meta_ref, *refs):
        ns, ws, o_ref = refs[:count], refs[count:-1], refs[-1]
        n = jnp.concatenate([r[...] for r in ns], axis=1)
        w = jnp.concatenate([r[...] for r in ws], axis=0)
        o_ref[...] = jnp.dot(n, w, preferred_element_type=F32)

    return call(
        kernel,
        (TILES,),
        [whole(p.shape) for p in pieces]
        + [pl.BlockSpec((part, tile), lambda n, m, s=s: (m[1] ^ s, m[2] * TILES + n)) for s in range(4)],
        pl.BlockSpec((rows, tile), lambda n, m: (0, n)),
        jax.ShapeDtypeStruct((rows, columns), F32),
        10**6,
        1024,
    )(meta, *pieces, *[weight] * 4)


def project_more(meta, total, pieces, weights, dtype):
    rows, columns = total.shape
    tile = columns // TILES
    count = len(pieces)
    flat, specs, places = [], [], []
    for ws in weights:
        start = 0
        for w in ws:
            first, last = start // tile, (start + w.shape[1] - 1) // tile
            places.append((first, last))
            flat.append(w)
            specs.append(
                pl.BlockSpec(
                    (w.shape[0], min(tile, w.shape[1])),
                    lambda n, m, first=first, last=last: (0, jnp.clip(n - first, 0, last - first)),
                )
            )
            start += w.shape[1]
    per_slot = [len(ws) for ws in weights]

    def kernel(meta_ref, t_ref, *refs):
        ns, ws, o_ref = refs[:count], refs[count:-1], refs[-1]
        n = jnp.concatenate([r[...] for r in ns], axis=1)
        for c in range(TILES):

            @pl.when(pl.program_id(0) == c)
            def _():
                rows_of, at = [], 0
                for size in per_slot:
                    here = range(at, at + size)
                    held = [ws[i][...] for i in here if places[i][0] <= c <= places[i][1]]
                    rows_of.append(jnp.concatenate(held, axis=1))
                    at += size
                w = jnp.concatenate(rows_of, axis=0)
                o_ref[...] = (t_ref[...] + jnp.dot(n, w, preferred_element_type=F32)).astype(dtype)

    out_spec = pl.BlockSpec((rows, tile), lambda n, m: (0, n ^ (m[3] * (TILES // 2))))
    return call(
        kernel,
        (TILES,),
        [out_spec] + [whole(p.shape) for p in pieces] + specs,
        out_spec,
        jax.ShapeDtypeStruct((rows, columns), dtype),
        10**6,
        1024,
    )(meta, total, *pieces, *flat)


def pair_body(n_seq, query, key, value, doc_lengths, gain, weight):
    rows, width = query.shape
    docs = doc_lengths.shape[0]
    plane, part = 4, width // 4
    columns = weight.shape[1] // 2
    half = columns // 2
    block = lax.axis_index("seq").astype(jnp.int32)
    group = lax.axis_index("head").astype(jnp.int32)
    member = block % plane
    side = (block // plane) % 2
    meta = jnp.concatenate([
        jnp.stack([block, member, group, side]), jnp.zeros((LENS - 4,), jnp.int32), doc_lengths
    ])

    def swap(x, bit):
        return lax.ppermute(x, "seq", [(i, i ^ bit) for i in range(n_seq)])

    def shift(x, count):
        return lax.ppermute(x, "seq", [(i, i + count) for i in range(n_seq - count)])

    def flip(x):
        return lax.ppermute(x, "head", [(0, 1), (1, 0)])

    def behind(x, *arrays):
        return lax.optimization_barrier((x, *arrays))[0]

    quarter = half // 2
    sent = [(side * half, half), ((1 - side) * half, quarter)]
    sent = [
        lax.dynamic_slice(weight, (member * part, (1 - group) * columns + at), (part, size))
        for at, size in sent
    ]
    w0 = [flip(x) for x in sent]

    send, keep = split_states(after(meta, *sent), key, value, docs)
    core_got = swap(send, 1)
    query = behind(query, send)
    within0, mask = within_slot(after(meta, send), query, key, value, docs, 0)
    chip0, chip2 = join_core(after(meta, within0), keep, core_got, rows, docs)
    chip_got = swap(chip2, 2)
    within1 = within_slot(after(meta, chip0), query, key, value, docs, 1, mask)
    plane_sum = join_chips(after(meta, within1), chip0, chip_got, rows, docs)
    near = shift(plane_sum, plane)
    within2 = within_slot(after(meta, plane_sum), query, key, value, docs, 2, mask)
    both = join_planes(after(meta, within2), plane_sum, near, rows, docs)
    far = shift(both, 2 * plane)
    w2 = [swap(behind(w0[0], both), 2)]
    within3 = within_slot(after(meta, both), query, key, value, docs, 3, mask)
    carry0, core_carry0, chip_carry = carry_first(
        after(meta, within3), near, far, chip0, chip_got, keep, core_got, rows, docs
    )
    carry1 = swap(core_carry0, 1)
    chip_carry2 = swap(chip_carry, 2)

    def norm(slots, withins, carries):
        return norm_heads(meta, query, withins, carries, gain, docs, slots)

    normed0 = norm((0,), [within0], [carry0])
    far0 = flip(normed0)
    normed1 = norm((1,), [within1], [carry1])
    far1 = flip(normed1)
    carry2, core_carry2 = carry_second(after(meta, far0, w2[0]), chip_carry2, keep, core_got, rows, docs)
    carry3 = swap(core_carry2, 1)
    normed2 = norm((2, 3), [within2, within3], [carry2, carry3])
    far2 = flip(normed2)

    total = project_own(after(meta, far1), [normed0, normed1, normed2], weight, columns)
    w0.append(swap(behind(w0[0], normed0)[:, quarter:], plane))
    w2.append(swap(behind(w0[1], chip_carry2), 2))
    w2.append(swap(behind(w2[0], carry2)[:, quarter:], plane))

    def cut(w, width):
        return [w[:, at : at + width] for at in range(0, w.shape[1], width)]

    w1 = [swap(x, 1) for w in w0 for x in cut(w, quarter)]
    w3 = [swap(x, 1) for w, width in zip(w2, (quarter, quarter // 2, quarter // 2)) for x in cut(w, width)]

    total = project_more(meta, total, [far0, far1], [w0, w1], F32)
    return project_more(meta, total, [far2], [w2, w3], BF16)


def body(n_seq, n_head, query, key, value, doc_lengths, gain, weight):
    rows, width = query.shape
    doc_count = doc_lengths.shape[0]
    plane = n_seq // PLANES
    if n_head == 2 and plane == 4 and width % (4 * DH) == 0:
        return pair_body(n_seq, query, key, value, doc_lengths, gain, weight)
    block = lax.axis_index("seq").astype(jnp.int32)
    group = lax.axis_index("head").astype(jnp.int32)
    member = block % plane
    meta = jnp.concatenate([
        jnp.stack([block, member, group]), jnp.zeros((LENS - 3,), jnp.int32), doc_lengths
    ])

    bounds = jnp.cumsum(doc_lengths)

    def first_block(token):
        starts = jnp.max(jnp.where(bounds <= token, bounds, 0))
        return starts // rows

    def weigh(condition):
        return condition.astype(F32)

    def swap(x, bit):
        return lax.ppermute(x, "seq", [(i, i ^ bit) for i in range(n_seq)])

    by_slot = (width // DH) % plane == 0
    steps = plane if by_slot else 1
    states = block_states(meta, key, value, doc_count, steps)
    if not by_slot:
        states = states.reshape(plane, width // plane, DH)[jnp.arange(plane, dtype=jnp.int32) ^ member]
    slots = [states[s] for s in range(plane)]

    kept = []
    bit = 1
    while bit < plane:
        mine, send = slots[0::2], slots[1::2]
        got = swap(jnp.stack(send), bit)
        got = [got[i] for i in range(len(send))]
        upper = (member & bit) != 0
        unit = block & ~(2 * bit - 1)
        joined = weigh(first_block((unit + 2 * bit) * rows - 1) < unit + bit)
        own_factor = jnp.where(upper, 1.0, joined)
        got_factor = jnp.where(upper, joined, 1.0)
        kept.append((mine, got, bit, upper, unit))
        slots = [
            (own_factor * a.astype(F32) + got_factor * b.astype(F32)).astype(BF16) for a, b in zip(mine, got)
        ]
        bit *= 2
    base = block - member
    begins = first_block(base * rows)
    carry = jnp.zeros(slots[0].shape, F32)
    for d in range(PLANES - 1, 0, -1):
        shift = d * plane
        got = lax.ppermute(slots[0], "seq", [(i, i + shift) for i in range(n_seq - shift)])
        carry = carry + weigh((base - shift + plane - 1 >= begins) & (base >= shift)) * got.astype(F32)
    carries = [carry]

    for mine, got, bit, upper, unit in reversed(kept):
        middle = unit + bit
        begins = first_block(middle * rows)
        through, joined = weigh(begins < unit), weigh(begins < middle)
        ours, theirs = [], []
        for carry, a, b in zip(carries, mine, got):
            lower_state = jnp.where(upper, b, a).astype(F32)
            after = through * carry + joined * lower_state
            ours.append(jnp.where(upper, after, carry))
            theirs.append(jnp.where(upper, carry, after).astype(BF16))
        back = swap(jnp.stack(theirs), bit)
        carries = [x for i, c in enumerate(ours) for x in (c, back[i])]
    carries = [c.astype(BF16) for c in carries]

    within = within_block(meta, query, key, value, doc_count)
    natural = jnp.stack(carries)[jnp.arange(plane, dtype=jnp.int32) ^ member].reshape(width, DH)
    normed = norm_heads(meta, query, [within], [natural], gain, doc_count)
    partial_sum = jnp.dot(normed, weight, preferred_element_type=F32)
    return lax.psum_scatter(partial_sum.astype(BF16), "head", scatter_dimension=1, tiled=True)


def solution(mesh):
    return jax.shard_map(
        functools.partial(body, mesh.shape["seq"], mesh.shape["head"]),
        mesh=mesh,
        in_specs=(
            P("seq", "head"),
            P("seq", "head"),
            P("seq", "head"),
            P(),
            P("head"),
            P("head", None),
        ),
        out_specs=P("seq", "head"),
        check_vma=False,
    )
```

```python
import functools

import jax
import jax.numpy as jnp
from jax import lax
from jax.experimental import pallas as pl
from jax.experimental.pallas import tpu as pltpu
from jax.sharding import PartitionSpec as P

DH = 128
PLANES = 4
F32, BF16 = jnp.float32, jnp.bfloat16
LENS = 8
VMEM_LIMIT = 16 * 1024 * 1024


def doc_start(meta, doc_count, token):
    bound = jnp.int32(0)
    start = jnp.int32(0)
    for d in range(doc_count):
        bound = bound + meta[LENS + d]
        start = jnp.where(bound <= token, bound, start)
    return start


def call(kernel, grid, in_specs, out_specs, out_shape, flops, bytes_accessed, scratch=(), vmem=VMEM_LIMIT, aliases={}):
    return pl.pallas_call(
        kernel,
        grid_spec=pltpu.PrefetchScalarGridSpec(
            num_scalar_prefetch=1,
            grid=grid,
            in_specs=in_specs,
            out_specs=out_specs,
            scratch_shapes=scratch,
        ),
        out_shape=out_shape,
        input_output_aliases=aliases,
        compiler_params=pltpu.CompilerParams(vmem_limit_bytes=vmem),
        cost_estimate=pl.CostEstimate(flops=flops, bytes_accessed=bytes_accessed, transcendentals=0),
    )


def block_states(meta, key, value, doc_count, steps):
    rows, width = key.shape
    part = width // steps

    def kernel(meta_ref, k_ref, v_ref, o_ref):
        offset = meta_ref[0] * rows
        first = doc_start(meta_ref, doc_count, offset + rows - 1) - offset
        live = lax.broadcasted_iota(jnp.int32, (rows, DH), 0) >= first
        for h in range(part // DH):
            cols = slice(h * DH, (h + 1) * DH)
            k = jnp.where(live, k_ref[:, cols], jnp.zeros((), BF16))
            s = lax.dot_general(k, v_ref[:, cols], (((0,), (0,)), ((), ())), preferred_element_type=F32)
            o_ref[0, cols, :] = s.astype(BF16)

    def slot(g, m):
        return (g ^ m[1], 0, 0) if steps > 1 else (0, 0, 0)

    return call(
        kernel,
        (steps,),
        [pl.BlockSpec((rows, part), lambda g, m: (0, g))] * 2,
        pl.BlockSpec((1, part, DH), slot),
        jax.ShapeDtypeStruct((steps, part, DH), BF16),
        2 * rows * width * DH,
        2 * 2 * rows * width,
    )(meta, key, value)


def within_block(meta, query, key, value, doc_count):
    rows, width = query.shape
    part = DH
    for heads in (4, 3, 2):
        if width % (heads * DH) == 0:
            part = heads * DH
            break
    tile = rows // 2

    def kernel(meta_ref, q_ref, k_ref, v_ref, o_ref, mask_ref):
        @pl.when(pl.program_id(0) == 0)
        def _():
            offset = meta_ref[0] * rows
            t = lax.broadcasted_iota(jnp.int32, (rows, rows), 0)
            s = lax.broadcasted_iota(jnp.int32, (rows, rows), 1)
            pos = lax.broadcasted_iota(jnp.int32, (rows, 1), 0)
            first = jnp.zeros((rows, 1), jnp.int32)
            bound = -offset
            for d in range(doc_count):
                bound = bound + meta_ref[LENS + d]
                first = jnp.where(bound <= pos, bound, first)
            mask_ref[...] = jnp.where((s <= t) & (s >= first), 1.0, 0.0).astype(BF16)

        for h in range(part // DH):
            cols = slice(h * DH, (h + 1) * DH)
            for i in range(2):
                r = slice(i * tile, (i + 1) * tile)
                seen = (i + 1) * tile
                scores = lax.dot_general(
                    q_ref[r, cols], k_ref[:seen, cols], (((1,), (1,)), ((), ())), preferred_element_type=F32
                )
                scores = scores.astype(BF16) * mask_ref[r, :seen]
                o_ref[r, cols] = jnp.dot(scores, v_ref[:seen, cols], preferred_element_type=F32)

    spec = pl.BlockSpec((rows, part), lambda g, m: (0, g))
    return call(
        kernel,
        (width // part,),
        [spec] * 3,
        spec,
        jax.ShapeDtypeStruct((rows, width), F32),
        3 * rows * rows * width,
        10 * rows * width,
        [pltpu.VMEM((rows, rows), BF16)],
    )(meta, query, key, value)


def whole(shape):
    return pl.BlockSpec(shape, lambda *_: (0,) * len(shape))


def local(kernel, meta, arrays, shapes, micros, limit=4, specs=None):
    return call(
        kernel,
        (1,),
        specs or [whole(a.shape) for a in arrays],
        [whole(s.shape) for s in shapes],
        shapes,
        int(micros * 1e9),
        1024,
        (),
        limit * 1024 * 1024,
    )(meta, *arrays)


def group(rows, part, slot):
    return pl.BlockSpec((rows, part), lambda i, m: (0, m[1] ^ slot))


def after(meta, *arrays):
    return lax.optimization_barrier((meta, *arrays))[0]


def factor(condition):
    return jnp.where(condition, 1.0, 0.0)


def slice_weights(meta, weight, columns):
    part, half = weight.shape[0] // 4, columns // 2
    shapes = [jax.ShapeDtypeStruct((part, half), BF16), jax.ShapeDtypeStruct((part, half // 2), BF16)]

    def kernel(meta_ref, w_ref, a_ref, b_ref, sems):
        rows = pl.ds(pl.multiple_of(meta_ref[1] * part, DH), part)
        base = (1 - meta_ref[2]) * columns
        starts = (base + meta_ref[3] * half, base + (1 - meta_ref[3]) * half)
        copies = []
        for n, (o_ref, start) in enumerate(zip((a_ref, b_ref), starts)):
            cols = pl.ds(pl.multiple_of(start, DH), shapes[n].shape[1])
            copies.append(pltpu.make_async_copy(w_ref.at[rows, cols], o_ref, sems.at[n]))
            copies[-1].start()
        for copy in copies:
            copy.wait()

    return call(
        kernel,
        (1,),
        [pl.BlockSpec(memory_space=pl.ANY)],
        [pl.BlockSpec(memory_space=pl.ANY)] * 2,
        shapes,
        6 * 10**9,
        1024,
        [pltpu.SemaphoreType.DMA((2,))],
        50 * 1024 * 1024,
    )(meta, weight)


def split_states(meta, key, value, doc_count):
    rows, width = key.shape
    part = width // 4
    order = (1, 3, 0, 2)

    def kernel(meta_ref, *refs):
        offset = meta_ref[0] * rows
        first = doc_start(meta_ref, doc_count, offset + rows - 1) - offset
        live = lax.broadcasted_iota(jnp.int32, (rows, DH), 0) >= first
        for i in range(4):
            k_ref, v_ref, o_ref = refs[i], refs[4 + i], refs[8 + i // 2]
            for h in range(part // DH):
                cols = slice(h * DH, (h + 1) * DH)
                k = jnp.where(live, k_ref[:, cols], jnp.zeros((), BF16))
                state = lax.dot_general(
                    k, v_ref[:, cols], (((0,), (0,)), ((), ())), preferred_element_type=F32
                )
                o_ref[i % 2, cols, :] = state.astype(BF16)

    arrays, specs = [key] * 4 + [value] * 4, [group(rows, part, s) for s in order] * 2
    return local(kernel, meta, arrays, [jax.ShapeDtypeStruct((2, part, DH), BF16)] * 2, 2, 10, specs)


def seen_mask(meta_ref, rows, doc_count):
    offset = meta_ref[0] * rows
    t = lax.broadcasted_iota(jnp.int32, (rows, rows), 0)
    s = lax.broadcasted_iota(jnp.int32, (rows, rows), 1)
    pos = lax.broadcasted_iota(jnp.int32, (rows, 1), 0)
    first = jnp.zeros((rows, 1), jnp.int32)
    bound = -offset
    for d in range(doc_count):
        bound = bound + meta_ref[LENS + d]
        first = jnp.where(bound <= pos, bound, first)
    return jnp.where((s <= t) & (s >= first), 1.0, 0.0).astype(BF16)


def within_slot(meta, query, key, value, doc_count, slot, mask=None):
    rows, width = query.shape
    part = width // 4
    tile = rows // 2
    make = mask is None

    def kernel(meta_ref, q_ref, k_ref, v_ref, *rest):
        if make:
            o_ref, mask_ref = rest
            mask_ref[...] = seen_mask(meta_ref, rows, doc_count)
        else:
            mask_ref, o_ref = rest
        for h in range(part // DH):
            cols = slice(h * DH, (h + 1) * DH)
            for i in range(2):
                r = slice(i * tile, (i + 1) * tile)
                seen = (i + 1) * tile
                scores = lax.dot_general(
                    q_ref[r, cols], k_ref[:seen, cols], (((1,), (1,)), ((), ())), preferred_element_type=F32
                )
                scores = scores.astype(BF16) * mask_ref[r, :seen]
                o_ref[r, cols] = jnp.dot(scores, v_ref[:seen, cols], preferred_element_type=F32)

    shapes = [jax.ShapeDtypeStruct((rows, part), F32)]
    arrays, specs = [query, key, value], [group(rows, part, slot)] * 3
    if make:
        shapes = shapes + [jax.ShapeDtypeStruct((rows, rows), BF16)]
        return local(kernel, meta, arrays, shapes, 2, 10, specs)
    return local(kernel, meta, [*arrays, mask], shapes, 2, 10, [*specs, whole(mask.shape)])[0]


def small(kernel, meta, arrays, shape, count):
    return local(kernel, meta, arrays, [jax.ShapeDtypeStruct(shape, BF16)] * count, 0.6)


def join_core(meta, keep, got, rows, doc_count):
    def kernel(meta_ref, keep_ref, got_ref, a_ref, b_ref):
        low = meta_ref[0] & -2
        joined = factor(doc_start(meta_ref, doc_count, (low + 2) * rows - 1) < (low + 1) * rows)
        upper = (meta_ref[1] & 1) != 0
        own, other = jnp.where(upper, 1.0, joined), jnp.where(upper, joined, 1.0)
        for i, o_ref in enumerate((a_ref, b_ref)):
            o_ref[...] = (own * keep_ref[i].astype(F32) + other * got_ref[i].astype(F32)).astype(BF16)

    return small(kernel, meta, (keep, got), keep.shape[1:], 2)


def join_chips(meta, mine, got, rows, doc_count):
    def kernel(meta_ref, a_ref, b_ref, o_ref):
        low = meta_ref[0] & -4
        joined = factor(doc_start(meta_ref, doc_count, (low + 4) * rows - 1) < (low + 2) * rows)
        upper = (meta_ref[1] & 2) != 0
        own, other = jnp.where(upper, 1.0, joined), jnp.where(upper, joined, 1.0)
        o_ref[...] = (own * a_ref[...].astype(F32) + other * b_ref[...].astype(F32)).astype(BF16)

    return small(kernel, meta, (mine, got), mine.shape, 1)[0]


def join_planes(meta, plane_sum, previous, rows, doc_count):
    def kernel(meta_ref, a_ref, b_ref, o_ref):
        low = meta_ref[0] & -4
        joined = factor(doc_start(meta_ref, doc_count, (low + 4) * rows - 1) < low * rows)
        o_ref[...] = (a_ref[...].astype(F32) + joined * b_ref[...].astype(F32)).astype(BF16)

    return small(kernel, meta, (plane_sum, previous), plane_sum.shape, 1)[0]


def carry_in_chip(meta_ref, chip, keep, got, rows, doc_count):
    low = meta_ref[0] & -2
    begins = doc_start(meta_ref, doc_count, (low + 1) * rows)
    through, joined = factor(begins < low * rows), factor(begins < (low + 1) * rows)
    upper = (meta_ref[1] & 1) != 0
    later = through * chip + joined * jnp.where(upper, got, keep).astype(F32)
    return jnp.where(upper, later, chip), jnp.where(upper, chip, later)


def carry_first(meta, near, far, mine, got, keep, core_got, rows, doc_count):
    def kernel(meta_ref, near_ref, far_ref, a_ref, b_ref, keep_ref, got_ref, o_ref, core_ref, chip_ref):
        low = meta_ref[0] & -4
        begins = doc_start(meta_ref, doc_count, low * rows)
        first = factor(begins < low * rows) * near_ref[...].astype(F32)
        first = first + factor(begins < (low - 4) * rows) * far_ref[...].astype(F32)
        begins = doc_start(meta_ref, doc_count, (low + 2) * rows)
        through, joined = factor(begins < low * rows), factor(begins < (low + 2) * rows)
        upper = (meta_ref[1] & 2) != 0
        later = through * first + joined * jnp.where(upper, b_ref[...], a_ref[...]).astype(F32)
        chip_ref[...] = jnp.where(upper, first, later).astype(BF16)
        chip = jnp.where(upper, later, first)
        ours, theirs = carry_in_chip(meta_ref, chip, keep_ref[0], got_ref[0], rows, doc_count)
        o_ref[...] = ours.astype(BF16)
        core_ref[...] = theirs.astype(BF16)

    return small(kernel, meta, (near, far, mine, got, keep, core_got), mine.shape, 3)


def carry_second(meta, chip, keep, core_got, rows, doc_count):
    def kernel(meta_ref, chip_ref, keep_ref, got_ref, o_ref, core_ref):
        ours, theirs = carry_in_chip(
            meta_ref, chip_ref[...].astype(F32), keep_ref[1], got_ref[1], rows, doc_count
        )
        o_ref[...] = ours.astype(BF16)
        core_ref[...] = theirs.astype(BF16)

    return small(kernel, meta, (chip, keep, core_got), chip.shape, 2)


def norm_heads(meta, query, withins, carries, gain, doc_count, slots=None, split=None):
    rows = query.shape[0]
    part = carries[0].shape[0]
    count = len(carries)
    heights = split or (rows,)

    def kernel(meta_ref, *refs):
        offset = meta_ref[0] * rows
        begins = doc_start(meta_ref, doc_count, offset)
        bound = jnp.int32(0)
        end = jnp.int32(0)
        for d in range(doc_count):
            previous = bound
            bound = bound + meta_ref[LENS + d]
            end = jnp.where(previous <= offset, bound, end)
        stop = jnp.where(begins < offset, end - offset, 0)
        cross = lax.broadcasted_iota(jnp.int32, (rows, DH), 0) < stop
        outs = refs[4 * count :]
        for n in range(count):
            q_ref, w_ref, c_ref, g_ref = refs[4 * n : 4 * n + 4]
            for h in range(part // DH):
                cols = slice(h * DH, (h + 1) * DH)
                term = jnp.dot(q_ref[:, cols], c_ref[cols, :], preferred_element_type=F32)
                mixture = w_ref[:, cols] + jnp.where(cross, term, 0.0)
                mean = jnp.mean(mixture * mixture, axis=-1, keepdims=True)
                normed = (mixture * lax.rsqrt(mean + 1e-06) * g_ref[:, cols]).astype(BF16)
                top = 0
                for o_ref, height in zip(outs, heights):
                    o_ref[:, n * part + h * DH : n * part + (h + 1) * DH] = normed[top : top + height]
                    top += height

    gain = gain.reshape(1, -1)
    arrays, specs = [], []
    for n in range(count):
        arrays += [query, withins[n], carries[n], gain]
        wide = [whole((rows, part)), whole((1, part))] if slots is None else [
            group(rows, part, slots[n]), group(1, part, slots[n])
        ]
        specs += [wide[0], whole((rows, part)), whole((part, DH)), wide[1]]
    shapes = [jax.ShapeDtypeStruct((height, part * count), BF16) for height in heights]
    outs = local(kernel, meta, arrays, shapes, count, 10, specs)
    return outs if split else outs[0]


TILES = 4


def project_own(meta, pieces, weight, columns):
    rows = pieces[0].shape[0]
    part = weight.shape[0] // 4
    tile = columns // TILES
    count = len(pieces)

    def kernel(meta_ref, *refs):
        ns, ws, o_ref = refs[:count], refs[count:-1], refs[-1]
        last = jnp.concatenate([r[...] for r in ns[-2:]], axis=0)
        n = jnp.concatenate([*[r[...] for r in ns[:-2]], last], axis=1)
        w = jnp.concatenate([r[...] for r in ws], axis=0)
        o_ref[...] = jnp.dot(n, w, preferred_element_type=F32)

    return call(
        kernel,
        (TILES,),
        [whole(p.shape) for p in pieces]
        + [pl.BlockSpec((part, tile), lambda n, m, s=s: (m[1] ^ s, m[2] * TILES + n)) for s in range(4)],
        pl.BlockSpec((rows, tile), lambda n, m: (0, n)),
        jax.ShapeDtypeStruct((rows, columns), F32),
        10**6,
        1024,
    )(meta, *pieces, *[weight] * 4)


def project_more(meta, total, pieces, weights, dtype, row_block=0, into=None):
    rows, columns = pieces[0].shape[0], total.shape[1]
    tile = columns // TILES
    count = len(pieces)
    flat, specs, places = [], [], []
    for ws in weights:
        start = 0
        for w in ws:
            first, last = start // tile, (start + w.shape[1] - 1) // tile
            places.append((first, last))
            flat.append(w)
            specs.append(
                pl.BlockSpec(
                    (w.shape[0], min(tile, w.shape[1])),
                    lambda n, m, first=first, last=last: (0, jnp.clip(n - first, 0, last - first)),
                )
            )
            start += w.shape[1]
    per_slot = [len(ws) for ws in weights]

    def kernel(meta_ref, t_ref, *refs):
        ns, ws, o_ref = refs[:count], refs[count : count + len(flat)], refs[-1]
        n = jnp.concatenate([r[...] for r in ns], axis=1)
        for c in range(TILES):

            @pl.when(pl.program_id(0) == c)
            def _():
                rows_of, at = [], 0
                for size in per_slot:
                    here = range(at, at + size)
                    held = [ws[i][...] for i in here if places[i][0] <= c <= places[i][1]]
                    rows_of.append(jnp.concatenate(held, axis=1))
                    at += size
                w = jnp.concatenate(rows_of, axis=0)
                o_ref[...] = (t_ref[...] + jnp.dot(n, w, preferred_element_type=F32)).astype(dtype)

    out_spec = pl.BlockSpec((rows, tile), lambda n, m: (row_block, n ^ (m[3] * (TILES // 2))))
    held = [] if into is None else [into]
    return call(
        kernel,
        (TILES,),
        [out_spec] + [whole(p.shape) for p in pieces] + specs + [pl.BlockSpec(memory_space=pl.ANY)] * len(held),
        out_spec,
        jax.ShapeDtypeStruct(total.shape, dtype),
        10**6,
        1024,
        aliases={2 + count + len(flat): 0} if held else {},
    )(meta, total, *pieces, *flat, *held)


def pair_body(n_seq, query, key, value, doc_lengths, gain, weight):
    rows, width = query.shape
    docs = doc_lengths.shape[0]
    plane, part = 4, width // 4
    columns = weight.shape[1] // 2
    half = columns // 2
    block = lax.axis_index("seq").astype(jnp.int32)
    group = lax.axis_index("head").astype(jnp.int32)
    member = block % plane
    side = (block // plane) % 2
    meta = jnp.concatenate([
        jnp.stack([block, member, group, side]), jnp.zeros((LENS - 4,), jnp.int32), doc_lengths
    ])

    def swap(x, bit):
        return lax.ppermute(x, "seq", [(i, i ^ bit) for i in range(n_seq)])

    def shift(x, count):
        return lax.ppermute(x, "seq", [(i, i + count) for i in range(n_seq - count)])

    def flip(x):
        return lax.ppermute(x, "head", [(0, 1), (1, 0)])

    def behind(x, *arrays):
        return lax.optimization_barrier((x, *arrays))[0]

    quarter = half // 2
    sent = slice_weights(meta, weight, columns)
    w0 = [flip(x) for x in sent]

    send, keep = split_states(after(meta, *sent), key, value, docs)
    core_got = swap(send, 1)
    query = behind(query, send)
    within0, mask = within_slot(after(meta, send), query, key, value, docs, 0)
    chip0, chip2 = join_core(after(meta, within0), keep, core_got, rows, docs)
    chip_got = swap(chip2, 2)
    within1 = within_slot(after(meta, chip0), query, key, value, docs, 1, mask)
    plane_sum = join_chips(after(meta, within1), chip0, chip_got, rows, docs)
    near = shift(plane_sum, plane)
    within2 = within_slot(after(meta, plane_sum), query, key, value, docs, 2, mask)
    both = join_planes(after(meta, within2), plane_sum, near, rows, docs)
    far = shift(both, 2 * plane)
    w2 = [swap(behind(w0[0], both), 2)]
    within3 = within_slot(after(meta, both), query, key, value, docs, 3, mask)
    carry0, core_carry0, chip_carry = carry_first(
        after(meta, within3), near, far, chip0, chip_got, keep, core_got, rows, docs
    )
    carry1 = swap(core_carry0, 1)
    chip_carry2 = swap(chip_carry, 2)

    def norm(slots, withins, carries, split=None):
        return norm_heads(meta, query, withins, carries, gain, docs, slots, split)

    normed0 = norm((0,), [within0], [carry0])
    far0 = flip(normed0)
    normed1 = norm((1,), [within1], [carry1])
    far1 = flip(normed1)
    carry2, core_carry2 = carry_second(after(meta, far0, w2[0]), chip_carry2, keep, core_got, rows, docs)
    carry3 = swap(core_carry2, 1)
    low = rows // 4
    normed2 = norm((2, 3), [within2, within3], [carry2, carry3], (rows - low, low))
    far2 = [flip(x) for x in normed2]

    total = project_own(after(meta, far1), [normed0, normed1, *normed2], weight, columns)
    w0.append(swap(behind(w0[0], *normed2)[:, quarter:], plane))
    w2.append(swap(behind(w0[1], chip_carry2), 2))
    w2.append(swap(behind(w2[0], *normed2)[:, quarter:], plane))

    def cut(w, width):
        return [w[:, at : at + width] for at in range(0, w.shape[1], width)]

    w1 = [swap(x, 1) for w in w0 for x in cut(w, quarter)]
    w2 = [w2[0], *lax.optimization_barrier((*w2[1:], total))[:2]]
    w3 = [swap(x, 1) for w, width in zip(w2, (quarter, quarter // 2, quarter // 2)) for x in cut(w, width)]

    total = project_more(meta, total, [far0, far1], [w0, w1], F32)
    out = project_more(meta, total, [far2[0]], [w2, w3], BF16)
    return project_more(meta, total, [far2[1]], [w2, w3], BF16, (rows - low) // low, out)


def body(n_seq, n_head, query, key, value, doc_lengths, gain, weight):
    rows, width = query.shape
    doc_count = doc_lengths.shape[0]
    plane = n_seq // PLANES
    if n_head == 2 and plane == 4 and width % (4 * DH) == 0:
        return pair_body(n_seq, query, key, value, doc_lengths, gain, weight)
    block = lax.axis_index("seq").astype(jnp.int32)
    group = lax.axis_index("head").astype(jnp.int32)
    member = block % plane
    meta = jnp.concatenate([
        jnp.stack([block, member, group]), jnp.zeros((LENS - 3,), jnp.int32), doc_lengths
    ])

    bounds = jnp.cumsum(doc_lengths)

    def first_block(token):
        starts = jnp.max(jnp.where(bounds <= token, bounds, 0))
        return starts // rows

    def weigh(condition):
        return condition.astype(F32)

    def swap(x, bit):
        return lax.ppermute(x, "seq", [(i, i ^ bit) for i in range(n_seq)])

    by_slot = (width // DH) % plane == 0
    steps = plane if by_slot else 1
    states = block_states(meta, key, value, doc_count, steps)
    if not by_slot:
        states = states.reshape(plane, width // plane, DH)[jnp.arange(plane, dtype=jnp.int32) ^ member]
    slots = [states[s] for s in range(plane)]

    kept = []
    bit = 1
    while bit < plane:
        mine, send = slots[0::2], slots[1::2]
        got = swap(jnp.stack(send), bit)
        got = [got[i] for i in range(len(send))]
        upper = (member & bit) != 0
        unit = block & ~(2 * bit - 1)
        joined = weigh(first_block((unit + 2 * bit) * rows - 1) < unit + bit)
        own_factor = jnp.where(upper, 1.0, joined)
        got_factor = jnp.where(upper, joined, 1.0)
        kept.append((mine, got, bit, upper, unit))
        slots = [
            (own_factor * a.astype(F32) + got_factor * b.astype(F32)).astype(BF16) for a, b in zip(mine, got)
        ]
        bit *= 2
    base = block - member
    begins = first_block(base * rows)
    carry = jnp.zeros(slots[0].shape, F32)
    for d in range(PLANES - 1, 0, -1):
        shift = d * plane
        got = lax.ppermute(slots[0], "seq", [(i, i + shift) for i in range(n_seq - shift)])
        carry = carry + weigh((base - shift + plane - 1 >= begins) & (base >= shift)) * got.astype(F32)
    carries = [carry]

    for mine, got, bit, upper, unit in reversed(kept):
        middle = unit + bit
        begins = first_block(middle * rows)
        through, joined = weigh(begins < unit), weigh(begins < middle)
        ours, theirs = [], []
        for carry, a, b in zip(carries, mine, got):
            lower_state = jnp.where(upper, b, a).astype(F32)
            after = through * carry + joined * lower_state
            ours.append(jnp.where(upper, after, carry))
            theirs.append(jnp.where(upper, carry, after).astype(BF16))
        back = swap(jnp.stack(theirs), bit)
        carries = [x for i, c in enumerate(ours) for x in (c, back[i])]
    carries = [c.astype(BF16) for c in carries]

    within = within_block(meta, query, key, value, doc_count)
    natural = jnp.stack(carries)[jnp.arange(plane, dtype=jnp.int32) ^ member].reshape(width, DH)
    normed = norm_heads(meta, query, [within], [natural], gain, doc_count)
    partial_sum = jnp.dot(normed, weight, preferred_element_type=F32)
    return lax.psum_scatter(partial_sum.astype(BF16), "head", scatter_dimension=1, tiled=True)


def solution(mesh):
    return jax.shard_map(
        functools.partial(body, mesh.shape["seq"], mesh.shape["head"]),
        mesh=mesh,
        in_specs=(
            P("seq", "head"),
            P("seq", "head"),
            P("seq", "head"),
            P(),
            P("head"),
            P("head", None),
        ),
        out_specs=P("seq", "head"),
        check_vma=False,
    )
```

```python
import functools

import jax
import jax.numpy as jnp
from jax import lax
from jax.experimental import pallas as pl
from jax.experimental.pallas import tpu as pltpu
from jax.sharding import PartitionSpec as P

DH = 128
PLANES = 4
F32, BF16 = jnp.float32, jnp.bfloat16
LENS = 8
VMEM_LIMIT = 24 * 1024 * 1024


def doc_start(meta, doc_count, token):
    bound = jnp.int32(0)
    start = jnp.int32(0)
    for d in range(doc_count):
        bound = bound + meta[LENS + d]
        start = jnp.where(bound <= token, bound, start)
    return start


def call(kernel, grid, in_specs, out_specs, out_shape, flops, bytes_accessed, scratch=(), vmem=VMEM_LIMIT, aliases={}):
    return pl.pallas_call(
        kernel,
        grid_spec=pltpu.PrefetchScalarGridSpec(
            num_scalar_prefetch=1,
            grid=grid,
            in_specs=in_specs,
            out_specs=out_specs,
            scratch_shapes=scratch,
        ),
        out_shape=out_shape,
        input_output_aliases=aliases,
        compiler_params=pltpu.CompilerParams(vmem_limit_bytes=vmem),
        cost_estimate=pl.CostEstimate(flops=flops, bytes_accessed=bytes_accessed, transcendentals=0),
    )


def block_states(meta, key, value, doc_count, steps):
    rows, width = key.shape
    part = width // steps

    def kernel(meta_ref, k_ref, v_ref, o_ref):
        offset = meta_ref[0] * rows
        first = doc_start(meta_ref, doc_count, offset + rows - 1) - offset
        live = lax.broadcasted_iota(jnp.int32, (rows, DH), 0) >= first
        for h in range(part // DH):
            cols = slice(h * DH, (h + 1) * DH)
            k = jnp.where(live, k_ref[:, cols], jnp.zeros((), BF16))
            s = lax.dot_general(k, v_ref[:, cols], (((0,), (0,)), ((), ())), preferred_element_type=F32)
            o_ref[0, cols, :] = s.astype(BF16)

    def slot(g, m):
        return (g ^ m[1], 0, 0) if steps > 1 else (0, 0, 0)

    return call(
        kernel,
        (steps,),
        [pl.BlockSpec((rows, part), lambda g, m: (0, g))] * 2,
        pl.BlockSpec((1, part, DH), slot),
        jax.ShapeDtypeStruct((steps, part, DH), BF16),
        2 * rows * width * DH,
        2 * 2 * rows * width,
    )(meta, key, value)


def within_block(meta, query, key, value, doc_count):
    rows, width = query.shape
    part = DH
    for heads in (4, 3, 2):
        if width % (heads * DH) == 0:
            part = heads * DH
            break
    tile = rows // 2

    def kernel(meta_ref, q_ref, k_ref, v_ref, o_ref, mask_ref):
        @pl.when(pl.program_id(0) == 0)
        def _():
            offset = meta_ref[0] * rows
            t = lax.broadcasted_iota(jnp.int32, (rows, rows), 0)
            s = lax.broadcasted_iota(jnp.int32, (rows, rows), 1)
            pos = lax.broadcasted_iota(jnp.int32, (rows, 1), 0)
            first = jnp.zeros((rows, 1), jnp.int32)
            bound = -offset
            for d in range(doc_count):
                bound = bound + meta_ref[LENS + d]
                first = jnp.where(bound <= pos, bound, first)
            mask_ref[...] = jnp.where((s <= t) & (s >= first), 1.0, 0.0).astype(BF16)

        for h in range(part // DH):
            cols = slice(h * DH, (h + 1) * DH)
            for i in range(2):
                r = slice(i * tile, (i + 1) * tile)
                seen = (i + 1) * tile
                scores = lax.dot_general(
                    q_ref[r, cols], k_ref[:seen, cols], (((1,), (1,)), ((), ())), preferred_element_type=F32
                )
                scores = scores.astype(BF16) * mask_ref[r, :seen]
                o_ref[r, cols] = jnp.dot(scores, v_ref[:seen, cols], preferred_element_type=F32)

    spec = pl.BlockSpec((rows, part), lambda g, m: (0, g))
    return call(
        kernel,
        (width // part,),
        [spec] * 3,
        spec,
        jax.ShapeDtypeStruct((rows, width), F32),
        3 * rows * rows * width,
        10 * rows * width,
        [pltpu.VMEM((rows, rows), BF16)],
    )(meta, query, key, value)


def whole(shape):
    return pl.BlockSpec(shape, lambda *_: (0,) * len(shape))


def local(kernel, meta, arrays, shapes, micros, limit=4, specs=None):
    return call(
        kernel,
        (1,),
        specs or [whole(a.shape) for a in arrays],
        [whole(s.shape) for s in shapes],
        shapes,
        int(micros * 1e9),
        1024,
        (),
        limit * 1024 * 1024,
    )(meta, *arrays)


def group(rows, part, slot):
    return pl.BlockSpec((rows, part), lambda i, m: (0, m[1] ^ slot))


def after(meta, *arrays):
    return lax.optimization_barrier((meta, *arrays))[0]


def factor(condition):
    return jnp.where(condition, 1.0, 0.0)


def slice_weights(meta, weight, columns):
    part, half = weight.shape[0] // 4, columns // 2
    shapes = [jax.ShapeDtypeStruct((part, half), BF16), jax.ShapeDtypeStruct((part, half // 2), BF16)]

    def kernel(meta_ref, w_ref, a_ref, b_ref, sems):
        rows = pl.ds(pl.multiple_of(meta_ref[1] * part, DH), part)
        base = (1 - meta_ref[2]) * columns
        starts = (base + meta_ref[3] * half, base + (1 - meta_ref[3]) * half)
        copies = []
        for n, (o_ref, start) in enumerate(zip((a_ref, b_ref), starts)):
            cols = pl.ds(pl.multiple_of(start, DH), shapes[n].shape[1])
            copies.append(pltpu.make_async_copy(w_ref.at[rows, cols], o_ref, sems.at[n]))
            copies[-1].start()
        for copy in copies:
            copy.wait()

    return call(
        kernel,
        (1,),
        [pl.BlockSpec(memory_space=pl.ANY)],
        [pl.BlockSpec(memory_space=pl.ANY)] * 2,
        shapes,
        6 * 10**9,
        1024,
        [pltpu.SemaphoreType.DMA((2,))],
        50 * 1024 * 1024,
    )(meta, weight)


def split_states(meta, key, value, doc_count):
    rows, width = key.shape
    part = width // 4
    order = (1, 3, 0, 2)

    def kernel(meta_ref, *refs):
        offset = meta_ref[0] * rows
        first = doc_start(meta_ref, doc_count, offset + rows - 1) - offset
        live = lax.broadcasted_iota(jnp.int32, (rows, DH), 0) >= first
        for i in range(4):
            k_ref, v_ref, o_ref = refs[i], refs[4 + i], refs[8 + i // 2]
            for h in range(part // DH):
                cols = slice(h * DH, (h + 1) * DH)
                k = jnp.where(live, k_ref[:, cols], jnp.zeros((), BF16))
                state = lax.dot_general(
                    k, v_ref[:, cols], (((0,), (0,)), ((), ())), preferred_element_type=F32
                )
                o_ref[i % 2, cols, :] = state.astype(BF16)

    arrays, specs = [key] * 4 + [value] * 4, [group(rows, part, s) for s in order] * 2
    return local(kernel, meta, arrays, [jax.ShapeDtypeStruct((2, part, DH), BF16)] * 2, 2, 10, specs)


def seen_mask(meta_ref, rows, doc_count):
    offset = meta_ref[0] * rows
    t = lax.broadcasted_iota(jnp.int32, (rows, rows), 0)
    s = lax.broadcasted_iota(jnp.int32, (rows, rows), 1)
    pos = lax.broadcasted_iota(jnp.int32, (rows, 1), 0)
    first = jnp.zeros((rows, 1), jnp.int32)
    bound = -offset
    for d in range(doc_count):
        bound = bound + meta_ref[LENS + d]
        first = jnp.where(bound <= pos, bound, first)
    return jnp.where((s <= t) & (s >= first), 1.0, 0.0).astype(BF16)


def within_slot(meta, query, key, value, doc_count, slot, mask=None):
    rows, width = query.shape
    part = width // 4
    tile = rows // 2
    make = mask is None

    def kernel(meta_ref, q_ref, k_ref, v_ref, *rest):
        if make:
            o_ref, mask_ref = rest
            mask_ref[...] = seen_mask(meta_ref, rows, doc_count)
        else:
            mask_ref, o_ref = rest
        for h in range(part // DH):
            cols = slice(h * DH, (h + 1) * DH)
            for i in range(2):
                r = slice(i * tile, (i + 1) * tile)
                seen = (i + 1) * tile
                scores = lax.dot_general(
                    q_ref[r, cols], k_ref[:seen, cols], (((1,), (1,)), ((), ())), preferred_element_type=F32
                )
                scores = scores.astype(BF16) * mask_ref[r, :seen]
                o_ref[r, cols] = jnp.dot(scores, v_ref[:seen, cols], preferred_element_type=F32)

    shapes = [jax.ShapeDtypeStruct((rows, part), F32)]
    arrays, specs = [query, key, value], [group(rows, part, slot)] * 3
    if make:
        shapes = shapes + [jax.ShapeDtypeStruct((rows, rows), BF16)]
        return local(kernel, meta, arrays, shapes, 2, 10, specs)
    return local(kernel, meta, [*arrays, mask], shapes, 2, 10, [*specs, whole(mask.shape)])[0]


def small(kernel, meta, arrays, shape, count):
    return local(kernel, meta, arrays, [jax.ShapeDtypeStruct(shape, BF16)] * count, 0.6)


def join_core(meta, keep, got, rows, doc_count):
    def kernel(meta_ref, keep_ref, got_ref, a_ref, b_ref):
        low = meta_ref[0] & -2
        joined = factor(doc_start(meta_ref, doc_count, (low + 2) * rows - 1) < (low + 1) * rows)
        upper = (meta_ref[1] & 1) != 0
        own, other = jnp.where(upper, 1.0, joined), jnp.where(upper, joined, 1.0)
        for i, o_ref in enumerate((a_ref, b_ref)):
            o_ref[...] = (own * keep_ref[i].astype(F32) + other * got_ref[i].astype(F32)).astype(BF16)

    return small(kernel, meta, (keep, got), keep.shape[1:], 2)


def join_chips(meta, mine, got, rows, doc_count):
    def kernel(meta_ref, a_ref, b_ref, o_ref):
        low = meta_ref[0] & -4
        joined = factor(doc_start(meta_ref, doc_count, (low + 4) * rows - 1) < (low + 2) * rows)
        upper = (meta_ref[1] & 2) != 0
        own, other = jnp.where(upper, 1.0, joined), jnp.where(upper, joined, 1.0)
        o_ref[...] = (own * a_ref[...].astype(F32) + other * b_ref[...].astype(F32)).astype(BF16)

    return small(kernel, meta, (mine, got), mine.shape, 1)[0]


def join_planes(meta, plane_sum, previous, rows, doc_count):
    def kernel(meta_ref, a_ref, b_ref, o_ref):
        low = meta_ref[0] & -4
        joined = factor(doc_start(meta_ref, doc_count, (low + 4) * rows - 1) < low * rows)
        o_ref[...] = (a_ref[...].astype(F32) + joined * b_ref[...].astype(F32)).astype(BF16)

    return small(kernel, meta, (plane_sum, previous), plane_sum.shape, 1)[0]


def carry_in_chip(meta_ref, chip, keep, got, rows, doc_count):
    low = meta_ref[0] & -2
    begins = doc_start(meta_ref, doc_count, (low + 1) * rows)
    through, joined = factor(begins < low * rows), factor(begins < (low + 1) * rows)
    upper = (meta_ref[1] & 1) != 0
    later = through * chip + joined * jnp.where(upper, got, keep).astype(F32)
    return jnp.where(upper, later, chip), jnp.where(upper, chip, later)


def carry_first(meta, near, far, mine, got, keep, core_got, rows, doc_count):
    def kernel(meta_ref, near_ref, far_ref, a_ref, b_ref, keep_ref, got_ref, o_ref, core_ref, chip_ref):
        low = meta_ref[0] & -4
        begins = doc_start(meta_ref, doc_count, low * rows)
        first = factor(begins < low * rows) * near_ref[...].astype(F32)
        first = first + factor(begins < (low - 4) * rows) * far_ref[...].astype(F32)
        begins = doc_start(meta_ref, doc_count, (low + 2) * rows)
        through, joined = factor(begins < low * rows), factor(begins < (low + 2) * rows)
        upper = (meta_ref[1] & 2) != 0
        later = through * first + joined * jnp.where(upper, b_ref[...], a_ref[...]).astype(F32)
        chip_ref[...] = jnp.where(upper, first, later).astype(BF16)
        chip = jnp.where(upper, later, first)
        ours, theirs = carry_in_chip(meta_ref, chip, keep_ref[0], got_ref[0], rows, doc_count)
        o_ref[...] = ours.astype(BF16)
        core_ref[...] = theirs.astype(BF16)

    return small(kernel, meta, (near, far, mine, got, keep, core_got), mine.shape, 3)


def carry_second(meta, chip, keep, core_got, rows, doc_count):
    def kernel(meta_ref, chip_ref, keep_ref, got_ref, o_ref, core_ref):
        ours, theirs = carry_in_chip(
            meta_ref, chip_ref[...].astype(F32), keep_ref[1], got_ref[1], rows, doc_count
        )
        o_ref[...] = ours.astype(BF16)
        core_ref[...] = theirs.astype(BF16)

    return small(kernel, meta, (chip, keep, core_got), chip.shape, 2)


def norm_heads(meta, query, withins, carries, gain, doc_count, slots=None, split=None):
    rows = query.shape[0]
    part = carries[0].shape[0]
    count = len(carries)
    heights = split or (rows,)

    def kernel(meta_ref, *refs):
        offset = meta_ref[0] * rows
        begins = doc_start(meta_ref, doc_count, offset)
        bound = jnp.int32(0)
        end = jnp.int32(0)
        for d in range(doc_count):
            previous = bound
            bound = bound + meta_ref[LENS + d]
            end = jnp.where(previous <= offset, bound, end)
        stop = jnp.where(begins < offset, end - offset, 0)
        cross = lax.broadcasted_iota(jnp.int32, (rows, DH), 0) < stop
        outs = refs[4 * count :]
        for n in range(count):
            q_ref, w_ref, c_ref, g_ref = refs[4 * n : 4 * n + 4]
            for h in range(part // DH):
                cols = slice(h * DH, (h + 1) * DH)
                term = jnp.dot(q_ref[:, cols], c_ref[cols, :], preferred_element_type=F32)
                mixture = w_ref[:, cols] + jnp.where(cross, term, 0.0)
                mean = jnp.mean(mixture * mixture, axis=-1, keepdims=True)
                normed = (mixture * lax.rsqrt(mean + 1e-06) * g_ref[:, cols]).astype(BF16)
                top = 0
                for o_ref, height in zip(outs, heights):
                    o_ref[:, n * part + h * DH : n * part + (h + 1) * DH] = normed[top : top + height]
                    top += height

    gain = gain.reshape(1, -1)
    arrays, specs = [], []
    for n in range(count):
        arrays += [query, withins[n], carries[n], gain]
        wide = [whole((rows, part)), whole((1, part))] if slots is None else [
            group(rows, part, slots[n]), group(1, part, slots[n])
        ]
        specs += [wide[0], whole((rows, part)), whole((part, DH)), wide[1]]
    shapes = [jax.ShapeDtypeStruct((height, part * count), BF16) for height in heights]
    outs = local(kernel, meta, arrays, shapes, count, 10, specs)
    return outs if split else outs[0]


TILES = 4
OWN_TILES = 2


def project_own(meta, pieces, weight, columns):
    rows = pieces[0].shape[0]
    part = weight.shape[0] // 4
    tile = columns // OWN_TILES
    count = len(pieces)

    def kernel(meta_ref, *refs):
        ns, ws, o_ref = refs[:count], refs[count:-1], refs[-1]
        n = jnp.concatenate([r[...] for r in ns], axis=1)
        w = jnp.concatenate([r[...] for r in ws], axis=0)
        o_ref[...] = jnp.dot(n, w, preferred_element_type=F32)

    return call(
        kernel,
        (OWN_TILES,),
        [whole(p.shape) for p in pieces]
        + [pl.BlockSpec((part, tile), lambda n, m, s=s: (m[1] ^ s, m[2] * OWN_TILES + n)) for s in range(4)],
        pl.BlockSpec((rows, tile), lambda n, m: (0, n)),
        jax.ShapeDtypeStruct((rows, columns), F32),
        10**6,
        1024,
    )(meta, *pieces, *[weight] * 4)


def project_more(meta, total, pieces, weights, final):
    rows, columns = total.shape
    tile = columns // TILES
    count = len(pieces)
    flat = [w for ws in weights for w in ws]
    places = []
    for ws in weights:
        start, slot = 0, []
        for w in ws:
            slot.append((start, start + w.shape[1]))
            start += w.shape[1]
        places.append(slot)

    def kernel(meta_ref, t_ref, *refs):
        ns, ws, rest = refs[:count], refs[count : count + len(flat)], refs[count + len(flat) :]
        n = jnp.concatenate([r[...] for r in ns], axis=1)
        copies = []
        for c in range(TILES):
            low, high = c * tile, (c + 1) * tile
            rows_of, at = [], 0
            for slot in places:
                held = []
                for k, (start, stop) in enumerate(slot):
                    first, last = max(start, low), min(stop, high)
                    if first < last:
                        held.append(ws[at + k][:, first - start : last - start])
                rows_of.append(jnp.concatenate(held, axis=1))
                at += len(slot)
            w = jnp.concatenate(rows_of, axis=0)
            cols = pl.ds(pl.multiple_of((c ^ (meta_ref[3] * (TILES // 2))) * tile, DH), tile)
            value = t_ref[:, cols] + jnp.dot(n, w, preferred_element_type=F32)
            if final:
                o_ref, held_ref, sems = rest
                held_ref[c] = value.astype(BF16)
                copies.append(pltpu.make_async_copy(held_ref.at[c], o_ref.at[:, cols], sems.at[c]))
                copies[-1].start()
            else:
                rest[0][:, cols] = value
        for copy in copies:
            copy.wait()

    vmem = pl.BlockSpec(memory_space=pltpu.VMEM)
    scratch = [pltpu.VMEM((TILES, rows, tile), BF16), pltpu.SemaphoreType.DMA((TILES,))]
    return call(
        kernel,
        (1,),
        [vmem] * (1 + count + len(flat)),
        pl.BlockSpec(memory_space=pl.ANY) if final else vmem,
        jax.ShapeDtypeStruct((rows, columns), BF16 if final else F32),
        10**6,
        1024,
        scratch if final else (),
        aliases={} if final else {1: 0},
    )(meta, total, *pieces, *flat)


def pair_body(n_seq, query, key, value, doc_lengths, gain, weight):
    rows, width = query.shape
    docs = doc_lengths.shape[0]
    plane, part = 4, width // 4
    columns = weight.shape[1] // 2
    half = columns // 2
    block = lax.axis_index("seq").astype(jnp.int32)
    group = lax.axis_index("head").astype(jnp.int32)
    member = block % plane
    side = (block // plane) % 2
    meta = jnp.concatenate([
        jnp.stack([block, member, group, side]), jnp.zeros((LENS - 4,), jnp.int32), doc_lengths
    ])

    def swap(x, bit):
        return lax.ppermute(x, "seq", [(i, i ^ bit) for i in range(n_seq)])

    def shift(x, count):
        return lax.ppermute(x, "seq", [(i, i + count) for i in range(n_seq - count)])

    def flip(x):
        return lax.ppermute(x, "head", [(0, 1), (1, 0)])

    def behind(x, *arrays):
        return lax.optimization_barrier((x, *arrays))[0]

    quarter = half // 2
    sent = slice_weights(meta, weight, columns)
    w0 = [flip(sent[0])]
    w0.append(flip(sent[1]))
    send, keep = split_states(after(meta, *sent), key, value, docs)
    core_got = swap(send, 1)
    query = behind(query, send)
    within0, mask = within_slot(after(meta, send), query, key, value, docs, 0)
    chip0, chip2 = join_core(after(meta, within0), keep, core_got, rows, docs)
    chip_got = swap(chip2, 2)
    within1 = within_slot(after(meta, chip0), query, key, value, docs, 1, mask)
    plane_sum = join_chips(after(meta, within1), chip0, chip_got, rows, docs)
    near = shift(plane_sum, plane)
    within2 = within_slot(after(meta, plane_sum), query, key, value, docs, 2, mask)
    both = join_planes(after(meta, within2), plane_sum, near, rows, docs)
    far = shift(both, 2 * plane)
    carry0, core_carry0, chip_carry = carry_first(
        meta, near, far, chip0, chip_got, keep, core_got, rows, docs
    )
    carry1 = swap(core_carry0, 1)
    chip_carry2 = swap(chip_carry, 2)

    def norm(slots, withins, carries):
        return norm_heads(meta, query, withins, carries, gain, docs, slots)

    normed0 = norm((0,), [within0], [carry0])
    far0 = flip(normed0)
    within3 = within_slot(after(meta, normed0), query, key, value, docs, 3, mask)
    normed1 = norm((1,), [within1], [carry1])
    far1 = flip(normed1)
    w2 = [swap(behind(w0[0], both), 2)]
    carry2, core_carry2 = carry_second(after(meta, far0, w2[0], normed1), chip_carry2, keep, core_got, rows, docs)
    carry3 = swap(core_carry2, 1)
    normed2 = norm((2, 3), [within2, within3], [carry2, carry3])
    far2 = flip(normed2)

    total = project_own(after(meta, far1), [normed0, normed1, normed2], weight, columns)
    w0.append(swap(behind(w0[0], normed1)[:, quarter:], plane))
    w2.append(swap(behind(w0[1], far0), 2))
    w2.append(swap(behind(w2[0], carry2)[:, quarter:], plane))

    def cut(w, width):
        return [w[:, at : at + width] for at in range(0, w.shape[1], width)]

    w1 = [swap(x, 1) for w in w0 for x in cut(w, quarter)]
    w3 = [swap(x, 1) for w, width in zip(w2, (quarter, quarter // 2, quarter // 2)) for x in cut(w, width)]

    total = project_more(meta, total, [far0, far1], [w0, w1], False)
    return project_more(meta, total, [far2], [w2, w3], True)


def body(n_seq, n_head, query, key, value, doc_lengths, gain, weight):
    rows, width = query.shape
    doc_count = doc_lengths.shape[0]
    plane = n_seq // PLANES
    if n_head == 2 and plane == 4 and width % (4 * DH) == 0:
        return pair_body(n_seq, query, key, value, doc_lengths, gain, weight)
    block = lax.axis_index("seq").astype(jnp.int32)
    group = lax.axis_index("head").astype(jnp.int32)
    member = block % plane
    meta = jnp.concatenate([
        jnp.stack([block, member, group]), jnp.zeros((LENS - 3,), jnp.int32), doc_lengths
    ])

    bounds = jnp.cumsum(doc_lengths)

    def first_block(token):
        starts = jnp.max(jnp.where(bounds <= token, bounds, 0))
        return starts // rows

    def weigh(condition):
        return condition.astype(F32)

    def swap(x, bit):
        return lax.ppermute(x, "seq", [(i, i ^ bit) for i in range(n_seq)])

    by_slot = (width // DH) % plane == 0
    steps = plane if by_slot else 1
    states = block_states(meta, key, value, doc_count, steps)
    if not by_slot:
        states = states.reshape(plane, width // plane, DH)[jnp.arange(plane, dtype=jnp.int32) ^ member]
    slots = [states[s] for s in range(plane)]

    kept = []
    bit = 1
    while bit < plane:
        mine, send = slots[0::2], slots[1::2]
        got = swap(jnp.stack(send), bit)
        got = [got[i] for i in range(len(send))]
        upper = (member & bit) != 0
        unit = block & ~(2 * bit - 1)
        joined = weigh(first_block((unit + 2 * bit) * rows - 1) < unit + bit)
        own_factor = jnp.where(upper, 1.0, joined)
        got_factor = jnp.where(upper, joined, 1.0)
        kept.append((mine, got, bit, upper, unit))
        slots = [
            (own_factor * a.astype(F32) + got_factor * b.astype(F32)).astype(BF16) for a, b in zip(mine, got)
        ]
        bit *= 2
    base = block - member
    begins = first_block(base * rows)
    carry = jnp.zeros(slots[0].shape, F32)
    for d in range(PLANES - 1, 0, -1):
        shift = d * plane
        got = lax.ppermute(slots[0], "seq", [(i, i + shift) for i in range(n_seq - shift)])
        carry = carry + weigh((base - shift + plane - 1 >= begins) & (base >= shift)) * got.astype(F32)
    carries = [carry]

    for mine, got, bit, upper, unit in reversed(kept):
        middle = unit + bit
        begins = first_block(middle * rows)
        through, joined = weigh(begins < unit), weigh(begins < middle)
        ours, theirs = [], []
        for carry, a, b in zip(carries, mine, got):
            lower_state = jnp.where(upper, b, a).astype(F32)
            after = through * carry + joined * lower_state
            ours.append(jnp.where(upper, after, carry))
            theirs.append(jnp.where(upper, carry, after).astype(BF16))
        back = swap(jnp.stack(theirs), bit)
        carries = [x for i, c in enumerate(ours) for x in (c, back[i])]
    carries = [c.astype(BF16) for c in carries]

    within = within_block(meta, query, key, value, doc_count)
    natural = jnp.stack(carries)[jnp.arange(plane, dtype=jnp.int32) ^ member].reshape(width, DH)
    normed = norm_heads(meta, query, [within], [natural], gain, doc_count)
    partial_sum = jnp.dot(normed, weight, preferred_element_type=F32)
    return lax.psum_scatter(partial_sum.astype(BF16), "head", scatter_dimension=1, tiled=True)


def solution(mesh):
    return jax.shard_map(
        functools.partial(body, mesh.shape["seq"], mesh.shape["head"]),
        mesh=mesh,
        in_specs=(
            P("seq", "head"),
            P("seq", "head"),
            P("seq", "head"),
            P(),
            P("head"),
            P("head", None),
        ),
        out_specs=P("seq", "head"),
        check_vma=False,
    )
```

```python
import functools

import jax
import jax.numpy as jnp
from jax import lax
from jax.experimental import pallas as pl
from jax.experimental.pallas import tpu as pltpu
from jax.sharding import PartitionSpec as P

DH = 128
PLANES = 4
F32, BF16 = jnp.float32, jnp.bfloat16
LENS = 8
VMEM_LIMIT = 24 * 1024 * 1024


def doc_start(meta, doc_count, token):
    bound = jnp.int32(0)
    start = jnp.int32(0)
    for d in range(doc_count):
        bound = bound + meta[LENS + d]
        start = jnp.where(bound <= token, bound, start)
    return start


def call(kernel, grid, in_specs, out_specs, out_shape, flops, bytes_accessed, scratch=(), vmem=VMEM_LIMIT, aliases={}):
    return pl.pallas_call(
        kernel,
        grid_spec=pltpu.PrefetchScalarGridSpec(
            num_scalar_prefetch=1,
            grid=grid,
            in_specs=in_specs,
            out_specs=out_specs,
            scratch_shapes=scratch,
        ),
        out_shape=out_shape,
        input_output_aliases=aliases,
        compiler_params=pltpu.CompilerParams(vmem_limit_bytes=vmem),
        cost_estimate=pl.CostEstimate(flops=flops, bytes_accessed=bytes_accessed, transcendentals=0),
    )


def block_states(meta, key, value, doc_count, steps):
    rows, width = key.shape
    part = width // steps

    def kernel(meta_ref, k_ref, v_ref, o_ref):
        offset = meta_ref[0] * rows
        first = doc_start(meta_ref, doc_count, offset + rows - 1) - offset
        live = lax.broadcasted_iota(jnp.int32, (rows, DH), 0) >= first
        for h in range(part // DH):
            cols = slice(h * DH, (h + 1) * DH)
            k = jnp.where(live, k_ref[:, cols], jnp.zeros((), BF16))
            s = lax.dot_general(k, v_ref[:, cols], (((0,), (0,)), ((), ())), preferred_element_type=F32)
            o_ref[0, cols, :] = s.astype(BF16)

    def slot(g, m):
        return (g ^ m[1], 0, 0) if steps > 1 else (0, 0, 0)

    return call(
        kernel,
        (steps,),
        [pl.BlockSpec((rows, part), lambda g, m: (0, g))] * 2,
        pl.BlockSpec((1, part, DH), slot),
        jax.ShapeDtypeStruct((steps, part, DH), BF16),
        2 * rows * width * DH,
        2 * 2 * rows * width,
    )(meta, key, value)


def within_block(meta, query, key, value, doc_count):
    rows, width = query.shape
    part = DH
    for heads in (4, 3, 2):
        if width % (heads * DH) == 0:
            part = heads * DH
            break
    tile = rows // 2

    def kernel(meta_ref, q_ref, k_ref, v_ref, o_ref, mask_ref):
        @pl.when(pl.program_id(0) == 0)
        def _():
            offset = meta_ref[0] * rows
            t = lax.broadcasted_iota(jnp.int32, (rows, rows), 0)
            s = lax.broadcasted_iota(jnp.int32, (rows, rows), 1)
            pos = lax.broadcasted_iota(jnp.int32, (rows, 1), 0)
            first = jnp.zeros((rows, 1), jnp.int32)
            bound = -offset
            for d in range(doc_count):
                bound = bound + meta_ref[LENS + d]
                first = jnp.where(bound <= pos, bound, first)
            mask_ref[...] = jnp.where((s <= t) & (s >= first), 1.0, 0.0).astype(BF16)

        for h in range(part // DH):
            cols = slice(h * DH, (h + 1) * DH)
            for i in range(2):
                r = slice(i * tile, (i + 1) * tile)
                seen = (i + 1) * tile
                scores = lax.dot_general(
                    q_ref[r, cols], k_ref[:seen, cols], (((1,), (1,)), ((), ())), preferred_element_type=F32
                )
                scores = scores.astype(BF16) * mask_ref[r, :seen]
                o_ref[r, cols] = jnp.dot(scores, v_ref[:seen, cols], preferred_element_type=F32)

    spec = pl.BlockSpec((rows, part), lambda g, m: (0, g))
    return call(
        kernel,
        (width // part,),
        [spec] * 3,
        spec,
        jax.ShapeDtypeStruct((rows, width), F32),
        3 * rows * rows * width,
        10 * rows * width,
        [pltpu.VMEM((rows, rows), BF16)],
    )(meta, query, key, value)


def whole(shape):
    return pl.BlockSpec(shape, lambda *_: (0,) * len(shape))


def local(kernel, meta, arrays, shapes, micros, limit=4, specs=None):
    return call(
        kernel,
        (1,),
        specs or [whole(a.shape) for a in arrays],
        [whole(s.shape) for s in shapes],
        shapes,
        int(micros * 1e9),
        1024,
        (),
        limit * 1024 * 1024,
    )(meta, *arrays)


def group(rows, part, slot):
    return pl.BlockSpec((rows, part), lambda i, m: (0, m[1] ^ slot))


def after(meta, *arrays):
    return lax.optimization_barrier((meta, *arrays))[0]


def factor(condition):
    return jnp.where(condition, 1.0, 0.0)


def slice_weights(meta, weight, columns):
    part, half = weight.shape[0] // 4, columns // 2
    shapes = [jax.ShapeDtypeStruct((part, half), BF16)]

    def kernel(meta_ref, w_ref, o_ref, sem):
        rows = pl.ds(pl.multiple_of(meta_ref[1] * part, DH), part)
        start = (1 - meta_ref[2]) * columns + meta_ref[3] * half
        copy = pltpu.make_async_copy(w_ref.at[rows, pl.ds(pl.multiple_of(start, DH), half)], o_ref, sem)
        copy.start()
        copy.wait()

    return call(
        kernel,
        (1,),
        [pl.BlockSpec(memory_space=pl.ANY)],
        [pl.BlockSpec(memory_space=pltpu.VMEM)] * len(shapes),
        shapes,
        6 * 10**9,
        1024,
        [pltpu.SemaphoreType.DMA],
        50 * 1024 * 1024,
    )(meta, weight)


def split_states(meta, key, value, doc_count):
    rows, width = key.shape
    part = width // 4
    order = (1, 3, 0, 2)

    def kernel(meta_ref, *refs):
        offset = meta_ref[0] * rows
        first = doc_start(meta_ref, doc_count, offset + rows - 1) - offset
        live = lax.broadcasted_iota(jnp.int32, (rows, DH), 0) >= first
        for i in range(4):
            k_ref, v_ref, o_ref = refs[i], refs[4 + i], refs[8 + i // 2]
            for h in range(part // DH):
                cols = slice(h * DH, (h + 1) * DH)
                k = jnp.where(live, k_ref[:, cols], jnp.zeros((), BF16))
                state = lax.dot_general(
                    k, v_ref[:, cols], (((0,), (0,)), ((), ())), preferred_element_type=F32
                )
                o_ref[i % 2, cols, :] = state.astype(BF16)

    arrays, specs = [key] * 4 + [value] * 4, [group(rows, part, s) for s in order] * 2
    return local(kernel, meta, arrays, [jax.ShapeDtypeStruct((2, part, DH), BF16)] * 2, 2, 10, specs)


def seen_mask(meta_ref, rows, doc_count):
    offset = meta_ref[0] * rows
    t = lax.broadcasted_iota(jnp.int32, (rows, rows), 0)
    s = lax.broadcasted_iota(jnp.int32, (rows, rows), 1)
    pos = lax.broadcasted_iota(jnp.int32, (rows, 1), 0)
    first = jnp.zeros((rows, 1), jnp.int32)
    bound = -offset
    for d in range(doc_count):
        bound = bound + meta_ref[LENS + d]
        first = jnp.where(bound <= pos, bound, first)
    return jnp.where((s <= t) & (s >= first), 1.0, 0.0).astype(BF16)


def within_slot(meta, query, key, value, doc_count, slot, mask=None):
    rows, width = query.shape
    part = width // 4
    tile = rows // 2
    make = mask is None

    def kernel(meta_ref, q_ref, k_ref, v_ref, *rest):
        if make:
            o_ref, mask_ref = rest
            mask_ref[...] = seen_mask(meta_ref, rows, doc_count)
        else:
            mask_ref, o_ref = rest
        for h in range(part // DH):
            cols = slice(h * DH, (h + 1) * DH)
            for i in range(2):
                r = slice(i * tile, (i + 1) * tile)
                seen = (i + 1) * tile
                scores = lax.dot_general(
                    q_ref[r, cols], k_ref[:seen, cols], (((1,), (1,)), ((), ())), preferred_element_type=F32
                )
                scores = scores.astype(BF16) * mask_ref[r, :seen]
                o_ref[r, cols] = jnp.dot(scores, v_ref[:seen, cols], preferred_element_type=F32)

    shapes = [jax.ShapeDtypeStruct((rows, part), F32)]
    arrays, specs = [query, key, value], [group(rows, part, slot)] * 3
    if make:
        shapes = shapes + [jax.ShapeDtypeStruct((rows, rows), BF16)]
        return local(kernel, meta, arrays, shapes, 2, 10, specs)
    return local(kernel, meta, [*arrays, mask], shapes, 2, 10, [*specs, whole(mask.shape)])[0]


def small(kernel, meta, arrays, shape, count):
    return local(kernel, meta, arrays, [jax.ShapeDtypeStruct(shape, BF16)] * count, 0.6)


def join_core(meta, keep, got, rows, doc_count):
    def kernel(meta_ref, keep_ref, got_ref, a_ref, b_ref):
        low = meta_ref[0] & -2
        joined = factor(doc_start(meta_ref, doc_count, (low + 2) * rows - 1) < (low + 1) * rows)
        upper = (meta_ref[1] & 1) != 0
        own, other = jnp.where(upper, 1.0, joined), jnp.where(upper, joined, 1.0)
        for i, o_ref in enumerate((a_ref, b_ref)):
            o_ref[...] = (own * keep_ref[i].astype(F32) + other * got_ref[i].astype(F32)).astype(BF16)

    return small(kernel, meta, (keep, got), keep.shape[1:], 2)


def join_chips(meta, mine, got, rows, doc_count):
    def kernel(meta_ref, a_ref, b_ref, o_ref):
        low = meta_ref[0] & -4
        joined = factor(doc_start(meta_ref, doc_count, (low + 4) * rows - 1) < (low + 2) * rows)
        upper = (meta_ref[1] & 2) != 0
        own, other = jnp.where(upper, 1.0, joined), jnp.where(upper, joined, 1.0)
        o_ref[...] = (own * a_ref[...].astype(F32) + other * b_ref[...].astype(F32)).astype(BF16)

    return small(kernel, meta, (mine, got), mine.shape, 1)[0]


def join_planes(meta, plane_sum, previous, rows, doc_count):
    def kernel(meta_ref, a_ref, b_ref, o_ref):
        low = meta_ref[0] & -4
        joined = factor(doc_start(meta_ref, doc_count, (low + 4) * rows - 1) < low * rows)
        o_ref[...] = (a_ref[...].astype(F32) + joined * b_ref[...].astype(F32)).astype(BF16)

    return small(kernel, meta, (plane_sum, previous), plane_sum.shape, 1)[0]


def carry_in_chip(meta_ref, chip, keep, got, rows, doc_count):
    low = meta_ref[0] & -2
    begins = doc_start(meta_ref, doc_count, (low + 1) * rows)
    through, joined = factor(begins < low * rows), factor(begins < (low + 1) * rows)
    upper = (meta_ref[1] & 1) != 0
    later = through * chip + joined * jnp.where(upper, got, keep).astype(F32)
    return jnp.where(upper, later, chip), jnp.where(upper, chip, later)


def carry_first(meta, near, far, mine, got, keep, core_got, rows, doc_count):
    def kernel(meta_ref, near_ref, far_ref, a_ref, b_ref, keep_ref, got_ref, o_ref, core_ref, chip_ref):
        low = meta_ref[0] & -4
        begins = doc_start(meta_ref, doc_count, low * rows)
        first = factor(begins < low * rows) * near_ref[...].astype(F32)
        first = first + factor(begins < (low - 4) * rows) * far_ref[...].astype(F32)
        begins = doc_start(meta_ref, doc_count, (low + 2) * rows)
        through, joined = factor(begins < low * rows), factor(begins < (low + 2) * rows)
        upper = (meta_ref[1] & 2) != 0
        later = through * first + joined * jnp.where(upper, b_ref[...], a_ref[...]).astype(F32)
        chip_ref[...] = jnp.where(upper, first, later).astype(BF16)
        chip = jnp.where(upper, later, first)
        ours, theirs = carry_in_chip(meta_ref, chip, keep_ref[0], got_ref[0], rows, doc_count)
        o_ref[...] = ours.astype(BF16)
        core_ref[...] = theirs.astype(BF16)

    return small(kernel, meta, (near, far, mine, got, keep, core_got), mine.shape, 3)


def carry_second(meta, chip, keep, core_got, rows, doc_count):
    def kernel(meta_ref, chip_ref, keep_ref, got_ref, o_ref, core_ref):
        ours, theirs = carry_in_chip(
            meta_ref, chip_ref[...].astype(F32), keep_ref[1], got_ref[1], rows, doc_count
        )
        o_ref[...] = ours.astype(BF16)
        core_ref[...] = theirs.astype(BF16)

    return small(kernel, meta, (chip, keep, core_got), chip.shape, 2)


def norm_heads(meta, query, withins, carries, gain, doc_count, slots=None, split=None):
    rows = query.shape[0]
    part = carries[0].shape[0]
    count = len(carries)
    heights = split or (rows,)

    def kernel(meta_ref, *refs):
        offset = meta_ref[0] * rows
        begins = doc_start(meta_ref, doc_count, offset)
        bound = jnp.int32(0)
        end = jnp.int32(0)
        for d in range(doc_count):
            previous = bound
            bound = bound + meta_ref[LENS + d]
            end = jnp.where(previous <= offset, bound, end)
        stop = jnp.where(begins < offset, end - offset, 0)
        cross = lax.broadcasted_iota(jnp.int32, (rows, DH), 0) < stop
        outs = refs[4 * count :]
        for n in range(count):
            q_ref, w_ref, c_ref, g_ref = refs[4 * n : 4 * n + 4]
            for h in range(part // DH):
                cols = slice(h * DH, (h + 1) * DH)
                term = jnp.dot(q_ref[:, cols], c_ref[cols, :], preferred_element_type=F32)
                mixture = w_ref[:, cols] + jnp.where(cross, term, 0.0)
                mean = jnp.mean(mixture * mixture, axis=-1, keepdims=True)
                normed = (mixture * lax.rsqrt(mean + 1e-06) * g_ref[:, cols]).astype(BF16)
                top = 0
                for o_ref, height in zip(outs, heights):
                    o_ref[:, n * part + h * DH : n * part + (h + 1) * DH] = normed[top : top + height]
                    top += height

    gain = gain.reshape(1, -1)
    arrays, specs = [], []
    for n in range(count):
        arrays += [query, withins[n], carries[n], gain]
        wide = [whole((rows, part)), whole((1, part))] if slots is None else [
            group(rows, part, slots[n]), group(1, part, slots[n])
        ]
        specs += [wide[0], whole((rows, part)), whole((part, DH)), wide[1]]
    shapes = [jax.ShapeDtypeStruct((height, part * count), BF16) for height in heights]
    outs = local(kernel, meta, arrays, shapes, count, 10, specs)
    return outs if split else outs[0]


TILES = 4
OWN_TILES = 2


def project_own(meta, pieces, weight, columns):
    rows = pieces[0].shape[0]
    part = weight.shape[0] // 4
    tile = columns // OWN_TILES
    count = len(pieces)

    def kernel(meta_ref, *refs):
        ns, ws, o_ref = refs[:count], refs[count:-1], refs[-1]
        n = jnp.concatenate([r[...] for r in ns], axis=1)
        w = jnp.concatenate([r[...] for r in ws], axis=0)
        o_ref[...] = jnp.dot(n, w, preferred_element_type=F32)

    return call(
        kernel,
        (OWN_TILES,),
        [whole(p.shape) for p in pieces]
        + [pl.BlockSpec((part, tile), lambda n, m, s=s: (m[1] ^ s, m[2] * OWN_TILES + n)) for s in range(4)],
        pl.BlockSpec((rows, tile), lambda n, m: (0, n)),
        jax.ShapeDtypeStruct((rows, columns), F32),
        10**6,
        1024,
    )(meta, *pieces, *[weight] * 4)


def project_more(meta, total, pieces, weights, final):
    rows, columns = total.shape
    tile = columns // TILES
    count = len(pieces)
    flat = [w for ws in weights for w in ws]
    places = []
    for ws in weights:
        start, slot = 0, []
        for w in ws:
            slot.append((start, start + w.shape[1]))
            start += w.shape[1]
        places.append(slot)

    def kernel(meta_ref, t_ref, *refs):
        ns, ws, rest = refs[:count], refs[count : count + len(flat)], refs[count + len(flat) :]
        n = jnp.concatenate([r[...] for r in ns], axis=1)
        copies = []
        for c in range(TILES):
            low, high = c * tile, (c + 1) * tile
            rows_of, at = [], 0
            for slot in places:
                held = []
                for k, (start, stop) in enumerate(slot):
                    first, last = max(start, low), min(stop, high)
                    if first < last:
                        held.append(ws[at + k][:, first - start : last - start])
                rows_of.append(jnp.concatenate(held, axis=1))
                at += len(slot)
            w = jnp.concatenate(rows_of, axis=0)
            cols = pl.ds(pl.multiple_of((c ^ (meta_ref[3] * (TILES // 2))) * tile, DH), tile)
            value = t_ref[:, cols] + jnp.dot(n, w, preferred_element_type=F32)
            if final:
                o_ref, held_ref, sems = rest
                held_ref[c] = value.astype(BF16)
                copies.append(pltpu.make_async_copy(held_ref.at[c], o_ref.at[:, cols], sems.at[c]))
                copies[-1].start()
            else:
                rest[0][:, cols] = value
        for copy in copies:
            copy.wait()

    vmem = pl.BlockSpec(memory_space=pltpu.VMEM)
    scratch = [pltpu.VMEM((TILES, rows, tile), BF16), pltpu.SemaphoreType.DMA((TILES,))]
    return call(
        kernel,
        (1,),
        [vmem] * (1 + count + len(flat)),
        pl.BlockSpec(memory_space=pl.ANY) if final else vmem,
        jax.ShapeDtypeStruct((rows, columns), BF16 if final else F32),
        10**6,
        1024,
        scratch if final else (),
        aliases={} if final else {1: 0},
    )(meta, total, *pieces, *flat)


def pair_body(n_seq, query, key, value, doc_lengths, gain, weight):
    rows, width = query.shape
    docs = doc_lengths.shape[0]
    plane, part = 4, width // 4
    columns = weight.shape[1] // 2
    half = columns // 2
    block = lax.axis_index("seq").astype(jnp.int32)
    group = lax.axis_index("head").astype(jnp.int32)
    member = block % plane
    side = (block // plane) % 2
    meta = jnp.concatenate([
        jnp.stack([block, member, group, side]), jnp.zeros((LENS - 4,), jnp.int32), doc_lengths
    ])

    def swap(x, bit):
        return lax.ppermute(x, "seq", [(i, i ^ bit) for i in range(n_seq)])

    def shift(x, count):
        return lax.ppermute(x, "seq", [(i, i + count) for i in range(n_seq - count)])

    def flip(x):
        return lax.ppermute(x, "head", [(0, 1), (1, 0)])

    def behind(x, *arrays):
        return lax.optimization_barrier((x, *arrays))[0]

    quarter = half // 2
    sent = slice_weights(meta, weight, columns)
    w0 = [flip(sent[0])]
    send, keep = split_states(after(meta, *sent), key, value, docs)
    core_got = swap(send, 1)
    query = behind(query, send)
    within0, mask = within_slot(after(meta, send), query, key, value, docs, 0)
    chip0, chip2 = join_core(after(meta, within0), keep, core_got, rows, docs)
    chip_got = swap(chip2, 2)
    within1 = within_slot(after(meta, chip0), query, key, value, docs, 1, mask)
    plane_sum = join_chips(after(meta, within1), chip0, chip_got, rows, docs)
    near = shift(plane_sum, plane)
    within2 = within_slot(after(meta, plane_sum), query, key, value, docs, 2, mask)
    both = join_planes(after(meta, within2), plane_sum, near, rows, docs)
    far = shift(both, 2 * plane)
    carry0, core_carry0, chip_carry = carry_first(
        meta, near, far, chip0, chip_got, keep, core_got, rows, docs
    )
    carry1 = swap(core_carry0, 1)
    chip_carry2 = swap(chip_carry, 2)

    def norm(slots, withins, carries):
        return norm_heads(meta, query, withins, carries, gain, docs, slots)

    normed0 = norm((0,), [within0], [carry0])
    far0 = flip(normed0)
    within3 = within_slot(after(meta, normed0), query, key, value, docs, 3, mask)
    normed1 = norm((1,), [within1], [carry1])
    far1 = flip(normed1)
    w2 = [swap(behind(w0[0], both), 2)]
    carry2, core_carry2 = carry_second(after(meta, far0, w2[0], normed1), chip_carry2, keep, core_got, rows, docs)
    carry3 = swap(core_carry2, 1)
    normed2 = norm((2, 3), [within2, within3], [carry2, carry3])
    far2 = flip(normed2)

    total = project_own(after(meta, far0), [normed0, normed1, normed2], weight, columns)
    w0.append(swap(behind(w0[0], normed0), plane))
    w2.append(swap(behind(w0[1], normed2)[:, :quarter], 2))
    w2.append(swap(behind(w2[0], normed2)[:, quarter:], plane))

    def cut(w, width):
        return [w[:, at : at + width] for at in range(0, w.shape[1], width)]

    w1 = [swap(x, 1) for w in w0 for x in cut(w, quarter)]
    w3 = [swap(x, 1) for w, width in zip(w2, (quarter, quarter // 2, quarter // 2)) for x in cut(w, width)]

    total = project_more(meta, total, [far0, far1], [w0, w1], False)
    return project_more(meta, total, [far2], [w2, w3], True)


def body(n_seq, n_head, query, key, value, doc_lengths, gain, weight):
    rows, width = query.shape
    doc_count = doc_lengths.shape[0]
    plane = n_seq // PLANES
    if n_head == 2 and plane == 4 and width % (4 * DH) == 0:
        return pair_body(n_seq, query, key, value, doc_lengths, gain, weight)
    block = lax.axis_index("seq").astype(jnp.int32)
    group = lax.axis_index("head").astype(jnp.int32)
    member = block % plane
    meta = jnp.concatenate([
        jnp.stack([block, member, group]), jnp.zeros((LENS - 3,), jnp.int32), doc_lengths
    ])

    bounds = jnp.cumsum(doc_lengths)

    def first_block(token):
        starts = jnp.max(jnp.where(bounds <= token, bounds, 0))
        return starts // rows

    def weigh(condition):
        return condition.astype(F32)

    def swap(x, bit):
        return lax.ppermute(x, "seq", [(i, i ^ bit) for i in range(n_seq)])

    by_slot = (width // DH) % plane == 0
    steps = plane if by_slot else 1
    states = block_states(meta, key, value, doc_count, steps)
    if not by_slot:
        states = states.reshape(plane, width // plane, DH)[jnp.arange(plane, dtype=jnp.int32) ^ member]
    slots = [states[s] for s in range(plane)]

    kept = []
    bit = 1
    while bit < plane:
        mine, send = slots[0::2], slots[1::2]
        got = swap(jnp.stack(send), bit)
        got = [got[i] for i in range(len(send))]
        upper = (member & bit) != 0
        unit = block & ~(2 * bit - 1)
        joined = weigh(first_block((unit + 2 * bit) * rows - 1) < unit + bit)
        own_factor = jnp.where(upper, 1.0, joined)
        got_factor = jnp.where(upper, joined, 1.0)
        kept.append((mine, got, bit, upper, unit))
        slots = [
            (own_factor * a.astype(F32) + got_factor * b.astype(F32)).astype(BF16) for a, b in zip(mine, got)
        ]
        bit *= 2
    base = block - member
    begins = first_block(base * rows)
    carry = jnp.zeros(slots[0].shape, F32)
    for d in range(PLANES - 1, 0, -1):
        shift = d * plane
        got = lax.ppermute(slots[0], "seq", [(i, i + shift) for i in range(n_seq - shift)])
        carry = carry + weigh((base - shift + plane - 1 >= begins) & (base >= shift)) * got.astype(F32)
    carries = [carry]

    for mine, got, bit, upper, unit in reversed(kept):
        middle = unit + bit
        begins = first_block(middle * rows)
        through, joined = weigh(begins < unit), weigh(begins < middle)
        ours, theirs = [], []
        for carry, a, b in zip(carries, mine, got):
            lower_state = jnp.where(upper, b, a).astype(F32)
            after = through * carry + joined * lower_state
            ours.append(jnp.where(upper, after, carry))
            theirs.append(jnp.where(upper, carry, after).astype(BF16))
        back = swap(jnp.stack(theirs), bit)
        carries = [x for i, c in enumerate(ours) for x in (c, back[i])]
    carries = [c.astype(BF16) for c in carries]

    within = within_block(meta, query, key, value, doc_count)
    natural = jnp.stack(carries)[jnp.arange(plane, dtype=jnp.int32) ^ member].reshape(width, DH)
    normed = norm_heads(meta, query, [within], [natural], gain, doc_count)
    partial_sum = jnp.dot(normed, weight, preferred_element_type=F32)
    return lax.psum_scatter(partial_sum.astype(BF16), "head", scatter_dimension=1, tiled=True)


def solution(mesh):
    return jax.shard_map(
        functools.partial(body, mesh.shape["seq"], mesh.shape["head"]),
        mesh=mesh,
        in_specs=(
            P("seq", "head"),
            P("seq", "head"),
            P("seq", "head"),
            P(),
            P("head"),
            P("head", None),
        ),
        out_specs=P("seq", "head"),
        check_vma=False,
    )
```

```python
import functools

import jax
import jax.numpy as jnp
from jax import lax
from jax.experimental import pallas as pl
from jax.experimental.pallas import tpu as pltpu
from jax.sharding import PartitionSpec as P

DH = 128
PLANES = 4
F32, BF16 = jnp.float32, jnp.bfloat16
LENS = 8
VMEM_LIMIT = 24 * 1024 * 1024


def doc_start(meta, doc_count, token):
    bound = jnp.int32(0)
    start = jnp.int32(0)
    for d in range(doc_count):
        bound = bound + meta[LENS + d]
        start = jnp.where(bound <= token, bound, start)
    return start


def call(kernel, grid, in_specs, out_specs, out_shape, flops, bytes_accessed, scratch=(), vmem=VMEM_LIMIT, aliases={}):
    return pl.pallas_call(
        kernel,
        grid_spec=pltpu.PrefetchScalarGridSpec(
            num_scalar_prefetch=1,
            grid=grid,
            in_specs=in_specs,
            out_specs=out_specs,
            scratch_shapes=scratch,
        ),
        out_shape=out_shape,
        input_output_aliases=aliases,
        compiler_params=pltpu.CompilerParams(vmem_limit_bytes=vmem),
        cost_estimate=pl.CostEstimate(flops=flops, bytes_accessed=bytes_accessed, transcendentals=0),
    )


def block_states(meta, key, value, doc_count, steps):
    rows, width = key.shape
    part = width // steps

    def kernel(meta_ref, k_ref, v_ref, o_ref):
        offset = meta_ref[0] * rows
        first = doc_start(meta_ref, doc_count, offset + rows - 1) - offset
        live = lax.broadcasted_iota(jnp.int32, (rows, DH), 0) >= first
        for h in range(part // DH):
            cols = slice(h * DH, (h + 1) * DH)
            k = jnp.where(live, k_ref[:, cols], jnp.zeros((), BF16))
            s = lax.dot_general(k, v_ref[:, cols], (((0,), (0,)), ((), ())), preferred_element_type=F32)
            o_ref[0, cols, :] = s.astype(BF16)

    def slot(g, m):
        return (g ^ m[1], 0, 0) if steps > 1 else (0, 0, 0)

    return call(
        kernel,
        (steps,),
        [pl.BlockSpec((rows, part), lambda g, m: (0, g))] * 2,
        pl.BlockSpec((1, part, DH), slot),
        jax.ShapeDtypeStruct((steps, part, DH), BF16),
        2 * rows * width * DH,
        2 * 2 * rows * width,
    )(meta, key, value)


def within_block(meta, query, key, value, doc_count):
    rows, width = query.shape
    part = DH
    for heads in (4, 3, 2):
        if width % (heads * DH) == 0:
            part = heads * DH
            break
    tile = rows // 2

    def kernel(meta_ref, q_ref, k_ref, v_ref, o_ref, mask_ref):
        @pl.when(pl.program_id(0) == 0)
        def _():
            offset = meta_ref[0] * rows
            t = lax.broadcasted_iota(jnp.int32, (rows, rows), 0)
            s = lax.broadcasted_iota(jnp.int32, (rows, rows), 1)
            pos = lax.broadcasted_iota(jnp.int32, (rows, 1), 0)
            first = jnp.zeros((rows, 1), jnp.int32)
            bound = -offset
            for d in range(doc_count):
                bound = bound + meta_ref[LENS + d]
                first = jnp.where(bound <= pos, bound, first)
            mask_ref[...] = jnp.where((s <= t) & (s >= first), 1.0, 0.0).astype(BF16)

        for h in range(part // DH):
            cols = slice(h * DH, (h + 1) * DH)
            for i in range(2):
                r = slice(i * tile, (i + 1) * tile)
                seen = (i + 1) * tile
                scores = lax.dot_general(
                    q_ref[r, cols], k_ref[:seen, cols], (((1,), (1,)), ((), ())), preferred_element_type=F32
                )
                scores = scores.astype(BF16) * mask_ref[r, :seen]
                o_ref[r, cols] = jnp.dot(scores, v_ref[:seen, cols], preferred_element_type=F32)

    spec = pl.BlockSpec((rows, part), lambda g, m: (0, g))
    return call(
        kernel,
        (width // part,),
        [spec] * 3,
        spec,
        jax.ShapeDtypeStruct((rows, width), F32),
        3 * rows * rows * width,
        10 * rows * width,
        [pltpu.VMEM((rows, rows), BF16)],
    )(meta, query, key, value)


def whole(shape):
    return pl.BlockSpec(shape, lambda *_: (0,) * len(shape))


def local(kernel, meta, arrays, shapes, micros, limit=4, specs=None):
    return call(
        kernel,
        (1,),
        specs or [whole(a.shape) for a in arrays],
        [whole(s.shape) for s in shapes],
        shapes,
        int(micros * 1e9),
        1024,
        (),
        limit * 1024 * 1024,
    )(meta, *arrays)


def group(rows, part, slot):
    return pl.BlockSpec((rows, part), lambda i, m: (0, m[1] ^ slot))


def after(meta, *arrays):
    return lax.optimization_barrier((meta, *arrays))[0]


def factor(condition):
    return jnp.where(condition, 1.0, 0.0)


def slice_weights(meta, weight, columns):
    part, half = weight.shape[0] // 4, columns // 2
    shapes = [jax.ShapeDtypeStruct((part, half), BF16)]

    def kernel(meta_ref, w_ref, o_ref, sem):
        rows = pl.ds(pl.multiple_of(meta_ref[1] * part, DH), part)
        start = (1 - meta_ref[2]) * columns + meta_ref[3] * half
        copy = pltpu.make_async_copy(w_ref.at[rows, pl.ds(pl.multiple_of(start, DH), half)], o_ref, sem)
        copy.start()
        copy.wait()

    return call(
        kernel,
        (1,),
        [pl.BlockSpec(memory_space=pl.ANY)],
        [pl.BlockSpec(memory_space=pltpu.VMEM)] * len(shapes),
        shapes,
        6 * 10**9,
        1024,
        [pltpu.SemaphoreType.DMA],
        50 * 1024 * 1024,
    )(meta, weight)


def split_states(meta, key, value, doc_count):
    rows, width = key.shape
    part = width // 4
    order = (1, 3, 0, 2)

    def kernel(meta_ref, *refs):
        offset = meta_ref[0] * rows
        first = doc_start(meta_ref, doc_count, offset + rows - 1) - offset
        live = lax.broadcasted_iota(jnp.int32, (rows, DH), 0) >= first
        for i in range(4):
            k_ref, v_ref, o_ref = refs[i], refs[4 + i], refs[8 + i // 2]
            for h in range(part // DH):
                cols = slice(h * DH, (h + 1) * DH)
                k = jnp.where(live, k_ref[:, cols], jnp.zeros((), BF16))
                state = lax.dot_general(
                    k, v_ref[:, cols], (((0,), (0,)), ((), ())), preferred_element_type=F32
                )
                o_ref[i % 2, cols, :] = state.astype(BF16)

    arrays, specs = [key] * 4 + [value] * 4, [group(rows, part, s) for s in order] * 2
    return local(kernel, meta, arrays, [jax.ShapeDtypeStruct((2, part, DH), BF16)] * 2, 2, 10, specs)


def seen_mask(meta_ref, rows, doc_count):
    offset = meta_ref[0] * rows
    t = lax.broadcasted_iota(jnp.int32, (rows, rows), 0)
    s = lax.broadcasted_iota(jnp.int32, (rows, rows), 1)
    pos = lax.broadcasted_iota(jnp.int32, (rows, 1), 0)
    first = jnp.zeros((rows, 1), jnp.int32)
    bound = -offset
    for d in range(doc_count):
        bound = bound + meta_ref[LENS + d]
        first = jnp.where(bound <= pos, bound, first)
    return jnp.where((s <= t) & (s >= first), 1.0, 0.0).astype(BF16)


def within_slot(meta, query, key, value, doc_count, slot, mask=None):
    rows, width = query.shape
    part = width // 4
    tile = rows // 2
    make = mask is None

    def kernel(meta_ref, q_ref, k_ref, v_ref, *rest):
        if make:
            o_ref, mask_ref = rest
            mask_ref[...] = seen_mask(meta_ref, rows, doc_count)
        else:
            mask_ref, o_ref = rest
        for h in range(part // DH):
            cols = slice(h * DH, (h + 1) * DH)
            for i in range(2):
                r = slice(i * tile, (i + 1) * tile)
                seen = (i + 1) * tile
                scores = lax.dot_general(
                    q_ref[r, cols], k_ref[:seen, cols], (((1,), (1,)), ((), ())), preferred_element_type=F32
                )
                scores = scores.astype(BF16) * mask_ref[r, :seen]
                o_ref[r, cols] = jnp.dot(scores, v_ref[:seen, cols], preferred_element_type=F32)

    shapes = [jax.ShapeDtypeStruct((rows, part), F32)]
    arrays, specs = [query, key, value], [group(rows, part, slot)] * 3
    if make:
        shapes = shapes + [jax.ShapeDtypeStruct((rows, rows), BF16)]
        return local(kernel, meta, arrays, shapes, 2, 10, specs)
    return local(kernel, meta, [*arrays, mask], shapes, 2, 10, [*specs, whole(mask.shape)])[0]


def small(kernel, meta, arrays, shape, count):
    return local(kernel, meta, arrays, [jax.ShapeDtypeStruct(shape, BF16)] * count, 0.6)


def join_core(meta, keep, got, rows, doc_count):
    def kernel(meta_ref, keep_ref, got_ref, a_ref, b_ref):
        low = meta_ref[0] & -2
        joined = factor(doc_start(meta_ref, doc_count, (low + 2) * rows - 1) < (low + 1) * rows)
        upper = (meta_ref[1] & 1) != 0
        own, other = jnp.where(upper, 1.0, joined), jnp.where(upper, joined, 1.0)
        for i, o_ref in enumerate((a_ref, b_ref)):
            o_ref[...] = (own * keep_ref[i].astype(F32) + other * got_ref[i].astype(F32)).astype(BF16)

    return small(kernel, meta, (keep, got), keep.shape[1:], 2)


def join_chips(meta, mine, got, rows, doc_count):
    def kernel(meta_ref, a_ref, b_ref, o_ref):
        low = meta_ref[0] & -4
        joined = factor(doc_start(meta_ref, doc_count, (low + 4) * rows - 1) < (low + 2) * rows)
        upper = (meta_ref[1] & 2) != 0
        own, other = jnp.where(upper, 1.0, joined), jnp.where(upper, joined, 1.0)
        o_ref[...] = (own * a_ref[...].astype(F32) + other * b_ref[...].astype(F32)).astype(BF16)

    return small(kernel, meta, (mine, got), mine.shape, 1)[0]


def join_planes(meta, plane_sum, previous, rows, doc_count):
    def kernel(meta_ref, a_ref, b_ref, o_ref):
        low = meta_ref[0] & -4
        joined = factor(doc_start(meta_ref, doc_count, (low + 4) * rows - 1) < low * rows)
        o_ref[...] = (a_ref[...].astype(F32) + joined * b_ref[...].astype(F32)).astype(BF16)

    return small(kernel, meta, (plane_sum, previous), plane_sum.shape, 1)[0]


def carry_in_chip(meta_ref, chip, keep, got, rows, doc_count):
    low = meta_ref[0] & -2
    begins = doc_start(meta_ref, doc_count, (low + 1) * rows)
    through, joined = factor(begins < low * rows), factor(begins < (low + 1) * rows)
    upper = (meta_ref[1] & 1) != 0
    later = through * chip + joined * jnp.where(upper, got, keep).astype(F32)
    return jnp.where(upper, later, chip), jnp.where(upper, chip, later)


def carry_first(meta, near, far, mine, got, keep, core_got, rows, doc_count):
    def kernel(meta_ref, near_ref, far_ref, a_ref, b_ref, keep_ref, got_ref, o_ref, core_ref, chip_ref):
        low = meta_ref[0] & -4
        begins = doc_start(meta_ref, doc_count, low * rows)
        first = factor(begins < low * rows) * near_ref[...].astype(F32)
        first = first + factor(begins < (low - 4) * rows) * far_ref[...].astype(F32)
        begins = doc_start(meta_ref, doc_count, (low + 2) * rows)
        through, joined = factor(begins < low * rows), factor(begins < (low + 2) * rows)
        upper = (meta_ref[1] & 2) != 0
        later = through * first + joined * jnp.where(upper, b_ref[...], a_ref[...]).astype(F32)
        chip_ref[...] = jnp.where(upper, first, later).astype(BF16)
        chip = jnp.where(upper, later, first)
        ours, theirs = carry_in_chip(meta_ref, chip, keep_ref[0], got_ref[0], rows, doc_count)
        o_ref[...] = ours.astype(BF16)
        core_ref[...] = theirs.astype(BF16)

    return small(kernel, meta, (near, far, mine, got, keep, core_got), mine.shape, 3)


def carry_second(meta, chip, keep, core_got, rows, doc_count):
    def kernel(meta_ref, chip_ref, keep_ref, got_ref, o_ref, core_ref):
        ours, theirs = carry_in_chip(
            meta_ref, chip_ref[...].astype(F32), keep_ref[1], got_ref[1], rows, doc_count
        )
        o_ref[...] = ours.astype(BF16)
        core_ref[...] = theirs.astype(BF16)

    return small(kernel, meta, (chip, keep, core_got), chip.shape, 2)


def norm_heads(meta, query, withins, carries, gain, doc_count, slots=None, split=None):
    rows = query.shape[0]
    part = carries[0].shape[0]
    count = len(carries)
    heights = split or (rows,)

    def kernel(meta_ref, *refs):
        offset = meta_ref[0] * rows
        begins = doc_start(meta_ref, doc_count, offset)
        bound = jnp.int32(0)
        end = jnp.int32(0)
        for d in range(doc_count):
            previous = bound
            bound = bound + meta_ref[LENS + d]
            end = jnp.where(previous <= offset, bound, end)
        stop = jnp.where(begins < offset, end - offset, 0)
        cross = lax.broadcasted_iota(jnp.int32, (rows, DH), 0) < stop
        outs = refs[4 * count :]
        for n in range(count):
            q_ref, w_ref, c_ref, g_ref = refs[4 * n : 4 * n + 4]
            for h in range(part // DH):
                cols = slice(h * DH, (h + 1) * DH)
                term = jnp.dot(q_ref[:, cols], c_ref[cols, :], preferred_element_type=F32)
                mixture = w_ref[:, cols] + jnp.where(cross, term, 0.0)
                mean = jnp.mean(mixture * mixture, axis=-1, keepdims=True)
                normed = (mixture * lax.rsqrt(mean + 1e-06) * g_ref[:, cols]).astype(BF16)
                top = 0
                for o_ref, height in zip(outs, heights):
                    o_ref[:, n * part + h * DH : n * part + (h + 1) * DH] = normed[top : top + height]
                    top += height

    gain = gain.reshape(1, -1)
    arrays, specs = [], []
    for n in range(count):
        arrays += [query, withins[n], carries[n], gain]
        wide = [whole((rows, part)), whole((1, part))] if slots is None else [
            group(rows, part, slots[n]), group(1, part, slots[n])
        ]
        specs += [wide[0], whole((rows, part)), whole((part, DH)), wide[1]]
    shapes = [jax.ShapeDtypeStruct((height, part * count), BF16) for height in heights]
    outs = local(kernel, meta, arrays, shapes, count, 10, specs)
    return outs if split else outs[0]


TILES = 4
OWN_TILES = 2


def project_own(meta, pieces, weight, columns):
    rows = pieces[0].shape[0]
    part = weight.shape[0] // 4
    tile = columns // OWN_TILES
    count = len(pieces)

    def kernel(meta_ref, *refs):
        ns, ws, o_ref = refs[:count], refs[count:-1], refs[-1]
        n = jnp.concatenate([r[...] for r in ns], axis=1)
        w = jnp.concatenate([r[...] for r in ws], axis=0)
        o_ref[...] = jnp.dot(n, w, preferred_element_type=F32)

    return call(
        kernel,
        (OWN_TILES,),
        [whole(p.shape) for p in pieces]
        + [pl.BlockSpec((part, tile), lambda n, m, s=s: (m[1] ^ s, m[2] * OWN_TILES + n)) for s in range(4)],
        pl.BlockSpec((rows, tile), lambda n, m: (0, n)),
        jax.ShapeDtypeStruct((rows, columns), F32),
        10**6,
        1024,
    )(meta, *pieces, *[weight] * 4)


def project_more(meta, total, pieces, weights, final):
    rows, columns = total.shape
    tile = columns // TILES
    count = len(pieces)
    flat = [w for ws in weights for w in ws]
    places = []
    for ws in weights:
        start, slot = 0, []
        for w in ws:
            slot.append((start, start + w.shape[1]))
            start += w.shape[1]
        places.append(slot)

    def kernel(meta_ref, t_ref, *refs):
        ns, ws, rest = refs[:count], refs[count : count + len(flat)], refs[count + len(flat) :]
        n = jnp.concatenate([r[...] for r in ns], axis=1)
        copies = []
        for c in range(TILES):
            low, high = c * tile, (c + 1) * tile
            rows_of, at = [], 0
            for slot in places:
                held = []
                for k, (start, stop) in enumerate(slot):
                    first, last = max(start, low), min(stop, high)
                    if first < last:
                        held.append(ws[at + k][:, first - start : last - start])
                rows_of.append(jnp.concatenate(held, axis=1))
                at += len(slot)
            w = jnp.concatenate(rows_of, axis=0)
            cols = pl.ds(pl.multiple_of((c ^ (meta_ref[3] * (TILES // 2))) * tile, DH), tile)
            value = t_ref[:, cols] + jnp.dot(n, w, preferred_element_type=F32)
            if final:
                o_ref, held_ref, sems = rest
                held_ref[c] = value.astype(BF16)
                copies.append(pltpu.make_async_copy(held_ref.at[c], o_ref.at[:, cols], sems.at[c]))
                copies[-1].start()
            else:
                rest[0][:, cols] = value
        for copy in copies:
            copy.wait()

    vmem = pl.BlockSpec(memory_space=pltpu.VMEM)
    scratch = [pltpu.VMEM((TILES, rows, tile), BF16), pltpu.SemaphoreType.DMA((TILES,))]
    return call(
        kernel,
        (1,),
        [vmem] * (1 + count + len(flat)),
        pl.BlockSpec(memory_space=pl.ANY) if final else vmem,
        jax.ShapeDtypeStruct((rows, columns), BF16 if final else F32),
        10**6,
        1024,
        scratch if final else (),
        aliases={} if final else {1: 0},
    )(meta, total, *pieces, *flat)


def pair_body(n_seq, query, key, value, doc_lengths, gain, weight):
    rows, width = query.shape
    docs = doc_lengths.shape[0]
    plane, part = 4, width // 4
    columns = weight.shape[1] // 2
    half = columns // 2
    block = lax.axis_index("seq").astype(jnp.int32)
    group = lax.axis_index("head").astype(jnp.int32)
    member = block % plane
    side = (block // plane) % 2
    meta = jnp.concatenate([
        jnp.stack([block, member, group, side]), jnp.zeros((LENS - 4,), jnp.int32), doc_lengths
    ])

    def swap(x, bit):
        return lax.ppermute(x, "seq", [(i, i ^ bit) for i in range(n_seq)])

    def shift(x, count):
        return lax.ppermute(x, "seq", [(i, i + count) for i in range(n_seq - count)])

    def flip(x):
        return lax.ppermute(x, "head", [(0, 1), (1, 0)])

    def behind(x, *arrays):
        return lax.optimization_barrier((x, *arrays))[0]

    quarter = half // 2
    sent = slice_weights(meta, weight, columns)
    w0 = [flip(sent[0])]
    send, keep = split_states(after(meta, *sent), key, value, docs)
    core_got = swap(send, 1)
    query = behind(query, send)
    within0, mask = within_slot(after(meta, send), query, key, value, docs, 0)
    chip0, chip2 = join_core(after(meta, within0), keep, core_got, rows, docs)
    chip_got = swap(chip2, 2)
    within1 = within_slot(after(meta, chip0), query, key, value, docs, 1, mask)
    plane_sum = join_chips(after(meta, within1), chip0, chip_got, rows, docs)
    near = shift(plane_sum, plane)
    within2 = within_slot(after(meta, plane_sum), query, key, value, docs, 2, mask)
    both = join_planes(after(meta, within2), plane_sum, near, rows, docs)
    far = shift(both, 2 * plane)
    carry0, core_carry0, chip_carry = carry_first(
        meta, near, far, chip0, chip_got, keep, core_got, rows, docs
    )
    carry1 = swap(core_carry0, 1)
    chip_carry2 = swap(chip_carry, 2)

    def norm(slots, withins, carries):
        return norm_heads(meta, query, withins, carries, gain, docs, slots)

    normed0 = norm((0,), [within0], [carry0])
    far0 = flip(normed0)
    within3 = within_slot(after(meta, normed0), query, key, value, docs, 3, mask)
    normed1 = norm((1,), [within1], [carry1])
    far1 = flip(normed1)
    w2 = [swap(behind(w0[0], both), 2)]
    carry2, core_carry2 = carry_second(after(meta, far0, w2[0], normed1), chip_carry2, keep, core_got, rows, docs)
    carry3 = swap(core_carry2, 1)
    normed2 = norm((2, 3), [within2, within3], [carry2, carry3])
    far2 = flip(normed2)

    total = project_own(meta, [normed0, normed1, normed2], weight, columns)
    w0.append(swap(behind(w0[0], normed0), plane))
    w2.append(swap(behind(w0[1], normed2)[:, :quarter], 2))
    w2.append(swap(behind(w2[0], normed2)[:, quarter:], plane))

    def cut(w, width):
        return [w[:, at : at + width] for at in range(0, w.shape[1], width)]

    w1 = [swap(x, 1) for w in w0 for x in cut(w, quarter)]
    w3 = [swap(x, 1) for w, width in zip(w2, (quarter, quarter // 2, quarter // 2)) for x in cut(w, width)]

    total = project_more(meta, total, [far0, far1], [w0, w1], False)
    return project_more(meta, total, [far2], [w2, w3], True)


def body(n_seq, n_head, query, key, value, doc_lengths, gain, weight):
    rows, width = query.shape
    doc_count = doc_lengths.shape[0]
    plane = n_seq // PLANES
    if n_head == 2 and plane == 4 and width % (4 * DH) == 0:
        return pair_body(n_seq, query, key, value, doc_lengths, gain, weight)
    block = lax.axis_index("seq").astype(jnp.int32)
    group = lax.axis_index("head").astype(jnp.int32)
    member = block % plane
    meta = jnp.concatenate([
        jnp.stack([block, member, group]), jnp.zeros((LENS - 3,), jnp.int32), doc_lengths
    ])

    bounds = jnp.cumsum(doc_lengths)

    def first_block(token):
        starts = jnp.max(jnp.where(bounds <= token, bounds, 0))
        return starts // rows

    def weigh(condition):
        return condition.astype(F32)

    def swap(x, bit):
        return lax.ppermute(x, "seq", [(i, i ^ bit) for i in range(n_seq)])

    by_slot = (width // DH) % plane == 0
    steps = plane if by_slot else 1
    states = block_states(meta, key, value, doc_count, steps)
    if not by_slot:
        states = states.reshape(plane, width // plane, DH)[jnp.arange(plane, dtype=jnp.int32) ^ member]
    slots = [states[s] for s in range(plane)]

    kept = []
    bit = 1
    while bit < plane:
        mine, send = slots[0::2], slots[1::2]
        got = swap(jnp.stack(send), bit)
        got = [got[i] for i in range(len(send))]
        upper = (member & bit) != 0
        unit = block & ~(2 * bit - 1)
        joined = weigh(first_block((unit + 2 * bit) * rows - 1) < unit + bit)
        own_factor = jnp.where(upper, 1.0, joined)
        got_factor = jnp.where(upper, joined, 1.0)
        kept.append((mine, got, bit, upper, unit))
        slots = [
            (own_factor * a.astype(F32) + got_factor * b.astype(F32)).astype(BF16) for a, b in zip(mine, got)
        ]
        bit *= 2
    base = block - member
    begins = first_block(base * rows)
    carry = jnp.zeros(slots[0].shape, F32)
    for d in range(PLANES - 1, 0, -1):
        shift = d * plane
        got = lax.ppermute(slots[0], "seq", [(i, i + shift) for i in range(n_seq - shift)])
        carry = carry + weigh((base - shift + plane - 1 >= begins) & (base >= shift)) * got.astype(F32)
    carries = [carry]

    for mine, got, bit, upper, unit in reversed(kept):
        middle = unit + bit
        begins = first_block(middle * rows)
        through, joined = weigh(begins < unit), weigh(begins < middle)
        ours, theirs = [], []
        for carry, a, b in zip(carries, mine, got):
            lower_state = jnp.where(upper, b, a).astype(F32)
            after = through * carry + joined * lower_state
            ours.append(jnp.where(upper, after, carry))
            theirs.append(jnp.where(upper, carry, after).astype(BF16))
        back = swap(jnp.stack(theirs), bit)
        carries = [x for i, c in enumerate(ours) for x in (c, back[i])]
    carries = [c.astype(BF16) for c in carries]

    within = within_block(meta, query, key, value, doc_count)
    natural = jnp.stack(carries)[jnp.arange(plane, dtype=jnp.int32) ^ member].reshape(width, DH)
    normed = norm_heads(meta, query, [within], [natural], gain, doc_count)
    partial_sum = jnp.dot(normed, weight, preferred_element_type=F32)
    return lax.psum_scatter(partial_sum.astype(BF16), "head", scatter_dimension=1, tiled=True)


def solution(mesh):
    return jax.shard_map(
        functools.partial(body, mesh.shape["seq"], mesh.shape["head"]),
        mesh=mesh,
        in_specs=(
            P("seq", "head"),
            P("seq", "head"),
            P("seq", "head"),
            P(),
            P("head"),
            P("head", None),
        ),
        out_specs=P("seq", "head"),
        check_vma=False,
    )
```
